32 devices in a mesh: dp: 8 (over z, y), tensor: 4 (over x, core).
Axes of the slice: x: 2, y: 2, z: 4, core: 2. Of those that a mesh axis runs over, the one named last changes fastest.
Arguments:
- latents: bfloat16 [8192, 1536], P(('dp', 'tensor')), may hold values from -6 to 6
- cotangent: float32 [8192, 1536], P(('dp', 'tensor')), may hold values from -6 to 6
- captions: bfloat16 [16384, 4096], P('dp', 'tensor'), may hold values from -17 to 17, as said below
- conditions: float32 [64, 1024], replicated, may hold values from -6 to 6
- image_ids: int32 [8, 1024], P('dp'), may hold values from 0 to 7, never falling along the last dimension, each value on 1 to 512 neighbouring positions
- rope_rows: int32 [8, 1024], P('dp'), may hold values from 0 to 47
- rope_cols: int32 [8, 1024], P('dp'), may hold values from 0 to 47
- caption_lengths: int32 [8, 8], P('dp'), may hold values from 1 to 256
- attention_in: float32 [3, 1536, 1536], P(None, 'dp', 'tensor'), may hold values from -0.15625 to 0.15625
- attention_out: float32 [1536, 1536], P('tensor', 'dp'), may hold values from -0.15625 to 0.15625
- feed_in: float32 [2, 1536, 4096], P(None, 'dp', 'tensor'), may hold values from -0.15625 to 0.15625
- feed_out: float32 [4096, 1536], P('tensor', 'dp'), may hold values from -0.09375 to 0.09375
- caption_in: float32 [2, 4096, 1536], P(None, 'tensor', 'dp'), may hold values from -0.09375 to 0.09375
- modulator: float32 [1025, 6144], P(None, ('dp', 'tensor')), may hold values from -0.1875 to 0.1875
- channels: float32 [8, 1536], P(None, 'dp'), may hold values from 0.2 to 2.3, as said below
- moment_attention_in: float32 [3, 1536, 1536], P(None, 'dp', 'tensor'), may hold values from -9.1552734e-05 to 9.1552734e-05
- square_attention_in: float32 [3, 1536, 1536], P(None, 'dp', 'tensor'), may hold values from 1.1227779e-09 to 4.4487423e-09
- moment_attention_out: float32 [1536, 1536], P('tensor', 'dp'), may hold values from -9.1552734e-05 to 9.1552734e-05
- square_attention_out: float32 [1536, 1536], P('tensor', 'dp'), may hold values from 1.1227779e-09 to 4.4487423e-09
- moment_feed_in: float32 [2, 1536, 4096], P(None, 'dp', 'tensor'), may hold values from -9.1552734e-05 to 9.1552734e-05
- square_feed_in: float32 [2, 1536, 4096], P(None, 'dp', 'tensor'), may hold values from 1.1227779e-09 to 4.4487423e-09
- moment_feed_out: float32 [4096, 1536], P('tensor', 'dp'), may hold values from -9.1552734e-05 to 9.1552734e-05
- square_feed_out: float32 [4096, 1536], P('tensor', 'dp'), may hold values from 1.1227779e-09 to 4.4487423e-09
- moment_caption_in: float32 [2, 4096, 1536], P(None, 'tensor', 'dp'), may hold values from -9.1552734e-05 to 9.1552734e-05
- square_caption_in: float32 [2, 4096, 1536], P(None, 'tensor', 'dp'), may hold values from 1.1227779e-09 to 4.4487423e-09
- moment_modulator: float32 [1025, 6144], P(None, ('dp', 'tensor')), may hold values from -9.1552734e-05 to 9.1552734e-05
- square_modulator: float32 [1025, 6144], P(None, ('dp', 'tensor')), may hold values from 1.1227779e-09 to 4.4487423e-09
- moment_channels: float32 [8, 1536], P(None, 'dp'), may hold values from -0.00036621094 to 0.00036621094
- square_channels: float32 [8, 1536], P(None, 'dp'), may hold values from 3.389518e-09 to 1.3558072e-08
Outputs:
- block_out: float32 [8192, 1536], P(('dp', 'tensor'))
- latent_grad: float32 [8192, 1536], P(('dp', 'tensor'))
- grad_norm: float32 [], replicated
- moment_attention_in_new: float32 [3, 1536, 1536], P(None, 'dp', 'tensor')
- square_attention_in_new: float32 [3, 1536, 1536], P(None, 'dp', 'tensor')
- attention_in_new: float32 [3, 1536, 1536], P(None, 'dp', 'tensor')
- moment_attention_out_new: float32 [1536, 1536], P('tensor', 'dp')
- square_attention_out_new: float32 [1536, 1536], P('tensor', 'dp')
- attention_out_new: float32 [1536, 1536], P('tensor', 'dp')
- moment_feed_in_new: float32 [2, 1536, 4096], P(None, 'dp', 'tensor')
- square_feed_in_new: float32 [2, 1536, 4096], P(None, 'dp', 'tensor')
- feed_in_new: float32 [2, 1536, 4096], P(None, 'dp', 'tensor')
- moment_feed_out_new: float32 [4096, 1536], P('tensor', 'dp')
- square_feed_out_new: float32 [4096, 1536], P('tensor', 'dp')
- feed_out_new: float32 [4096, 1536], P('tensor', 'dp')
- moment_caption_in_new: float32 [2, 4096, 1536], P(None, 'tensor', 'dp')
- square_caption_in_new: float32 [2, 4096, 1536], P(None, 'tensor', 'dp')
- caption_in_new: float32 [2, 4096, 1536], P(None, 'tensor', 'dp')
- moment_modulator_new: float32 [1025, 6144], P(None, ('dp', 'tensor'))
- square_modulator_new: float32 [1025, 6144], P(None, ('dp', 'tensor'))
- modulator_new: float32 [1025, 6144], P(None, ('dp', 'tensor'))
- moment_channels_new: float32 [8, 1536], P(None, 'dp')
- square_channels_new: float32 [8, 1536], P(None, 'dp')
- channels_new: float32 [8, 1536], P(None, 'dp')
The draws below stay inside these ranges and needn't reach their ends.
Inputs may be any that keep to these rules, and one draw needn't show every extreme that they name: `image_ids`: each row holds all 8 images as runs of consecutive tokens numbered in order, none longer than 512 tokens. `captions`: caption features of order one. `channels`: positive gains and gate values of order one.
All inputs are finite; a program needn't handle non-finite values.
Results may differ from the reference program's by a relative error of at most 0.015.
The reference program's roundings to bfloat16 on the way count: a program that leaves them out, or rounds other values in their place, can miss the bound.
Values may be sent and summed in bfloat16 or wider, within the bound.
A program may use at most 320 MiB of HBM per device.

```python
import math
import jax
import jax.numpy as jnp
import numpy as np
from jax import lax

D = 1536
HEADS = 24
HEAD = 64
FF = 4096
TEXT = 4096
CDIM = 1024
CAP = 256
IMG_DEV = 8
STEP = 10
TOK_DEV = 1024
ROWS = 8
TOKENS = 8192
IMAGES = 64
CAPTOKENS = 16384
PARAMS = 47204352


def draw_captions(key, part):
    first, second = jax.random.split(jax.random.fold_in(key, 11))
    place = jnp.arange(TEXT, dtype=jnp.float32) / (TEXT - 1)
    rough = jax.random.uniform(second, (TEXT,), jnp.float32, 0.7, 1.4)
    spread = (1.0 + 2.0 * place) * rough
    values = jax.random.truncated_normal(first, -4.0, 4.0, (CAPTOKENS, TEXT), jnp.float32)
    return (values * spread[None, :]).astype(jnp.bfloat16)


def draw_channels(key, part):
    first, second = jax.random.split(jax.random.fold_in(key, 23))
    place = jnp.arange(D, dtype=jnp.float32) / (D - 1)
    rough = jax.random.uniform(first, (7, D), jnp.float32, 0.85, 1.18)
    gate = jax.random.uniform(second, (1, D), jnp.float32, 0.2, 1.2)
    gains = (0.7 + 0.9 * place)[None, :] * rough
    return jnp.concatenate([gains, gate], axis=0).astype(jnp.float32)


def plant(drawn, own_key, low, top_value):
    spot = [jax.random.randint(jax.random.fold_in(own_key, axis), (), 0, length) for axis, length in enumerate(drawn.shape)]
    widest = drawn.shape.index(max(drawn.shape))
    neighbour = spot[:widest] + [(spot[widest] + 1) % drawn.shape[widest]] + spot[widest + 1:]
    return drawn.at[tuple(spot)].set(low).at[tuple(neighbour)].set(top_value)


def block_scale(own_key, dims, cuts, low, largest):
    level, own = 1.0, jax.random.fold_in(own_key, 6)
    for axis_at, parts in cuts:
        draws = jnp.exp(jax.random.uniform(jax.random.fold_in(own, axis_at), (parts,), jnp.float32, low / len(cuts), largest / len(cuts)))
        level = level * jnp.repeat(draws, dims[axis_at] // parts).reshape([-1 if axis == axis_at else 1 for axis in range(len(dims))])
    return level


def profile(number_of, total, reach, skew):
    loads = [(1 << 20) // math.isqrt(rank ** skew) + 1 for rank in range(2, number_of + 1)]
    spare, holding = total - reach - (number_of - 1), [1] * (number_of - 1)
    while spare > 0:
        movable = [i for i in range(number_of - 1) if holding[i] < reach]
        pool, left = sum([loads[i] for i in movable]), spare
        for i in movable:
            more = min(reach - holding[i], max(1, left * loads[i] // pool), spare)
            holding[i] = holding[i] + more
            spare = spare - more
    return np.array([reach] + holding)


def uneven_parts(key, count, total, limit, slope):
    if count == 2:
        one = jax.random.randint(key, (), max(1, total - limit), min(limit, total - 1) + 1)
        return jnp.stack([one, total - one])
    sizes = jnp.asarray(profile(count, total, limit, slope), jnp.int32)
    twos = (count - 1) // 2
    giver, receiver = sizes[1:1 + 2 * twos:2], sizes[2:2 + 2 * twos:2]
    slack = jnp.minimum(giver - 1, limit - receiver)
    shifted = jax.random.randint(jax.random.fold_in(key, 1), (twos,), 0, 1 << 20) % (slack + 1)
    sizes = sizes.at[1:1 + 2 * twos:2].set(giver - shifted).at[2:2 + 2 * twos:2].set(receiver + shifted)
    return sizes[jax.random.permutation(jax.random.fold_in(key, 2), count)]


def scatter_about(stream_key, extent, deviation, most, shards=(), kind=jnp.bfloat16):
    drawn = deviation * jax.random.normal(stream_key, extent, jnp.float32)
    if shards:
        drawn = drawn * block_scale(stream_key, extent, shards, -0.22, 0.18)
    return jnp.clip(drawn, -most, most).astype(kind)


def setup_inputs(seed: int = 0) -> dict:
    key_of = jax.random.split(jax.random.key(seed), 30)
    return {
        "latents": scatter_about(key_of[0], (TOKENS, D), 1.0, 6.0, ((0, 32),)),
        "cotangent": scatter_about(key_of[1], (TOKENS, D), 1.0, 6.0, ((0, 32),), jnp.float32),
        "captions": draw_captions(jax.random.fold_in(key_of[29], 71), 0),
        "conditions": scatter_about(key_of[3], (IMAGES, CDIM), 1.0, 6.0, (), jnp.float32),
        "image_ids": jax.vmap(lambda own: jnp.searchsorted(jnp.cumsum(uneven_parts(own, IMG_DEV, TOK_DEV, TOK_DEV // 2, 2)), jnp.arange(TOK_DEV), side="right"))(jax.random.split(key_of[4], ROWS)).reshape((ROWS, TOK_DEV)).astype(jnp.int32),
        "rope_rows": plant(jax.random.randint(key_of[5], (ROWS, TOK_DEV), 0, 48), jax.random.fold_in(key_of[5], 1), 0, 47).astype(jnp.int32),
        "rope_cols": plant(jax.random.randint(key_of[6], (ROWS, TOK_DEV), 0, 48), jax.random.fold_in(key_of[6], 1), 0, 47).astype(jnp.int32),
        "caption_lengths": plant(jax.random.randint(key_of[7], (ROWS, IMG_DEV), 1, CAP + 1), jax.random.fold_in(key_of[7], 1), 1, CAP).astype(jnp.int32),
        "attention_in": scatter_about(key_of[8], (3, D, D), D ** -0.5, 0.15625, ((1, 8), (2, 4)), jnp.float32),
        "attention_out": scatter_about(key_of[9], (D, D), D ** -0.5, 0.15625, ((0, 4), (1, 8)), jnp.float32),
        "feed_in": scatter_about(key_of[10], (2, D, FF), D ** -0.5, 0.15625, ((1, 8), (2, 4)), jnp.float32),
        "feed_out": scatter_about(key_of[11], (FF, D), FF ** -0.5, 0.09375, ((0, 4), (1, 8)), jnp.float32),
        "caption_in": scatter_about(key_of[12], (2, TEXT, D), TEXT ** -0.5, 0.09375, ((1, 4), (2, 8)), jnp.float32),
        "modulator": scatter_about(key_of[13], (CDIM + 1, 4 * D), CDIM ** -0.5, 0.1875, ((1, 32),), jnp.float32),
        "channels": draw_channels(jax.random.fold_in(key_of[29], 71), 0),
        "moment_attention_in": scatter_about(key_of[15], (3, D, D), (0.11 * PARAMS ** -0.5), 9.1552734375e-05, ((1, 8), (2, 4)), jnp.float32),
        "square_attention_in": jnp.clip(jnp.exp(math.log(4.448742263463146e-09) - 1.3768156 * jax.random.uniform(key_of[16], (3, D, D), jnp.float32) ** block_scale(key_of[16], (3, D, D), ((1, 8), (2, 4)), -0.2, 0.2)), 1.1227778706768277e-09, 4.448742263463146e-09),
        "moment_attention_out": scatter_about(key_of[17], (D, D), (0.11 * PARAMS ** -0.5), 9.1552734375e-05, ((0, 4), (1, 8)), jnp.float32),
        "square_attention_out": jnp.clip(jnp.exp(math.log(4.448742263463146e-09) - 1.3768156 * jax.random.uniform(key_of[18], (D, D), jnp.float32) ** block_scale(key_of[18], (D, D), ((0, 4), (1, 8)), -0.2, 0.2)), 1.1227778706768277e-09, 4.448742263463146e-09),
        "moment_feed_in": scatter_about(key_of[19], (2, D, FF), (0.11 * PARAMS ** -0.5), 9.1552734375e-05, ((1, 8), (2, 4)), jnp.float32),
        "square_feed_in": jnp.clip(jnp.exp(math.log(4.448742263463146e-09) - 1.3768156 * jax.random.uniform(key_of[20], (2, D, FF), jnp.float32) ** block_scale(key_of[20], (2, D, FF), ((1, 8), (2, 4)), -0.2, 0.2)), 1.1227778706768277e-09, 4.448742263463146e-09),
        "moment_feed_out": scatter_about(key_of[21], (FF, D), (0.11 * PARAMS ** -0.5), 9.1552734375e-05, ((0, 4), (1, 8)), jnp.float32),
        "square_feed_out": jnp.clip(jnp.exp(math.log(4.448742263463146e-09) - 1.3768156 * jax.random.uniform(key_of[22], (FF, D), jnp.float32) ** block_scale(key_of[22], (FF, D), ((0, 4), (1, 8)), -0.2, 0.2)), 1.1227778706768277e-09, 4.448742263463146e-09),
        "moment_caption_in": scatter_about(key_of[23], (2, TEXT, D), (0.11 * PARAMS ** -0.5), 9.1552734375e-05, ((1, 4), (2, 8)), jnp.float32),
        "square_caption_in": jnp.clip(jnp.exp(math.log(4.448742263463146e-09) - 1.3768156 * jax.random.uniform(key_of[24], (2, TEXT, D), jnp.float32) ** block_scale(key_of[24], (2, TEXT, D), ((1, 4), (2, 8)), -0.2, 0.2)), 1.1227778706768277e-09, 4.448742263463146e-09),
        "moment_modulator": scatter_about(key_of[25], (CDIM + 1, 4 * D), (0.11 * PARAMS ** -0.5), 9.1552734375e-05, ((1, 32),), jnp.float32),
        "square_modulator": jnp.clip(jnp.exp(math.log(4.448742263463146e-09) - 1.3768156 * jax.random.uniform(key_of[26], (CDIM + 1, 4 * D), jnp.float32) ** block_scale(key_of[26], (CDIM + 1, 4 * D), ((1, 32),), -0.2, 0.2)), 1.1227778706768277e-09, 4.448742263463146e-09),
        "moment_channels": scatter_about(key_of[27], (8, D), (0.44 * PARAMS ** -0.5), 0.00036621094, ((1, 8),), jnp.float32),
        "square_channels": jnp.clip(jnp.exp(math.log(1.3558071998431842e-08) - 1.3862944 * jax.random.uniform(key_of[28], (8, D), jnp.float32) ** block_scale(key_of[28], (8, D), ((1, 8),), -0.2, 0.2)), 3.3895179996079605e-09, 1.3558071998431842e-08),
    }


@jax.custom_vjp
def low(v):
    return lax.optimization_barrier(v.astype(jnp.bfloat16)).astype(jnp.float32)

@jax.custom_vjp
def low_back(v):
    return v

def low_keep(v):
    return (low(v), None)

def low_pass(kept, grad):
    return (grad,)

def back_keep(v):
    return (v, None)

def back_low(kept, grad):
    return (low(grad),)
low.defvjp(low_keep, low_pass)
low_back.defvjp(back_keep, back_low)
EPS = 1e-06
NEG = -1e+30
THETA = 10000.0
BETA1 = 0.9
BETA2 = 0.95
RATE = 0.05
GAIN_RATE = 0.8
DECAY = 0.1
ADAM_EPS = 1e-08
CLIP = 1.0
HIGH = lax.Precision.HIGHEST

def matmul(left, right):
    return jnp.dot(left, right, precision=HIGH, preferred_element_type=jnp.float32)

def rms(value, gain):
    return value * lax.rsqrt(lax.optimization_barrier(jnp.mean(value * value, axis=-1, keepdims=True)) + EPS) * gain

def rope_tables(rows, columns, head):
    quarter = head // 4
    frequency = THETA ** (-jnp.arange(quarter, dtype=jnp.float32) / quarter)
    angles = jnp.concatenate([rows.astype(jnp.float32)[:, None] * frequency[None, :], columns.astype(jnp.float32)[:, None] * frequency[None, :]], axis=1)
    return (jnp.cos(angles)[:, None, :], jnp.sin(angles)[:, None, :])

def rotate(value, cosine, sine):
    middle = value.shape[-1] // 2
    first = value[..., :middle]
    second = value[..., middle:]
    return jnp.concatenate([first * cosine - second * sine, second * cosine + first * sine], axis=-1)

def split_heads(value):
    return value.reshape(value.shape[0], HEADS, HEAD)

def row_attention(queries, keys, values, text_keys, text_values, segment, lengths):
    scale = HEAD ** (-0.5)
    block = min(512, TOK_DEV)
    slot_ids = jnp.arange(IMG_DEV * CAP, dtype=jnp.int32)
    slot_image = slot_ids // CAP
    slot_live = slot_ids % CAP < lengths[slot_image]

    def attend(pair):
        query, ids = pair
        scores = low_back(jnp.einsum('qhd,khd->hqk', query, keys, precision=HIGH) * scale)
        scores = jnp.where((ids[:, None] == segment[None, :])[None], scores, NEG)
        probs = jax.nn.softmax(scores, axis=-1)
        own = low_back(jnp.einsum('hqk,khd->qhd', low(probs), values, precision=HIGH))
        cross = low_back(jnp.einsum('qhd,khd->hqk', query, text_keys, precision=HIGH) * scale)
        allowed = (ids[:, None] == slot_image[None, :]) & slot_live[None, :]
        cross = jnp.where(allowed[None], cross, NEG)
        cross_probs = jax.nn.softmax(cross, axis=-1)
        other = low_back(jnp.einsum('hqk,khd->qhd', low(cross_probs), text_values, precision=HIGH))
        return (own, other)
    count = TOK_DEV // block
    own, other = lax.map(jax.checkpoint(attend), (queries.reshape(count, block, HEADS, HEAD), segment.reshape(count, block)))
    return (own.reshape(TOK_DEV, HEADS, HEAD), other.reshape(TOK_DEV, HEADS, HEAD))

def layer(source, attention_in, attention_out, feed_in, feed_out, caption_in, modulator, channels, captions, conditions, image_ids, rope_rows, rope_cols, caption_lengths):
    augmented = low(jnp.concatenate([jax.nn.silu(conditions), jnp.ones((IMAGES, 1), jnp.float32)], axis=1))
    factors = matmul(augmented, modulator)
    image_index = (jnp.arange(ROWS, dtype=jnp.int32)[:, None] * IMG_DEV + image_ids).reshape(-1)
    token_factor = factors[image_index]
    scale_attn = token_factor[:, :D]
    gate_attn = token_factor[:, D:2 * D]
    scale_feed = token_factor[:, 2 * D:3 * D]
    gate_feed = token_factor[:, 3 * D:]
    attn_input = low(rms(source, channels[0]) * (1.0 + scale_attn))
    query_raw = low_back(matmul(attn_input, attention_in[0]))
    key_raw = low_back(matmul(attn_input, attention_in[1]))
    values = low(low_back(matmul(attn_input, attention_in[2])))
    cosine, sine = rope_tables(rope_rows.reshape(-1), rope_cols.reshape(-1), HEAD)
    queries = low(rotate(rms(split_heads(query_raw), channels[4].reshape(HEADS, HEAD)), cosine, sine))
    keys = low(rotate(rms(split_heads(key_raw), channels[5].reshape(HEADS, HEAD)), cosine, sine))
    text_keys = low(rms(split_heads(low_back(matmul(captions, caption_in[0]))), channels[6].reshape(HEADS, HEAD)))
    text_values = low(split_heads(low_back(matmul(captions, caption_in[1]))))
    shape_rows = (ROWS, TOK_DEV, HEADS, HEAD)
    shape_text = (ROWS, IMG_DEV * CAP, HEADS, HEAD)
    own, other = lax.map(lambda group: row_attention(*group), (queries.reshape(shape_rows), keys.reshape(shape_rows), split_heads(values).reshape(shape_rows), text_keys.reshape(shape_text), text_values.reshape(shape_text), image_ids, caption_lengths))
    own = own.reshape(TOKENS, HEADS, HEAD)
    other = other.reshape(TOKENS, HEADS, HEAD)
    mixed = low((own + jnp.tanh(channels[7]).reshape(HEADS, HEAD) * other).reshape(TOKENS, D))
    attn_sum = low_back(matmul(mixed, attention_out))
    middle = source + jnp.tanh(gate_attn) * rms(attn_sum, channels[1])
    feed_input = low(rms(middle, channels[2]) * (1.0 + scale_feed))
    gate_part = low_back(matmul(feed_input, feed_in[0]))
    up_part = low_back(matmul(feed_input, feed_in[1]))
    hidden = low(jax.nn.silu(gate_part) * up_part)
    feed_sum = low_back(matmul(hidden, feed_out))
    return middle + jnp.tanh(gate_feed) * rms(feed_sum, channels[3])

def adamw(grad, weight, moment, square, decay, rate):
    moment_new = BETA1 * moment + (1.0 - BETA1) * grad
    square_new = BETA2 * square + (1.0 - BETA2) * grad * grad
    step_size = moment_new / (1.0 - BETA1 ** STEP) / (jnp.sqrt(square_new / (1.0 - BETA2 ** STEP)) + ADAM_EPS)
    return (moment_new, square_new, weight - rate * (step_size + decay * weight))

def rounded(weight):
    return lax.optimization_barrier(weight.astype(jnp.bfloat16)).astype(jnp.float32)

def reference(latents, cotangent, captions, conditions, image_ids, rope_rows, rope_cols, caption_lengths, attention_in, attention_out, feed_in, feed_out, caption_in, modulator, channels, moment_attention_in, square_attention_in, moment_attention_out, square_attention_out, moment_feed_in, square_feed_in, moment_feed_out, square_feed_out, moment_caption_in, square_caption_in, moment_modulator, square_modulator, moment_channels, square_channels):
    masters = (attention_in, attention_out, feed_in, feed_out, caption_in, modulator, channels)
    params = tuple((rounded(weight) for weight in masters))
    captions_wide = captions.astype(jnp.float32)

    def run(source, *weights):
        return layer(source, *weights, captions_wide, conditions, image_ids, rope_rows, rope_cols, caption_lengths)
    block_out, pull = jax.vjp(run, latents.astype(jnp.float32), *params)
    grads = pull(cotangent)
    latent_grad = grads[0]
    weight_grads = grads[1:]
    total = jnp.zeros((), jnp.float32)
    for grad in weight_grads:
        total = total + jnp.sum(grad * grad)
    grad_norm = jnp.sqrt(total)
    factor = CLIP / jnp.maximum(grad_norm, CLIP)
    results = []
    moments = (moment_attention_in, moment_attention_out, moment_feed_in, moment_feed_out, moment_caption_in, moment_modulator, moment_channels)
    squares = (square_attention_in, square_attention_out, square_feed_in, square_feed_out, square_caption_in, square_modulator, square_channels)
    decays = (DECAY, DECAY, DECAY, DECAY, DECAY, DECAY, 0.0)
    rates = (RATE, RATE, RATE, RATE, RATE, RATE, GAIN_RATE)
    for grad, weight, moment, square, decay, rate in zip(weight_grads, masters, moments, squares, decays, rates):
        results.append(adamw(grad * factor, weight, moment, square, decay, rate))
    return (block_out, latent_grad, grad_norm, results[0][0], results[0][1], results[0][2], results[1][0], results[1][1], results[1][2], results[2][0], results[2][1], results[2][2], results[3][0], results[3][1], results[3][2], results[4][0], results[4][1], results[4][2], results[5][0], results[5][1], results[5][2], results[6][0], results[6][1], results[6][2])
```

```python
import functools
import math

import jax
import jax.numpy as jnp
from jax import lax
from jax.experimental import pallas as pl
from jax.experimental.pallas import tpu as pltpu
from jax.sharding import PartitionSpec as P

HEAD = 64
CAP = 256
STEP = 10


EPS = 1e-06
NEG = -1e30
THETA = 10000.0
BETA1 = 0.9
BETA2 = 0.95
RATE = 0.05
GAIN_RATE = 0.8
DECAY = 0.1
ADAM_EPS = 1e-08
CLIP = 1.0
HIGH = lax.Precision.HIGHEST


def half(value):
    return value.astype(jnp.bfloat16)


TILE = 256
LOG2E = 1.0 / math.log(2.0)


def dot(left, right, left_dim, right_dim):
    return lax.dot_general(
        left, right, (((left_dim,), (right_dim,)), ((), ())), preferred_element_type=jnp.float32
    )


def rms_parts(value, axis=-1):
    inverse = lax.rsqrt(jnp.mean(value * value, axis=axis, keepdims=True) + EPS)
    return (value * inverse, inverse)


def rms_back(normed, inverse, grad, axis=-1):
    return inverse * (grad - normed * jnp.mean(grad * normed, axis=axis, keepdims=True))


def rope_tables(rows, columns):
    quarter = HEAD // 4
    frequency = THETA ** (-jnp.arange(quarter, dtype=jnp.float32) / quarter)
    angles = jnp.concatenate(
        [
            frequency[:, None] * rows.astype(jnp.float32)[None, :],
            frequency[:, None] * columns.astype(jnp.float32)[None, :],
        ],
        axis=0,
    )
    return (jnp.cos(angles)[None], jnp.sin(angles)[None])


def rotate(value, cosine, sine):
    middle = value.shape[1] // 2
    first = value[:, :middle]
    second = value[:, middle:]
    return jnp.concatenate(
        [first * cosine - second * sine, second * cosine + first * sine], axis=1
    )


def near_swap(value):
    return lax.ppermute(value, "dp", [(i, i ^ 1) for i in range(lax.axis_size("dp"))])


def far_groups():
    count = lax.axis_size("dp")
    return [list(range(near, count, 2)) for near in range(2)]


def gather_dp(value, near_first=False):
    odd = lax.axis_index("dp") % 2
    groups = far_groups()
    if near_first:
        other = near_swap(value)
        pair = jnp.concatenate(
            [jnp.where(odd == 0, value, other), jnp.where(odd == 0, other, value)], axis=0
        )
        return lax.all_gather(pair, "dp", axis=0, tiled=True, axis_index_groups=groups)
    line = lax.all_gather(value, "dp", axis=0, tiled=True, axis_index_groups=groups)
    other = near_swap(line)
    rows, columns = value.shape
    line = line.reshape(-1, rows, columns)
    other = other.reshape(-1, rows, columns)
    both = jnp.stack(
        [jnp.where(odd == 0, line, other), jnp.where(odd == 0, other, line)], axis=1
    )
    return both.reshape(-1, columns)


def scatter_dp(value):
    count = lax.axis_size("dp")
    odd = lax.axis_index("dp") % 2
    rows, columns = value.shape[0] // count, value.shape[1]
    parts = value.reshape(count // 2, 2, rows, columns)
    keep = lax.dynamic_index_in_dim(parts, odd, 1, keepdims=False)
    send = lax.dynamic_index_in_dim(parts, 1 - odd, 1, keepdims=False)
    got = near_swap(send.reshape(-1, columns)).reshape(-1, rows, columns)
    summed = half(keep.astype(jnp.float32) + got.astype(jnp.float32)).reshape(-1, columns)
    return lax.psum_scatter(
        summed, "dp", scatter_dimension=0, tiled=True, axis_index_groups=far_groups()
    )


def swap_tensor(value, bits):
    return lax.ppermute(value, "tensor", [(i, i ^ bits) for i in range(lax.axis_size("tensor"))])


def owner(place):
    if lax.axis_size("tensor") == 4:
        return lax.axis_index("tensor") ^ place
    return jnp.int32(place)


def spread(value):
    count = lax.axis_size("tensor")
    if count == 4:
        near = swap_tensor(value, 1)
        far = swap_tensor(value, 2)
        return [value, near, far, swap_tensor(far, 1)]
    whole = lax.all_gather(value, "tensor", axis=0, tiled=False)
    return [whole[i] for i in range(count)]


def collect(parts):
    if len(parts) == 4:
        rows = parts[0].shape[0]
        sent = swap_tensor(half(jnp.concatenate([parts[3], parts[1]], axis=0)), 1)
        sent = sent.astype(jnp.float32)
        far = swap_tensor(half(parts[2] + sent[:rows]), 2)
        return parts[0] + sent[rows:] + far.astype(jnp.float32)
    return lax.psum_scatter(
        half(jnp.concatenate(parts, axis=0)), "tensor", scatter_dimension=0, tiled=True
    ).astype(jnp.float32)


def in_place(blocks):
    if len(blocks) == 4:
        stacked = jnp.stack(blocks)
        mine = lax.axis_index("tensor")
        blocks = [
            lax.dynamic_index_in_dim(stacked, mine ^ i, 0, keepdims=False)
            for i in range(len(blocks))
        ]
    return jnp.concatenate(blocks, axis=0)


def attention_bias(cross, step, ids_row, ids_column, lengths):
    if cross:
        slots = lax.broadcasted_iota(jnp.int32, (TILE, 1), 0) < lengths[step]
        return jnp.where(slots & (ids_row[...] == step), 0.0, NEG)
    start = pl.multiple_of(step * TILE, TILE)
    return jnp.where(ids_column[pl.ds(start, TILE), :] == ids_row[...], 0.0, NEG)


def attention_kernel(
    heads, cross, meta, lengths, ids_row, ids_column, q_ref, k_ref, v_ref, out_ref, inv_ref, total
):
    place = pl.program_id(0)
    base = 2 * place
    factor = HEAD ** (-0.5) * LOG2E
    out_ref[...] = jnp.zeros_like(out_ref)
    total[...] = jnp.zeros_like(total)

    def step(index, carry):
        bias = attention_bias(cross, index, ids_row, ids_column, lengths)
        rows = pl.ds(pl.multiple_of(index * TILE, TILE), TILE)
        for head in range(heads):
            span = slice(head * HEAD, (head + 1) * HEAD)
            scores = dot(k_ref[head, rows, :], q_ref[span, :], 1, 0)
            expo = jnp.exp2(scores * factor + bias)
            total[head] += jnp.sum(expo.reshape(TILE // 8, 8, TILE), axis=0)
            out_ref[span, :] += dot(v_ref[span, rows], half(expo), 1, 0)
        return carry

    lax.fori_loop(meta[base], meta[base + 1], step, 0)
    for head in range(heads):
        span = slice(head * HEAD, (head + 1) * HEAD)
        inverse = 1.0 / jnp.sum(total[head], axis=0, keepdims=True)
        inv_ref[head] = jnp.broadcast_to(inverse, (8, TILE))
        out_ref[span, :] = out_ref[span, :] * inverse


def attention_back_kernel(
    heads,
    cross,
    meta,
    lengths,
    ids_row,
    ids_column,
    q_ref,
    k_ref,
    kt_ref,
    v_ref,
    inv_ref,
    o_ref,
    do_ref,
    dq_ref,
    dk_ref,
    dv_ref,
    centre,
):
    place = pl.program_id(0)
    base = 2 * place
    scale = HEAD ** (-0.5)
    factor = scale * LOG2E

    @pl.when(place == 0)
    def _():
        dk_ref[...] = jnp.zeros_like(dk_ref)
        dv_ref[...] = jnp.zeros_like(dv_ref)

    dq_ref[...] = jnp.zeros_like(dq_ref)
    for head in range(heads):
        span = slice(head * HEAD, (head + 1) * HEAD)
        both = o_ref[span, :] * do_ref[span, :].astype(jnp.float32)
        centre[head] = jnp.broadcast_to(jnp.sum(both, axis=0, keepdims=True), (8, TILE))

    def step(index, carry):
        bias = attention_bias(cross, index, ids_row, ids_column, lengths)
        rows = pl.ds(pl.multiple_of(index * TILE, TILE), TILE)
        for head in range(heads):
            span = slice(head * HEAD, (head + 1) * HEAD)
            query = q_ref[span, :]
            back = do_ref[span, :]
            scores = dot(k_ref[head, rows, :], query, 1, 0)
            probs = jnp.exp2(scores * factor + bias) * inv_ref[head, 0:1, :]
            prob_grad = dot(v_ref[head, rows, :], back, 1, 0)
            score_grad = half(probs * (prob_grad - centre[head, 0:1, :]))
            dv_ref[span, rows] += dot(back, half(probs), 1, 1)
            dk_ref[span, rows] += dot(query, score_grad, 1, 1) * scale
            dq_ref[span, :] += dot(kt_ref[span, rows], score_grad, 1, 0) * scale
        return carry

    lax.fori_loop(meta[base], meta[base + 1], step, 0)


def whole_block(array):
    return pl.BlockSpec(array.shape, lambda i, *_: (0,) * array.ndim)


def tile_block(array):
    lead = array.shape[:-1]
    return pl.BlockSpec((*lead, TILE), lambda i, *_: (*([0] * len(lead)), i))


def attention(cross, meta, lengths, ids_row, ids_column, query, key_rows, value):
    local, tokens = query.shape
    heads = local // HEAD
    outs = (
        jax.ShapeDtypeStruct((local, tokens), jnp.float32),
        jax.ShapeDtypeStruct((heads, 8, tokens), jnp.float32),
    )
    return pl.pallas_call(
        functools.partial(attention_kernel, heads, cross),
        grid_spec=pltpu.PrefetchScalarGridSpec(
            num_scalar_prefetch=2,
            grid=(tokens // TILE,),
            in_specs=[
                tile_block(ids_row),
                whole_block(ids_column),
                tile_block(query),
                whole_block(key_rows),
                whole_block(value),
            ],
            out_specs=[tile_block(out) for out in outs],
            scratch_shapes=[pltpu.VMEM((heads, 8, TILE), jnp.float32)],
        ),
        out_shape=outs,
        compiler_params=pltpu.CompilerParams(
            vmem_limit_bytes=48 * 1024 * 1024, dimension_semantics=("arbitrary",)
        ),
        cost_estimate=pl.CostEstimate(
            flops=4 * tokens * 512 * local,
            bytes_accessed=16 * tokens * local,
            transcendentals=tokens * 512 * heads,
        ),
        name="cross_forward" if cross else "self_forward",
    )(meta, lengths, ids_row, ids_column, query, key_rows, value)


def attention_back(
    cross, meta, lengths, ids_row, ids_column, query, key_rows, key, value_rows, inverse, out, grad
):
    local, tokens = query.shape
    heads = local // HEAD
    outs = (
        jax.ShapeDtypeStruct((local, tokens), jnp.float32),
        jax.ShapeDtypeStruct(key.shape, jnp.float32),
        jax.ShapeDtypeStruct(key.shape, jnp.float32),
    )
    return pl.pallas_call(
        functools.partial(attention_back_kernel, heads, cross),
        grid_spec=pltpu.PrefetchScalarGridSpec(
            num_scalar_prefetch=2,
            grid=(tokens // TILE,),
            in_specs=[
                tile_block(ids_row),
                whole_block(ids_column),
                tile_block(query),
                whole_block(key_rows),
                whole_block(key),
                whole_block(value_rows),
                tile_block(inverse),
                tile_block(out),
                tile_block(grad),
            ],
            out_specs=[tile_block(outs[0]), whole_block(outs[1]), whole_block(outs[2])],
            scratch_shapes=[pltpu.VMEM((heads, 8, TILE), jnp.float32)],
        ),
        out_shape=outs,
        compiler_params=pltpu.CompilerParams(
            vmem_limit_bytes=56 * 1024 * 1024, dimension_semantics=("arbitrary",)
        ),
        cost_estimate=pl.CostEstimate(
            flops=10 * tokens * 512 * local,
            bytes_accessed=30 * tokens * local,
            transcendentals=tokens * 512 * heads,
        ),
        name="cross_backward" if cross else "self_backward",
    )(
        meta,
        lengths,
        ids_row,
        ids_column,
        query,
        key_rows,
        key,
        value_rows,
        inverse,
        out,
        grad,
    )


def rows_of(value):
    return jnp.transpose(value.reshape(-1, HEAD, value.shape[1]), (0, 2, 1))


def adamw(grad, weight, moment, square, decay, rate):
    moment_new = BETA1 * moment + (1.0 - BETA1) * grad
    square_new = BETA2 * square + (1.0 - BETA2) * grad * grad
    step_size = (
        moment_new / (1.0 - BETA1**STEP) / (jnp.sqrt(square_new / (1.0 - BETA2**STEP)) + ADAM_EPS)
    )
    return (moment_new, square_new, weight - rate * (step_size + decay * weight))


def body(
    latents,
    cotangent,
    captions,
    conditions,
    image_ids,
    rope_rows,
    rope_cols,
    caption_lengths,
    attention_in,
    attention_out,
    feed_in,
    feed_out,
    caption_in,
    modulator,
    channels,
    moment_attention_in,
    square_attention_in,
    moment_attention_out,
    square_attention_out,
    moment_feed_in,
    square_feed_in,
    moment_feed_out,
    square_feed_out,
    moment_caption_in,
    square_caption_in,
    moment_modulator,
    square_modulator,
    moment_channels,
    square_channels,
):
    tensor_size = lax.axis_size("tensor")
    tensor_index = lax.axis_index("tensor")
    dp_size = lax.axis_size("dp")
    dp_index = lax.axis_index("dp")
    shard_rows, width = latents.shape
    local = attention_in.shape[2]
    heads = local // HEAD
    units = feed_in.shape[2]
    segment = image_ids[0]
    row_tokens = segment.shape[0]
    images = conditions.shape[0]
    per_row = caption_lengths.shape[1]
    lengths = caption_lengths[0]
    slots = captions.shape[0]
    offset = tensor_index * local
    own_ids = lax.dynamic_slice_in_dim(segment, tensor_index * shard_rows, shard_rows)

    caption_half = half(caption_in)
    key_full = gather_dp(caption_half[0].T)
    value_full = gather_dp(caption_half[1].T)
    in_half = half(attention_in)
    in_full = gather_dp(jnp.concatenate([in_half[0], in_half[1], in_half[2]], axis=1))
    out_full = gather_dp(half(attention_out).T)
    feed_half = half(feed_in)
    feed_full = gather_dp(jnp.concatenate([feed_half[0], feed_half[1]], axis=1))
    down_full = gather_dp(half(feed_out).T, near_first=True)

    channel_half = lax.all_gather(half(channels), "dp", axis=1, tiled=True)
    gains = channel_half.astype(jnp.float32)
    local_gains = lax.dynamic_slice_in_dim(gains, offset, local, 1).reshape(8, heads, HEAD, 1)
    augmented = half(
        jnp.concatenate([jax.nn.silu(conditions), jnp.ones((images, 1), jnp.float32)], axis=1)
    )
    factor_part = jnp.dot(augmented, half(modulator), preferred_element_type=jnp.float32)
    own_columns = factor_part.shape[1]
    factor_moved = lax.all_to_all(
        factor_part.reshape(dp_size, per_row, own_columns), "dp", 0, 0, tiled=True
    )
    factor_row = lax.all_gather(factor_moved, "tensor", axis=0, tiled=False)
    factor_row = jnp.transpose(factor_row, (2, 1, 0, 3)).reshape(per_row, -1)
    chooser = (own_ids[:, None] == jnp.arange(per_row, dtype=jnp.int32)[None, :]).astype(
        jnp.float32
    )
    token_factor = jnp.dot(chooser, factor_row, precision=HIGH)
    scale_attn = token_factor[:, :width]
    gate_attn = token_factor[:, width : 2 * width]
    scale_feed = token_factor[:, 2 * width : 3 * width]
    gate_feed = token_factor[:, 3 * width :]

    def caption_project(weight):
        return collect(
            [
                dot(
                    lax.dynamic_slice_in_dim(weight, owner(i) * local, local), captions, 1, 1
                )
                for i in range(tensor_size)
            ]
        )

    text_key_norm, text_key_inv = rms_parts(
        caption_project(key_full).reshape(heads, HEAD, slots), 1
    )
    text_keys = half(text_key_norm * local_gains[6]).reshape(local, slots)
    text_values = half(caption_project(value_full))
    text_key_rows, text_value_rows = rows_of(text_keys), rows_of(text_values)

    source = latents.astype(jnp.float32)
    attn_norm, attn_inv = rms_parts(source)
    attn_full = in_place(spread(half(attn_norm * gains[0] * (1.0 + scale_attn))))
    projected = dot(in_full, attn_full, 0, 1)
    query_norm, query_inv = rms_parts(projected[:local].reshape(heads, HEAD, row_tokens), 1)
    key_norm, key_inv = rms_parts(
        projected[local : 2 * local].reshape(heads, HEAD, row_tokens), 1
    )
    cosine, sine = rope_tables(rope_rows[0], rope_cols[0])
    queries = half(rotate(query_norm * local_gains[4], cosine, sine)).reshape(local, row_tokens)
    keys = half(rotate(key_norm * local_gains[5], cosine, sine)).reshape(local, row_tokens)
    values = half(projected[2 * local :])
    key_rows, value_rows = rows_of(keys), rows_of(values)

    tiles = row_tokens // TILE
    first_id = segment.reshape(tiles, TILE)[:, 0]
    last_id = segment.reshape(tiles, TILE)[:, TILE - 1]
    low = jnp.sum((segment[None] < first_id[:, None]).astype(jnp.int32), axis=1) // TILE
    high = (
        jnp.sum((segment[None] <= last_id[:, None]).astype(jnp.int32), axis=1) + TILE - 1
    ) // TILE
    self_meta = jnp.stack([low, high], axis=1).reshape(-1)
    cross_meta = jnp.stack([first_id, last_id + 1], axis=1).reshape(-1)
    ids_row = image_ids
    ids_column = segment[:, None]
    own_out, own_inv = attention(
        False, self_meta, lengths, ids_row, ids_column, queries, key_rows, values
    )
    other_out, other_inv = attention(
        True, cross_meta, lengths, ids_row, ids_column, queries, text_key_rows, text_values
    )
    cross_gate = jnp.tanh(local_gains[7]).reshape(local, 1)
    mixed = half(own_out + cross_gate * other_out)
    attn_sum = collect(
        [
            dot(
                lax.dynamic_slice_in_dim(mixed, owner(i) * shard_rows, shard_rows, 1),
                out_full,
                0,
                1,
            )
            for i in range(tensor_size)
        ]
    )
    first_norm, first_inv = rms_parts(attn_sum)
    branch_attn = first_norm * gains[1]
    tanh_attn = jnp.tanh(gate_attn)
    middle = source + tanh_attn * branch_attn
    feed_norm, feed_inv = rms_parts(middle)
    feed_all = jnp.concatenate(spread(half(feed_norm * gains[2] * (1.0 + scale_feed))), axis=0)
    gate_up = dot(feed_all, feed_full, 1, 0)
    gate_part, up_part = gate_up[:, :units], gate_up[:, units:]
    sigmoid_gate = jax.nn.sigmoid(gate_part)
    silu_gate = gate_part * sigmoid_gate
    hidden = half(silu_gate * up_part)

    def split(value):
        return [value[i * shard_rows : (i + 1) * shard_rows] for i in range(tensor_size)]

    feed_sum = collect(split(dot(hidden, down_full, 1, 1)))
    second_norm, second_inv = rms_parts(feed_sum)
    branch_feed = second_norm * gains[3]
    tanh_feed = jnp.tanh(gate_feed)
    block_out = middle + tanh_feed * branch_feed
    branch_feed_grad = tanh_feed * cotangent
    gate_feed_grad = cotangent * branch_feed * (1.0 - tanh_feed * tanh_feed)
    feed_sum_grad = jnp.concatenate(
        spread(half(rms_back(second_norm, second_inv, branch_feed_grad * gains[3]))), axis=0
    )
    hidden_grad = dot(feed_sum_grad, down_full, 1, 0)
    feed_out_sum = scatter_dp(half(dot(feed_sum_grad, hidden, 0, 0)))
    gate_grad = (
        hidden_grad * up_part * (sigmoid_gate + gate_part * sigmoid_gate * (1.0 - sigmoid_gate))
    )
    up_grad = hidden_grad * silu_gate
    pair_grad = jnp.concatenate([half(gate_grad), half(up_grad)], axis=1)
    feed_input_grad = collect(split(dot(pair_grad, feed_full, 1, 1)))
    feed_in_sum = scatter_dp(half(dot(feed_all, pair_grad, 0, 0)))
    scale_feed_grad = feed_input_grad * feed_norm * gains[2]
    middle_grad = cotangent + rms_back(
        feed_norm, feed_inv, feed_input_grad * gains[2] * (1.0 + scale_feed)
    )
    branch_attn_grad = tanh_attn * middle_grad
    gate_attn_grad = middle_grad * branch_attn * (1.0 - tanh_attn * tanh_attn)
    attn_sum_grad = in_place(
        spread(half(rms_back(first_norm, first_inv, branch_attn_grad * gains[1])))
    )
    mixed_grad = dot(out_full, attn_sum_grad, 0, 1)
    out_sum = scatter_dp(half(dot(attn_sum_grad, mixed, 0, 1)))
    gate_channel_grad = jnp.sum(mixed_grad * other_out, axis=1, keepdims=True) * (
        1.0 - cross_gate * cross_gate
    )
    own_grad = half(mixed_grad)
    other_grad = half(cross_gate * mixed_grad)
    query_two, text_key_grad, text_value_grad = attention_back(
        True,
        cross_meta,
        lengths,
        ids_row,
        ids_column,
        queries,
        text_key_rows,
        text_keys,
        text_value_rows,
        other_inv,
        other_out,
        other_grad,
    )
    text_value_full = in_place(spread(half(text_value_grad)))
    text_key_grad = text_key_grad.reshape(heads, HEAD, slots)
    text_gain_grad = jnp.sum(text_key_grad * text_key_norm, axis=2)
    text_raw_grad = rms_back(text_key_norm, text_key_inv, text_key_grad * local_gains[6], 1)
    text_key_full = in_place(spread(half(text_raw_grad).reshape(local, slots)))
    value_sum = scatter_dp(half(dot(text_value_full, captions, 1, 0)))
    key_sum = scatter_dp(half(dot(text_key_full, captions, 1, 0)))
    query_one, key_rot_grad, value_grad = attention_back(
        False,
        self_meta,
        lengths,
        ids_row,
        ids_column,
        queries,
        key_rows,
        keys,
        value_rows,
        own_inv,
        own_out,
        own_grad,
    )
    query_turn = rotate(
        (query_one + query_two).reshape(heads, HEAD, row_tokens), cosine, -sine
    )
    key_turn = rotate(key_rot_grad.reshape(heads, HEAD, row_tokens), cosine, -sine)
    query_gain_grad = jnp.sum(query_turn * query_norm, axis=2)
    key_gain_grad = jnp.sum(key_turn * key_norm, axis=2)
    query_raw_grad = rms_back(query_norm, query_inv, query_turn * local_gains[4], 1)
    key_raw_grad = rms_back(key_norm, key_inv, key_turn * local_gains[5], 1)
    triple_grad = jnp.concatenate(
        [
            half(query_raw_grad).reshape(local, row_tokens),
            half(key_raw_grad).reshape(local, row_tokens),
            half(value_grad),
        ],
        axis=0,
    )
    attn_input_grad = collect(
        [
            dot(
                lax.dynamic_slice_in_dim(triple_grad, owner(i) * shard_rows, shard_rows, 1),
                in_full,
                0,
                1,
            )
            for i in range(tensor_size)
        ]
    )
    in_sum = scatter_dp(half(dot(attn_full, triple_grad, 0, 1)))
    scale_attn_grad = attn_input_grad * attn_norm * gains[0]
    latent_grad = middle_grad + rms_back(
        attn_norm, attn_inv, attn_input_grad * gains[0] * (1.0 + scale_attn)
    )
    shared_rows = jnp.stack(
        [
            jnp.sum(attn_input_grad * attn_norm * (1.0 + scale_attn), axis=0),
            jnp.sum(branch_attn_grad * first_norm, axis=0),
            jnp.sum(feed_input_grad * feed_norm * (1.0 + scale_feed), axis=0),
            jnp.sum(branch_feed_grad * second_norm, axis=0),
        ]
    )
    head_rows = jnp.stack(
        [
            query_gain_grad.reshape(local),
            key_gain_grad.reshape(local),
            text_gain_grad.reshape(local),
            gate_channel_grad.reshape(local),
        ]
    )
    head_full = lax.dynamic_update_slice(
        jnp.zeros((4, width), jnp.float32), head_rows, (jnp.zeros((), jnp.int32), offset)
    )
    channel_total = lax.psum(
        jnp.concatenate([shared_rows, head_full], axis=0), ("dp", "tensor")
    )
    channel_columns = channels.shape[1]
    channel_sum = lax.dynamic_slice_in_dim(
        channel_total, dp_index * channel_columns, channel_columns, 1
    )
    factor_tokens = jnp.concatenate(
        [scale_attn_grad, gate_attn_grad, scale_feed_grad, gate_feed_grad], axis=1
    )
    factor_image = jnp.dot(chooser.T, factor_tokens, precision=HIGH)
    factor_image = jnp.transpose(
        factor_image.reshape(per_row, dp_size, tensor_size, own_columns), (2, 1, 0, 3)
    )
    factor_mine = lax.psum_scatter(factor_image, "tensor", scatter_dimension=0, tiled=False)
    factor_grad = lax.all_to_all(factor_mine, "dp", 0, 0, tiled=True).reshape(images, own_columns)
    modulator_sum = jnp.dot(augmented.astype(jnp.float32).T, factor_grad, precision=HIGH)

    in_sum, out_sum, feed_in_sum, feed_out_sum, key_sum, value_sum = (
        value.astype(jnp.float32)
        for value in (in_sum, out_sum, feed_in_sum, feed_out_sum, key_sum, value_sum)
    )
    squares = (
        jnp.sum(in_sum * in_sum)
        + jnp.sum(out_sum * out_sum)
        + jnp.sum(feed_in_sum * feed_in_sum)
        + jnp.sum(feed_out_sum * feed_out_sum)
        + jnp.sum(key_sum * key_sum)
        + jnp.sum(value_sum * value_sum)
        + jnp.sum(modulator_sum * modulator_sum)
        + jnp.sum(channel_sum * channel_sum) / tensor_size
    )
    in_sum = jnp.stack([in_sum[:, i * local : (i + 1) * local] for i in range(3)])
    feed_in_sum = jnp.stack([feed_in_sum[:, i * units : (i + 1) * units] for i in range(2)])
    caption_sum = jnp.stack([key_sum.T, value_sum.T])
    grad_norm = jnp.sqrt(lax.psum(squares, ("dp", "tensor")))
    factor = CLIP / jnp.maximum(grad_norm, CLIP)
    results = [
        adamw(grad * factor, weight, moment, square, DECAY, RATE)
        for grad, weight, moment, square in (
            (in_sum, attention_in, moment_attention_in, square_attention_in),
            (out_sum.T, attention_out, moment_attention_out, square_attention_out),
            (feed_in_sum, feed_in, moment_feed_in, square_feed_in),
            (feed_out_sum.T, feed_out, moment_feed_out, square_feed_out),
            (caption_sum, caption_in, moment_caption_in, square_caption_in),
            (modulator_sum, modulator, moment_modulator, square_modulator),
        )
    ]
    results.append(
        adamw(channel_sum * factor, channels, moment_channels, square_channels, 0.0, GAIN_RATE)
    )
    return (block_out, latent_grad, grad_norm, *(part for result in results for part in result))


def solution(mesh):
    return jax.shard_map(
        body,
        mesh=mesh,
        in_specs=(
            P(("dp", "tensor"), None),
            P(("dp", "tensor"), None),
            P("dp", "tensor"),
            P(),
            P("dp", None),
            P("dp", None),
            P("dp", None),
            P("dp", None),
            P(None, "dp", "tensor"),
            P("tensor", "dp"),
            P(None, "dp", "tensor"),
            P("tensor", "dp"),
            P(None, "tensor", "dp"),
            P(None, ("dp", "tensor")),
            P(None, "dp"),
            P(None, "dp", "tensor"),
            P(None, "dp", "tensor"),
            P("tensor", "dp"),
            P("tensor", "dp"),
            P(None, "dp", "tensor"),
            P(None, "dp", "tensor"),
            P("tensor", "dp"),
            P("tensor", "dp"),
            P(None, "tensor", "dp"),
            P(None, "tensor", "dp"),
            P(None, ("dp", "tensor")),
            P(None, ("dp", "tensor")),
            P(None, "dp"),
            P(None, "dp"),
        ),
        out_specs=(
            P(("dp", "tensor"), None),
            P(("dp", "tensor"), None),
            P(),
            P(None, "dp", "tensor"),
            P(None, "dp", "tensor"),
            P(None, "dp", "tensor"),
            P("tensor", "dp"),
            P("tensor", "dp"),
            P("tensor", "dp"),
            P(None, "dp", "tensor"),
            P(None, "dp", "tensor"),
            P(None, "dp", "tensor"),
            P("tensor", "dp"),
            P("tensor", "dp"),
            P("tensor", "dp"),
            P(None, "tensor", "dp"),
            P(None, "tensor", "dp"),
            P(None, "tensor", "dp"),
            P(None, ("dp", "tensor")),
            P(None, ("dp", "tensor")),
            P(None, ("dp", "tensor")),
            P(None, "dp"),
            P(None, "dp"),
            P(None, "dp"),
        ),
        check_vma=False,
    )
```

```python
import functools
import math

import jax
import jax.numpy as jnp
from jax import lax
from jax.experimental import pallas as pl
from jax.experimental.pallas import tpu as pltpu
from jax.sharding import PartitionSpec as P

HEAD = 64
CAP = 256
STEP = 10


EPS = 1e-06
NEG = -1e30
THETA = 10000.0
BETA1 = 0.9
BETA2 = 0.95
RATE = 0.05
GAIN_RATE = 0.8
DECAY = 0.1
ADAM_EPS = 1e-08
CLIP = 1.0
HIGH = lax.Precision.HIGHEST


def half(value):
    return value.astype(jnp.bfloat16)


TILE = 256
LOG2E = 1.0 / math.log(2.0)
MESH = pl.DeviceIdType.MESH


def dot(left, right, left_dim, right_dim):
    return lax.dot_general(
        left, right, (((left_dim,), (right_dim,)), ((), ())), preferred_element_type=jnp.float32
    )


def rms_parts(value, axis=-1):
    inverse = lax.rsqrt(jnp.mean(value * value, axis=axis, keepdims=True) + EPS)
    return (value * inverse, inverse)


def rms_back(normed, inverse, grad, axis=-1):
    return inverse * (grad - normed * jnp.mean(grad * normed, axis=axis, keepdims=True))


def rope_tables(rows, columns):
    quarter = HEAD // 4
    frequency = THETA ** (-jnp.arange(quarter, dtype=jnp.float32) / quarter)
    angles = jnp.concatenate(
        [
            frequency[:, None] * rows.astype(jnp.float32)[None, :],
            frequency[:, None] * columns.astype(jnp.float32)[None, :],
        ],
        axis=0,
    )
    return (jnp.cos(angles), jnp.sin(angles))


def gate_kernel(value, after, out):
    del value, after, out


def gate(value, after):
    anywhere = pl.BlockSpec(memory_space=pl.ANY)
    return pl.pallas_call(
        gate_kernel,
        out_shape=jax.ShapeDtypeStruct(value.shape, value.dtype),
        in_specs=[anywhere, anywhere],
        out_specs=anywhere,
        input_output_aliases={0: 0},
        name="gate",
    )(value, after)


def near_swap(value):
    return lax.ppermute(value, "dp", [(i, i ^ 1) for i in range(lax.axis_size("dp"))])


def far_groups():
    count = lax.axis_size("dp")
    return [list(range(near, count, 2)) for near in range(2)]


def near_pair(value, other):
    odd = lax.axis_index("dp") % 2
    return jnp.concatenate(
        [jnp.where(odd == 0, value, other), jnp.where(odd == 0, other, value)], axis=0
    )


def gather_far(value):
    return lax.all_gather(value, "dp", axis=0, tiled=True, axis_index_groups=far_groups())


def join_near(line, other, rows, start=0, stop=None):
    odd = lax.axis_index("dp") % 2
    line = line[:, start:stop]
    other = other[:, start:stop]
    columns = line.shape[1]
    line = line.reshape(-1, rows, columns)
    other = other.reshape(-1, rows, columns)
    both = jnp.stack(
        [jnp.where(odd == 0, line, other), jnp.where(odd == 0, other, line)], axis=1
    )
    return both.reshape(-1, columns)


def swap_half(parts):
    odd = lax.axis_index("dp") % 2
    send = lax.dynamic_index_in_dim(parts, 1 - odd, 1, keepdims=False)
    return near_swap(send.reshape(-1, send.shape[2])).reshape(send.shape)


def scatter_far(parts, others):
    odd = lax.axis_index("dp") % 2
    summed = [
        half(
            lax.dynamic_index_in_dim(part, odd, 1, keepdims=False).astype(jnp.float32)
            + other.astype(jnp.float32)
        )
        for part, other in zip(parts, others)
    ]
    summed = jnp.concatenate(summed, axis=2)
    return lax.psum_scatter(
        summed.reshape(-1, summed.shape[2]),
        "dp",
        scatter_dimension=0,
        tiled=True,
        axis_index_groups=far_groups(),
    )


def swap_tensor(value, bits):
    return lax.ppermute(value, "tensor", [(i, i ^ bits) for i in range(lax.axis_size("tensor"))])


def owner(place):
    if lax.axis_size("tensor") == 4:
        return lax.axis_index("tensor") ^ place
    return jnp.int32(place)


def spread(value):
    count = lax.axis_size("tensor")
    if count == 4:
        near = swap_tensor(value, 1)
        far = swap_tensor(value, 2)
        return [value, near, far, swap_tensor(far, 1)]
    whole = lax.all_gather(value, "tensor", axis=0, tiled=False)
    return [whole[i] for i in range(count)]


def collect_near(parts):
    if len(parts) == 4:
        rows = parts[0].shape[0]
        sent = swap_tensor(half(jnp.concatenate([parts[3], parts[1]], axis=0)), 1)
        sent = sent.astype(jnp.float32)
        return (parts[0] + sent[rows:], half(parts[2] + sent[:rows]))
    return (half(jnp.concatenate(parts, axis=0)),)


def collect_far(sums):
    if len(sums) == 2:
        return sums[0] + swap_tensor(sums[1], 2).astype(jnp.float32)
    return lax.psum_scatter(
        sums[0], "tensor", scatter_dimension=0, tiled=True
    ).astype(jnp.float32)


def collect(parts):
    return collect_far(collect_near(parts))


def in_place(blocks):
    if len(blocks) == 4:
        stacked = jnp.stack(blocks)
        mine = lax.axis_index("tensor")
        blocks = [
            lax.dynamic_index_in_dim(stacked, mine ^ i, 0, keepdims=False)
            for i in range(len(blocks))
        ]
    return jnp.concatenate(blocks, axis=0)


def dp_neighbour():
    mine = lax.axis_index("dp")
    return mine + 1 - 2 * (mine % 2)


def meet(everyone, carries):
    barrier = pltpu.get_barrier_semaphore()
    if everyone:
        others = [
            {axis: (lax.axis_index(axis) + step) % lax.axis_size(axis)}
            for axis in ("dp", "tensor")
            for step in range(1, lax.axis_size(axis))
        ]
    else:
        _, near, far, _ = row_peers()
        others = [{"tensor": near}, {"tensor": far}]
        if carries:
            others.append({"dp": dp_neighbour()})
    for other in others:
        pl.semaphore_signal(barrier, inc=1, device_id=other, device_id_type=MESH)
    pl.semaphore_wait(barrier, len(others))


def remote_call(
    kernel, name, number, operands, outs, scratch, carry=(), everyone=False, after=()
):
    copies = sum(1 if len(array.shape) == 2 else array.shape[0] for array in carry)
    swapped = [
        jax.ShapeDtypeStruct(
            array.shape if len(array.shape) == 2 else (array.shape[0], *array.shape[2:]),
            array.dtype,
        )
        for array in carry
    ]

    def run(*refs):
        refs = list(refs)
        ins = [refs.pop(0) for _ in operands]
        sources = [refs.pop(0) for _ in carry]
        del refs[: len(after)]
        results = [refs.pop(0) for _ in outs]
        targets = [refs.pop(0) for _ in carry]
        meet(everyone, bool(carry))
        started = []
        if carry:
            sems = refs.pop()
            other = dp_neighbour()
            pairs = []
            for source, target in zip(sources, targets):
                if len(source.shape) == 2:
                    pairs.append((source, target))
                else:
                    pairs += [
                        (source.at[i, other % 2], target.at[i]) for i in range(source.shape[0])
                    ]
            for i, (source, target) in enumerate(pairs):
                copy = pltpu.make_async_remote_copy(
                    src_ref=source,
                    dst_ref=target,
                    send_sem=sems.at[0, i],
                    recv_sem=sems.at[1, i],
                    device_id={"dp": other},
                    device_id_type=MESH,
                )
                copy.start()
                started.append(copy)
        kernel(*ins, *results, *refs)
        for copy in started:
            copy.wait()

    whole = pl.BlockSpec(memory_space=pltpu.VMEM)
    anywhere = pl.BlockSpec(memory_space=pl.ANY)
    return pl.pallas_call(
        run,
        out_shape=[*outs, *swapped],
        in_specs=[whole] * len(operands) + [anywhere] * (len(carry) + len(after)),
        out_specs=[whole] * len(outs) + [anywhere] * len(carry),
        scratch_shapes=[
            *scratch,
            *([pltpu.SemaphoreType.DMA((2, copies))] if carry else []),
        ],
        compiler_params=pltpu.CompilerParams(
            collective_id=number, has_side_effects=True, vmem_limit_bytes=60 * 1024 * 1024
        ),
        name=name,
    )(*operands, *carry, *after)


def send_blocks(axis, pick, target, send_sem, recv_sem):
    count = lax.axis_size(axis)
    mine = lax.axis_index(axis)

    def copy(other, place):
        return pltpu.make_async_remote_copy(
            src_ref=pick(other),
            dst_ref=target.at[place],
            send_sem=send_sem.at[other],
            recv_sem=recv_sem.at[place],
            device_id={axis: other},
            device_id_type=MESH,
        )

    others = [(mine + step) % count for step in range(1, count)]
    for other in others:
        copy(other, mine).start()
    for other in others:
        copy(other, mine).wait_send()
        copy(other, other).wait_recv()


def spread_kernel(source, target, middle, send_dp, recv_dp, send_tensor, recv_tensor):
    mine = lax.axis_index("dp")
    middle[mine] = source[mine]
    send_blocks("dp", lambda other: source.at[other], middle, send_dp, recv_dp)
    target[lax.axis_index("tensor")] = middle[...]
    send_blocks("tensor", lambda other: middle, target, send_tensor, recv_tensor)


def return_kernel(
    source, target, middle, summed, last, send_dp, recv_dp, send_tensor, recv_tensor
):
    place = lax.axis_index("tensor")
    middle[place] = source[place]
    send_blocks("tensor", lambda other: source.at[other], middle, send_tensor, recv_tensor)
    total = middle[0]
    for other in range(1, lax.axis_size("tensor")):
        total += middle[other]
    summed[...] = total
    mine = lax.axis_index("dp")
    last[mine] = summed[mine]
    send_blocks("dp", lambda other: summed.at[other], last, send_dp, recv_dp)
    target[...] = last[...]


def total_kernel(source, target, near, far, part, send_dp, recv_dp, send_tensor, recv_tensor):
    near[lax.axis_index("tensor")] = source[...]
    send_blocks("tensor", lambda other: source, near, send_tensor, recv_tensor)
    part[...] = jnp.sum(near[...], axis=0)
    far[lax.axis_index("dp")] = part[...]
    send_blocks("dp", lambda other: part, far, send_dp, recv_dp)
    target[...] = jnp.sum(far[...], axis=0)


def exchange_scratch(shapes):
    sizes = (lax.axis_size("dp"),) * 2 + (lax.axis_size("tensor"),) * 2
    return [pltpu.VMEM(shape, jnp.float32) for shape in shapes] + [
        pltpu.SemaphoreType.DMA((size,)) for size in sizes
    ]


CHUNKS = 4


def row_peers():
    mine = lax.axis_index("tensor")
    near = mine + 1 - 2 * (mine % 2)
    return (mine, near, (mine + 2) % 4, (near + 2) % 4)


def remote(source, target, sems, index, other):
    return pltpu.make_async_remote_copy(
        src_ref=source,
        dst_ref=target,
        send_sem=sems.at[0, index],
        recv_sem=sems.at[1, index],
        device_id={"tensor": other},
        device_id_type=MESH,
    )


def chunk_rows(total):
    size = total // CHUNKS
    return [slice(i * size, (i + 1) * size) for i in range(CHUNKS)]


def sum_blocks(partial, finish, work, sems):
    mine, near, far, both = row_peers()
    send_both, send_near, near_both, near_own, send_far, far_own, base = work
    chunks = chunk_rows(base.shape[0])

    def keep(columns, value):
        base[:, columns] = value

    def to_both(columns, value):
        send_both[:, columns] = half(value)

    def to_near(columns, value):
        send_near[:, columns] = half(value)

    partial(both, to_both)
    first = remote(send_both, near_both, sems, 0, near)
    first.start()
    partial(far, keep)
    first.wait()
    across = []
    for i, rows in enumerate(chunks):
        send_far[rows, :] = half(base[rows, :] + near_both[rows, :].astype(jnp.float32))
        across.append(remote(send_far.at[rows], far_own.at[rows], sems, 2 + i, far))
        across[i].start()
    partial(near, to_near)
    second = remote(send_near, near_own, sems, 1, near)
    second.start()
    partial(mine, keep)
    second.wait()
    for i, rows in enumerate(chunks):
        across[i].wait()
        finish(
            rows,
            base[rows, :]
            + near_own[rows, :].astype(jnp.float32)
            + far_own[rows, :].astype(jnp.float32),
        )


def sum_scratch(rows, columns):
    narrow = pltpu.VMEM((rows, columns), jnp.bfloat16)
    return [narrow] * 6 + [pltpu.VMEM((rows, columns), jnp.float32)]


class Spread:
    def __init__(self, gathered, sems, base):
        self.gathered, self.sems, self.base = gathered, sems, base
        self.mine, self.near, self.far, self.both = row_peers()
        self.chunks = chunk_rows(gathered.shape[1])
        self.started = []

    def copy(self, block, i, kind, other):
        part = self.gathered.at[block, self.chunks[i]]
        return remote(part, part, self.sems, self.base + CHUNKS * kind + i, other)

    def offer(self, i, value):
        self.gathered[self.mine, self.chunks[i], :] = value
        for kind, other in ((0, self.far), (1, self.near)):
            copy = self.copy(self.mine, i, kind, other)
            copy.start()
            self.started.append(copy)

    def settle(self):
        for i in range(CHUNKS):
            self.copy(self.far, i, 0, self.far).wait_recv()
            forward = self.copy(self.far, i, 2, self.near)
            forward.start()
            self.started.append(forward)
        for i in range(CHUNKS):
            self.copy(self.near, i, 1, self.near).wait_recv()
            self.copy(self.both, i, 2, self.near).wait_recv()
        for copy in self.started:
            copy.wait_send()


def tiles_of(total, size):
    def run(step):
        def body(index, carry):
            step(pl.ds(pl.multiple_of(index * size, size), size))
            return carry

        lax.fori_loop(0, total // size, body, 0)

    return run


def enter_kernel(latents, scale, gain, gathered, sems):
    share = Spread(gathered, sems, 0)
    for i, rows in enumerate(share.chunks):
        share.offer(i, enter_point(latents[rows, :].astype(jnp.float32), scale[rows, :], gain[0:1]))
    share.settle()


def project_kernel(weight, captions, total, *rest):
    work, sems = rest[:-1], rest[-1]
    local = total.shape[0]

    def partial(block, store):
        rows = pl.ds(pl.multiple_of(block * local, local), local)

        @tiles_of(captions.shape[0], 512)
        def _(columns):
            store(columns, dot(weight[rows, :], captions[columns, :], 1, 1))

    def finish(rows, value):
        total[rows, :] = value

    sum_blocks(partial, finish, work, sems)


def attention_out_kernel(
    mixed, weight, latents, gate, scale, gain, summed, middle, gathered, *rest
):
    lhs, work, sems = rest[0], rest[1:-1], rest[-1]
    size = latents.shape[0]

    def partial(block, store):
        own = pl.ds(pl.multiple_of(block * size, size), size)
        lhs[...] = mixed[:, own].astype(jnp.float32).T.astype(jnp.bfloat16)

        @tiles_of(weight.shape[0], 512)
        def _(columns):
            store(columns, dot(lhs[...], weight[columns, :], 1, 1))

    share = Spread(gathered, sems, 2 + CHUNKS)

    def finish(rows, value):
        summed[rows, :] = value
        middle[rows, :], out = middle_point(
            value,
            latents[rows, :].astype(jnp.float32),
            gate[rows, :],
            scale[rows, :],
            gain[1:2],
            gain[2:3],
        )
        share.offer(share.chunks.index(rows), out)

    sum_blocks(partial, finish, work, sems)
    share.settle()


def feed_kernel(
    inputs, feed, down, middle, gate, cotangent, gain, gate_up, hidden, summed, out, gathered, *rest
):
    work, sems = rest[:-1], rest[-1]
    size = middle.shape[0]
    units = hidden.shape[1]

    def partial(block, store):
        own = pl.ds(pl.multiple_of(block * size, size), size)

        @tiles_of(units, 256)
        def _(columns):
            start = pl.multiple_of(columns.start + units, 256)
            first = dot(inputs[own, :], feed[:, columns], 1, 0)
            second = dot(inputs[own, :], feed[:, pl.ds(start, 256)], 1, 0)
            gate_up[own, columns] = first
            gate_up[own, pl.ds(start, 256)] = second
            hidden[own, columns] = half(first * jax.nn.sigmoid(first) * second)

        @tiles_of(down.shape[0], 512)
        def _(columns):
            store(columns, dot(hidden[own, :], down[columns, :], 1, 1))

    share = Spread(gathered, sems, 2 + CHUNKS)

    def finish(rows, value):
        summed[rows, :] = value
        out[rows, :], back = end_point(
            value, middle[rows, :], gate[rows, :], cotangent[rows, :], gain[3:4]
        )
        share.offer(share.chunks.index(rows), back)

    sum_blocks(partial, finish, work, sems)
    share.settle()


def feed_back_kernel(
    back, gate_up, feed, down, summed, middle, gate, scale, cotangent, gain,
    pair, input_grad, middle_grad, gathered, *rest
):
    work, sems = rest[:-1], rest[-1]
    size = middle.shape[0]
    units = down.shape[1]

    def partial(block, store):
        own = pl.ds(pl.multiple_of(block * size, size), size)

        @tiles_of(units, 256)
        def _(columns):
            other = pl.ds(pl.multiple_of(columns.start + units, 256), 256)
            grad = dot(back[own, :], down[:, columns], 1, 0)
            first, second = gate_up[own, columns], gate_up[own, other]
            pair[own, columns], pair[own, other] = pair_point(grad, first, second)

        @tiles_of(feed.shape[0], 256)
        def _(columns):
            store(columns, dot(pair[own, :], feed[columns, :], 1, 1))

    share = Spread(gathered, sems, 2 + CHUNKS)

    def finish(rows, value):
        input_grad[rows, :] = value
        middle_grad[rows, :], out = middle_back_point(
            value,
            summed[rows, :],
            middle[rows, :],
            gate[rows, :],
            scale[rows, :],
            cotangent[rows, :],
            gain[1:2],
            gain[2:3],
        )
        share.offer(share.chunks.index(rows), out)

    sum_blocks(partial, finish, work, sems)
    share.settle()


def text_kernel(own, captions, grad, gathered, *rest):
    (sems,) = rest
    mine, near, far, both = row_peers()
    share = Spread(gathered, sems, 0)
    local = own.shape[0]
    size = local // CHUNKS

    def work(block, i):
        rows = pl.ds(pl.multiple_of(block * local + i * size, 16), size)
        grad[rows, :] = half(dot(gathered[block, share.chunks[i], :], captions[...], 1, 0))

    for i, rows in enumerate(share.chunks):
        share.offer(i, own[rows, :])
    for i in range(CHUNKS):
        work(mine, i)
    for i in range(CHUNKS):
        share.copy(near, i, 1, near).wait_recv()
        work(near, i)
    for i in range(CHUNKS):
        share.copy(far, i, 0, far).wait_recv()
        forward = share.copy(far, i, 2, near)
        forward.start()
        share.started.append(forward)
        work(far, i)
        if i:
            share.copy(both, i - 1, 2, near).wait_recv()
            work(both, i - 1)
    share.copy(both, CHUNKS - 1, 2, near).wait_recv()
    work(both, CHUNKS - 1)
    for copy in share.started:
        copy.wait_send()


def enter_back_kernel(triple, weight, total, *rest):
    lhs, work, sems = rest[0], rest[1:-1], rest[-1]
    size = total.shape[0]

    def partial(block, store):
        own = pl.ds(pl.multiple_of(block * size, size), size)
        lhs[...] = triple[:, own].astype(jnp.float32).T.astype(jnp.bfloat16)

        @tiles_of(weight.shape[0], 512)
        def _(columns):
            store(columns, dot(lhs[...], weight[columns, :], 1, 1))

    def finish(rows, value):
        total[rows, :] = value

    sum_blocks(partial, finish, work, sems)


def enter_point(source, scale, gain):
    normed, _ = rms_parts(source)
    return half(normed * gain * (1.0 + scale))


def middle_point(summed, source, gate, scale, first_gain, second_gain):
    normed, _ = rms_parts(summed)
    middle = source + jnp.tanh(gate) * (normed * first_gain)
    return (middle, enter_point(middle, scale, second_gain))


def end_point(summed, middle, gate, cotangent, gain):
    normed, inverse = rms_parts(summed)
    turned = jnp.tanh(gate)
    out = middle + turned * (normed * gain)
    return (out, half(rms_back(normed, inverse, turned * cotangent * gain)))


def pair_point(grad, first, second):
    sigmoid = jax.nn.sigmoid(first)
    return (
        half(grad * second * (sigmoid + first * sigmoid * (1.0 - sigmoid))),
        half(grad * (first * sigmoid)),
    )


def middle_back_point(
    input_grad, summed, middle, gate, scale, cotangent, first_gain, second_gain
):
    normed, inverse = rms_parts(middle)
    middle_grad = cotangent + rms_back(
        normed, inverse, input_grad * second_gain * (1.0 + scale)
    )
    normed, inverse = rms_parts(summed)
    back = jnp.tanh(gate) * middle_grad * first_gain
    return (middle_grad, half(rms_back(normed, inverse, back)))


def spans(heads):
    return [slice(head * HEAD, (head + 1) * HEAD) for head in range(heads)]


def head_norm(value):
    inverse = lax.rsqrt(jnp.mean(value * value, axis=0, keepdims=True) + EPS)
    return (value * inverse, inverse)


def head_back(normed, inverse, grad):
    return inverse * (grad - normed * jnp.mean(grad * normed, axis=0, keepdims=True))


def turn(value, cosine, sine):
    middle = HEAD // 2
    first, second = value[:middle], value[middle:]
    return jnp.concatenate(
        [first * cosine - second * sine, second * cosine + first * sine], axis=0
    )


def score_block(keys, query, bias):
    return jnp.exp2(dot(keys, query, 1, 0) * (HEAD ** (-0.5) * LOG2E) + bias)


def self_bias(step, ids_row, ids_column):
    start = pl.multiple_of(step * TILE, TILE)
    return jnp.where(ids_column[pl.ds(start, TILE), :] == ids_row[...], 0.0, NEG)


def cross_bias(step, ids_row, lengths):
    slots = lax.broadcasted_iota(jnp.int32, (TILE, 1), 0) < lengths[step]
    return jnp.where(slots & (ids_row[...] == step), 0.0, NEG)


def attend_tile(heads, meta, bias_of, query, key_rows, value, out, total, inv_ref):
    base = 2 * pl.program_id(0)
    out[...] = jnp.zeros_like(out)
    total[...] = jnp.zeros_like(total)

    def step(index, carry):
        bias = bias_of(index)
        rows = pl.ds(pl.multiple_of(index * TILE, TILE), TILE)
        for head, span in enumerate(spans(heads)):
            expo = score_block(key_rows[head, rows, :], query[span, :], bias)
            total[head] += jnp.sum(expo.reshape(TILE // 8, 8, TILE), axis=0)
            out[span, :] += dot(value[span, rows], half(expo), 1, 0)
        return carry

    lax.fori_loop(meta[base], meta[base + 1], step, 0)
    for head, span in enumerate(spans(heads)):
        inverse = 1.0 / jnp.sum(total[head], axis=0, keepdims=True)
        inv_ref[head] = jnp.broadcast_to(inverse, (8, TILE))
        out[span, :] = out[span, :] * inverse


def attend_back_tile(
    heads, meta, bias_of, query, key_rows, key, value_rows, inv_ref, out, back, dq, dk, dv, centre
):
    base = 2 * pl.program_id(0)
    scale = HEAD ** (-0.5)
    dq[...] = jnp.zeros_like(dq)
    for head, span in enumerate(spans(heads)):
        both = out[span, :] * back[span, :].astype(jnp.float32)
        centre[head] = jnp.broadcast_to(jnp.sum(both, axis=0, keepdims=True), (8, TILE))

    def step(index, carry):
        bias = bias_of(index)
        rows = pl.ds(pl.multiple_of(index * TILE, TILE), TILE)
        for head, span in enumerate(spans(heads)):
            probs = score_block(key_rows[head, rows, :], query[span, :], bias)
            probs = probs * inv_ref[head, 0:1, :]
            prob_grad = dot(value_rows[head, rows, :], back[span, :], 1, 0)
            score_grad = half(probs * (prob_grad - centre[head, 0:1, :]))
            dv[span, rows] += dot(back[span, :], half(probs), 1, 1)
            dk[span, rows] += dot(query[span, :], score_grad, 1, 1) * scale
            dq[span, :] += dot(key[span, rows], score_grad, 1, 0) * scale
        return carry

    lax.fori_loop(meta[base], meta[base + 1], step, 0)


def self_forward_kernel(
    heads,
    meta,
    ids_row,
    ids_column,
    gain,
    cosine,
    sine,
    cosine_all,
    sine_all,
    raw_query,
    raw_rest,
    query,
    key,
    key_rows,
    value_rows,
    out,
    inv_ref,
    value,
    total,
):
    local = heads * HEAD

    @pl.when(pl.program_id(0) == 0)
    def _():
        for head, span in enumerate(spans(heads)):
            normed, _ = head_norm(raw_rest[span, :])
            turned = turn(normed * gain[span, 1:2], cosine_all[...], sine_all[...])
            key[span, :] = half(turned)
            key_rows[head] = half(turned.T)
            plain = raw_rest[local + head * HEAD : local + (head + 1) * HEAD, :]
            value[span, :] = half(plain)
            value_rows[head] = half(plain.T)

    for span in spans(heads):
        normed, _ = head_norm(raw_query[span, :])
        query[span, :] = half(turn(normed * gain[span, 0:1], cosine[...], sine[...]))
    attend_tile(
        heads,
        meta,
        lambda index: self_bias(index, ids_row, ids_column),
        query,
        key_rows,
        value,
        out,
        total,
        inv_ref,
    )


def cross_forward_kernel(
    heads,
    meta,
    lengths,
    ids_row,
    gain,
    query,
    own_out,
    raw_key,
    raw_value,
    key,
    key_rows,
    value_rows,
    out,
    inv_ref,
    mixed,
    value,
    total,
):
    @pl.when(pl.program_id(0) == 0)
    def _():
        for head, span in enumerate(spans(heads)):
            normed, _ = head_norm(raw_key[span, :])
            normed = normed * gain[span, 2:3]
            key[span, :] = half(normed)
            key_rows[head] = half(normed.T)
            plain = raw_value[span, :]
            value[span, :] = half(plain)
            value_rows[head] = half(plain.T)

    attend_tile(
        heads,
        meta,
        lambda index: cross_bias(index, ids_row, lengths),
        query,
        key_rows,
        value,
        out,
        total,
        inv_ref,
    )
    mixed[...] = half(own_out[...] + jnp.tanh(gain[:, 3:4]) * out[...])


def cross_backward_kernel(
    heads,
    meta,
    lengths,
    ids_row,
    gain,
    query,
    key_rows,
    key,
    value_rows,
    inv_ref,
    out,
    mixed_grad,
    raw_key,
    dq,
    dk,
    dv,
    gain_grad,
    back,
    centre,
    dk_sum,
    dv_sum,
    gate_sum,
):
    place = pl.program_id(0)

    @pl.when(place == 0)
    def _():
        dk_sum[...] = jnp.zeros_like(dk_sum)
        dv_sum[...] = jnp.zeros_like(dv_sum)
        gate_sum[...] = jnp.zeros_like(gate_sum)

    gate = jnp.tanh(gain[:, 3:4])
    back[...] = half(gate * mixed_grad[...])
    gate_sum[...] += mixed_grad[...] * out[...]
    attend_back_tile(
        heads,
        meta,
        lambda index: cross_bias(index, ids_row, lengths),
        query,
        key_rows,
        key,
        value_rows,
        inv_ref,
        out,
        back,
        dq,
        dk_sum,
        dv_sum,
        centre,
    )

    @pl.when(place == pl.num_programs(0) - 1)
    def _():
        dv[...] = half(dv_sum[...])
        gate_grad = jnp.sum(gate_sum[...], axis=1, keepdims=True) * (1.0 - gate * gate)
        gain_grad[:, 0:128] = jnp.broadcast_to(gate_grad, (heads * HEAD, 128))
        for span in spans(heads):
            normed, inverse = head_norm(raw_key[span, :])
            grad = dk_sum[span, :]
            summed = jnp.sum(grad * normed, axis=1, keepdims=True)
            gain_grad[span, 128:256] = jnp.broadcast_to(summed, (HEAD, 128))
            dk[span, :] = half(head_back(normed, inverse, grad * gain[span, 2:3]))


def self_backward_kernel(
    heads,
    meta,
    ids_row,
    ids_column,
    gain,
    cosine,
    sine,
    cosine_all,
    sine_all,
    query,
    key_rows,
    key,
    value_rows,
    inv_ref,
    out,
    mixed_grad,
    other_dq,
    raw_query,
    raw_key,
    triple,
    gain_grad,
    back,
    centre,
    dq,
    dk_sum,
    dv_sum,
    query_sum,
):
    place = pl.program_id(0)
    local = heads * HEAD

    @pl.when(place == 0)
    def _():
        dk_sum[...] = jnp.zeros_like(dk_sum)
        dv_sum[...] = jnp.zeros_like(dv_sum)
        query_sum[...] = jnp.zeros_like(query_sum)

    back[...] = half(mixed_grad[...])
    attend_back_tile(
        heads,
        meta,
        lambda index: self_bias(index, ids_row, ids_column),
        query,
        key_rows,
        key,
        value_rows,
        inv_ref,
        out,
        back,
        dq,
        dk_sum,
        dv_sum,
        centre,
    )
    columns = pl.ds(pl.multiple_of(place * TILE, TILE), TILE)
    for span in spans(heads):
        normed, inverse = head_norm(raw_query[span, :])
        grad = turn(dq[span, :] + other_dq[span, :], cosine[...], -sine[...])
        query_sum[span, :] += grad * normed
        triple[span, columns] = half(head_back(normed, inverse, grad * gain[span, 0:1]))

    @pl.when(place == pl.num_programs(0) - 1)
    def _():
        summed = jnp.sum(query_sum[...], axis=1, keepdims=True)
        gain_grad[:, 0:128] = jnp.broadcast_to(summed, (local, 128))
        triple[2 * local :, :] = half(dv_sum[...])
        for head, span in enumerate(spans(heads)):
            normed, inverse = head_norm(raw_key[span, :])
            grad = turn(dk_sum[span, :], cosine_all[...], -sine_all[...])
            summed = jnp.sum(grad * normed, axis=1, keepdims=True)
            gain_grad[span, 128:256] = jnp.broadcast_to(summed, (HEAD, 128))
            triple[local + head * HEAD : local + (head + 1) * HEAD, :] = half(
                head_back(normed, inverse, grad * gain[span, 1:2])
            )


def attention_call(kernel, name, scalars, operands, outs, scratch, tokens, weight, after=()):
    def block(array, tiled):
        lead = array.shape[:-1]
        if tiled:
            return pl.BlockSpec((*lead, TILE), lambda i, *_: (*([0] * len(lead)), i))
        return pl.BlockSpec(array.shape, lambda i, *_: (0,) * len(array.shape))

    count = len(scalars) + len(operands)

    def run(*refs):
        kernel(*refs[:count], *refs[count + len(after) :])

    return pl.pallas_call(
        run,
        grid_spec=pltpu.PrefetchScalarGridSpec(
            num_scalar_prefetch=len(scalars),
            grid=(tokens // TILE,),
            in_specs=[block(*operand) for operand in operands]
            + [pl.BlockSpec(memory_space=pl.ANY)] * len(after),
            out_specs=[block(*out) for out in outs],
            scratch_shapes=scratch,
        ),
        out_shape=[out for out, _ in outs],
        compiler_params=pltpu.CompilerParams(
            vmem_limit_bytes=58 * 1024 * 1024, dimension_semantics=("arbitrary",)
        ),
        cost_estimate=pl.CostEstimate(
            flops=weight, bytes_accessed=weight, transcendentals=0
        ),
        name=name,
    )(*scalars, *(operand for operand, _ in operands), *after)


def adamw(grad, weight, moment, square, decay, rate):
    moment_new = BETA1 * moment + (1.0 - BETA1) * grad
    square_new = BETA2 * square + (1.0 - BETA2) * grad * grad
    step_size = (
        moment_new / (1.0 - BETA1**STEP) / (jnp.sqrt(square_new / (1.0 - BETA2**STEP)) + ADAM_EPS)
    )
    return (moment_new, square_new, weight - rate * (step_size + decay * weight))


def body(
    latents,
    cotangent,
    captions,
    conditions,
    image_ids,
    rope_rows,
    rope_cols,
    caption_lengths,
    attention_in,
    attention_out,
    feed_in,
    feed_out,
    caption_in,
    modulator,
    channels,
    moment_attention_in,
    square_attention_in,
    moment_attention_out,
    square_attention_out,
    moment_feed_in,
    square_feed_in,
    moment_feed_out,
    square_feed_out,
    moment_caption_in,
    square_caption_in,
    moment_modulator,
    square_modulator,
    moment_channels,
    square_channels,
):
    tensor_size = lax.axis_size("tensor")
    tensor_index = lax.axis_index("tensor")
    dp_size = lax.axis_size("dp")
    dp_index = lax.axis_index("dp")
    shard_rows, width = latents.shape
    local = attention_in.shape[2]
    heads = local // HEAD
    units = feed_in.shape[2]
    segment = image_ids[0]
    row_tokens = segment.shape[0]
    images = conditions.shape[0]
    per_row = caption_lengths.shape[1]
    lengths = caption_lengths[0]
    slots = captions.shape[0]
    offset = tensor_index * local
    own_ids = lax.dynamic_slice_in_dim(segment, tensor_index * shard_rows, shard_rows)

    rows = attention_in.shape[1]
    fused = tensor_size == 4
    caption_half = half(caption_in)
    key_line = gather_far(caption_half[0].T)
    value_line = gather_far(caption_half[1].T)
    in_half = half(attention_in)
    attention_line = gather_far(
        jnp.concatenate([in_half[0], in_half[1], in_half[2], half(attention_out).T], axis=1)
    )
    down_line = gather_far(half(feed_out).T)
    feed_half = half(feed_in)
    feed_own = jnp.concatenate([feed_half[0], feed_half[1]], axis=1)

    augmented = half(
        jnp.concatenate([jax.nn.silu(conditions), jnp.ones((images, 1), jnp.float32)], axis=1)
    )
    factor_part = jnp.dot(augmented, half(modulator), preferred_element_type=jnp.float32)
    own_columns = factor_part.shape[1]
    payload = jnp.concatenate(
        [
            factor_part.reshape(dp_size, per_row, own_columns),
            jnp.broadcast_to(
                lax.reduce_precision(channels, 8, 7).reshape(-1, own_columns),
                (dp_size, channels.size // own_columns, own_columns),
            ),
        ],
        axis=1,
    )
    received, feed_other = remote_call(
        spread_kernel,
        "modulation_exchange",
        0,
        [payload],
        [jax.ShapeDtypeStruct((tensor_size, *payload.shape), jnp.float32)],
        exchange_scratch([payload.shape]),
        [feed_own],
        everyone=True,
    )
    feed_full = gather_far(near_pair(feed_own, feed_other))
    factor_row = jnp.transpose(received[:, :, :per_row], (2, 1, 0, 3)).reshape(per_row, -1)
    gains = received[0, :, per_row:].reshape(dp_size, 8, -1)
    gains = jnp.transpose(gains, (1, 0, 2)).reshape(8, width)
    local_gains = lax.dynamic_slice_in_dim(gains[4:], offset, local, 1).T
    chooser = (own_ids[:, None] == jnp.arange(per_row, dtype=jnp.int32)[None, :]).astype(
        jnp.float32
    )
    token_factor = jnp.dot(chooser, factor_row, precision=HIGH)
    scale_attn = token_factor[:, :width]
    gate_attn = token_factor[:, width : 2 * width]
    scale_feed = token_factor[:, 2 * width : 3 * width]
    gate_feed = token_factor[:, 3 * width :]

    def split(value):
        return [value[i * shard_rows : (i + 1) * shard_rows] for i in range(tensor_size)]

    f32, bf16 = jnp.float32, jnp.bfloat16

    def shape(dims, dtype=f32):
        return jax.ShapeDtypeStruct(dims, dtype)

    gathered = shape((tensor_size, shard_rows, width), bf16)
    in_kernel = sum_scratch(shard_rows, width)

    def semaphores(count):
        return pltpu.SemaphoreType.DMA((2, count))

    sum_sems, all_sems = semaphores(2 + CHUNKS), semaphores(2 + 4 * CHUNKS)
    source = latents.astype(f32)
    attn_norm, attn_inv = rms_parts(source)

    def caption_project(weight, carry, number):
        if fused:
            return remote_call(
                project_kernel,
                "project",
                number,
                [weight, captions],
                [shape((local, slots))],
                [*sum_scratch(local, slots), sum_sems],
                [carry],
            )
        total = collect(
            [
                dot(
                    lax.dynamic_slice_in_dim(weight, owner(i) * local, local), captions, 1, 1
                )
                for i in range(tensor_size)
            ]
        )
        return (total, near_swap(carry))

    if fused:
        attn_full, key_other = remote_call(
            enter_kernel,
            "enter",
            3,
            [latents, scale_attn, gains],
            [gathered],
            [semaphores(3 * CHUNKS)],
            [key_line],
        )
        attn_full = attn_full.reshape(row_tokens, width)
    else:
        attn_full = in_place(spread(enter_point(source, scale_attn, gains[0])))
        key_other = near_swap(key_line)
    text_key_raw, value_other = caption_project(
        join_near(key_line, key_other, rows), value_line, 4
    )
    text_value_raw, attention_other = caption_project(
        join_near(value_line, value_other, rows), attention_line, 11
    )
    in_full = join_near(attention_line, attention_other, rows, 0, 3 * local)
    out_full = join_near(attention_line, attention_other, rows, 3 * local)
    projected = dot(in_full, attn_full, 0, 1)
    raw_query, raw_rest = projected[:local], projected[local:]
    cosine, sine = rope_tables(rope_rows[0], rope_cols[0])

    tiles = row_tokens // TILE
    first_id = segment.reshape(tiles, TILE)[:, 0]
    last_id = segment.reshape(tiles, TILE)[:, TILE - 1]
    low = jnp.sum((segment[None] < first_id[:, None]).astype(jnp.int32), axis=1) // TILE
    high = (
        jnp.sum((segment[None] <= last_id[:, None]).astype(jnp.int32), axis=1) + TILE - 1
    ) // TILE
    self_meta = jnp.stack([low, high], axis=1).reshape(-1)
    cross_meta = jnp.stack([first_id, last_id + 1], axis=1).reshape(-1)
    ids_row = image_ids
    ids_column = segment[:, None]
    wide = jax.ShapeDtypeStruct((local, row_tokens), jnp.float32)
    narrow = jax.ShapeDtypeStruct((local, row_tokens), jnp.bfloat16)
    sums = jax.ShapeDtypeStruct((heads, 8, row_tokens), jnp.float32)
    by_rows = jax.ShapeDtypeStruct((heads, row_tokens, HEAD), jnp.bfloat16)
    text_narrow = jax.ShapeDtypeStruct((local, slots), jnp.bfloat16)
    text_rows = jax.ShapeDtypeStruct((heads, slots, HEAD), jnp.bfloat16)
    gain_shape = jax.ShapeDtypeStruct((local, 256), jnp.float32)
    tile_sums = pltpu.VMEM((heads, 8, TILE), jnp.float32)
    tables = [(cosine, True), (sine, True), (cosine, False), (sine, False)]
    queries, keys, key_rows, value_rows, own_out, own_inv = attention_call(
        functools.partial(self_forward_kernel, heads),
        "self_forward",
        [self_meta],
        [
            (ids_row, True),
            (ids_column, False),
            (local_gains, False),
            *tables,
            (raw_query, True),
            (raw_rest, False),
        ],
        [
            (narrow, True),
            (narrow, False),
            (by_rows, False),
            (by_rows, False),
            (wide, True),
            (sums, True),
        ],
        [pltpu.VMEM((local, row_tokens), jnp.bfloat16), tile_sums],
        row_tokens,
        15000,
    )
    text_keys, text_key_rows, text_value_rows, other_out, other_inv, mixed = attention_call(
        functools.partial(cross_forward_kernel, heads),
        "cross_forward",
        [cross_meta, lengths],
        [
            (ids_row, True),
            (local_gains, False),
            (queries, True),
            (own_out, True),
            (text_key_raw, False),
            (text_value_raw, False),
        ],
        [
            (text_narrow, False),
            (text_rows, False),
            (text_rows, False),
            (wide, True),
            (sums, True),
            (narrow, True),
        ],
        [pltpu.VMEM((local, slots), jnp.bfloat16), tile_sums],
        row_tokens,
        18000,
    )
    norm_gains = gains
    if fused:
        attn_sum, middle, feed_all, down_other = remote_call(
            attention_out_kernel,
            "attention_out",
            5,
            [mixed, out_full, latents, gate_attn, scale_feed, norm_gains],
            [shape((shard_rows, width)), shape((shard_rows, width)), gathered],
            [pltpu.VMEM((shard_rows, local), bf16), *in_kernel, all_sems],
            [down_line],
        )
        feed_all = feed_all.reshape(row_tokens, width)
        down_full = join_near(down_line, down_other, rows)
        gate_up, hidden, feed_sum, block_out, feed_sum_grad = remote_call(
            feed_kernel,
            "feed_forward",
            6,
            [feed_all, feed_full, down_full, middle, gate_feed, cotangent, norm_gains],
            [
                shape((row_tokens, 2 * units)),
                shape((row_tokens, units), bf16),
                shape((shard_rows, width)),
                shape((shard_rows, width)),
                gathered,
            ],
            [*in_kernel, all_sems],
        )
        feed_sum_grad = feed_sum_grad.reshape(row_tokens, width)
    else:
        attn_sum = collect(
            [
                dot(
                    lax.dynamic_slice_in_dim(mixed, owner(i) * shard_rows, shard_rows, 1),
                    out_full,
                    0,
                    1,
                )
                for i in range(tensor_size)
            ]
        )
        middle, feed_block = middle_point(
            attn_sum, source, gate_attn, scale_feed, gains[1], gains[2]
        )
        feed_all = in_place(spread(feed_block))
        down_full = join_near(down_line, near_swap(down_line), rows)
        gate_up = dot(feed_all, feed_full, 1, 0)
        hidden = half(jax.nn.silu(gate_up[:, :units]) * gate_up[:, units:])
        feed_sum = collect(split(dot(hidden, down_full, 1, 1)))
        block_out, feed_block_grad = end_point(
            feed_sum, middle, gate_feed, cotangent, gains[3]
        )
        feed_sum_grad = in_place(spread(feed_block_grad))
    feed_out_grad = half(dot(feed_sum_grad, hidden, 0, 0))
    feed_out_parts = feed_out_grad.reshape(dp_size // 2, 2, -1, units)
    if fused:
        pair_grad, feed_input_grad, middle_grad, attn_sum_grad, feed_out_other = remote_call(
            feed_back_kernel,
            "feed_backward",
            7,
            [
                feed_sum_grad,
                gate_up,
                feed_full,
                down_full,
                attn_sum,
                middle,
                gate_attn,
                scale_feed,
                cotangent,
                norm_gains,
            ],
            [
                shape((row_tokens, 2 * units), bf16),
                shape((shard_rows, width)),
                shape((shard_rows, width)),
                gathered,
            ],
            [*in_kernel, all_sems],
            [feed_out_parts],
        )
        attn_sum_grad = attn_sum_grad.reshape(row_tokens, width)
    else:
        hidden_grad = dot(feed_sum_grad, down_full, 1, 0)
        pair_grad = jnp.concatenate(
            pair_point(hidden_grad, gate_up[:, :units], gate_up[:, units:]), axis=1
        )
        feed_input_grad = collect(split(dot(pair_grad, feed_full, 1, 1)))
        middle_grad, attn_block_grad = middle_back_point(
            feed_input_grad,
            attn_sum,
            middle,
            gate_attn,
            scale_feed,
            cotangent,
            gains[1],
            gains[2],
        )
        attn_sum_grad = in_place(spread(attn_block_grad))
        feed_out_other = swap_half(feed_out_parts)
    feed_out_sum = scatter_far((feed_out_parts,), (feed_out_other,))
    feed_in_grad = half(dot(feed_all, pair_grad, 0, 0))
    feed_in_both = lax.psum_scatter(
        feed_in_grad, "dp", scatter_dimension=0, tiled=True, axis_index_groups=far_groups()
    )
    mixed_grad = dot(out_full, gate(attn_sum_grad, feed_in_grad), 0, 1)
    out_parts = half(dot(attn_sum_grad, mixed, 0, 1)).reshape(dp_size // 2, 2, -1, local)
    query_two, text_key_grad, text_value_grad, text_gains = attention_call(
        functools.partial(cross_backward_kernel, heads),
        "cross_backward",
        [cross_meta, lengths],
        [
            (ids_row, True),
            (local_gains, False),
            (queries, True),
            (text_key_rows, False),
            (text_keys, False),
            (text_value_rows, False),
            (other_inv, True),
            (other_out, True),
            (mixed_grad, True),
            (text_key_raw, False),
        ],
        [(wide, True), (text_narrow, False), (text_narrow, False), (gain_shape, False)],
        [
            pltpu.VMEM((local, TILE), jnp.bfloat16),
            tile_sums,
            pltpu.VMEM((local, slots), jnp.float32),
            pltpu.VMEM((local, slots), jnp.float32),
            pltpu.VMEM((local, TILE), jnp.float32),
        ],
        row_tokens,
        25000,
    )
    triple_grad, own_gains = attention_call(
        functools.partial(self_backward_kernel, heads),
        "self_backward",
        [self_meta],
        [
            (ids_row, True),
            (ids_column, False),
            (local_gains, False),
            *tables,
            (queries, True),
            (key_rows, False),
            (keys, False),
            (value_rows, False),
            (own_inv, True),
            (own_out, True),
            (mixed_grad, True),
            (query_two, True),
            (raw_query, True),
            (raw_rest[:local], False),
        ],
        [
            (jax.ShapeDtypeStruct((3 * local, row_tokens), jnp.bfloat16), False),
            (gain_shape, False),
        ],
        [
            pltpu.VMEM((local, TILE), jnp.bfloat16),
            tile_sums,
            pltpu.VMEM((local, TILE), jnp.float32),
            pltpu.VMEM((local, row_tokens), jnp.float32),
            pltpu.VMEM((local, row_tokens), jnp.float32),
            pltpu.VMEM((local, TILE), jnp.float32),
        ],
        row_tokens,
        25000,
        [feed_out_sum],
    )
    in_parts = half(dot(attn_full, triple_grad, 0, 1)).reshape(dp_size // 2, 2, -1, 3 * local)

    def caption_back(grad, carry, after=()):
        if fused:
            grad, _, *others = remote_call(
                text_kernel,
                f"text_gradient_{len(carry)}",
                7 + len(carry),
                [grad, captions],
                [
                    shape((tensor_size * local, captions.shape[1]), bf16),
                    shape((tensor_size, local, slots), bf16),
                ],
                [semaphores(3 * CHUNKS)],
                carry,
                after=after,
            )
        else:
            grad = half(dot(in_place(spread(grad)), captions, 1, 0))
            others = [swap_half(parts) for parts in carry]
        return (grad.reshape(dp_size // 2, 2, -1, captions.shape[1]), *others)

    value_parts, in_other, out_other = caption_back(text_value_grad, [in_parts, out_parts])
    attention_sum = scatter_far((in_parts, out_parts), (in_other, out_other))
    key_parts, value_other = caption_back(text_key_grad, [value_parts], [feed_in_both])
    value_sum = scatter_far((value_parts,), (value_other,))
    if fused:
        attn_input_grad, key_other = remote_call(
            enter_back_kernel,
            "enter_backward",
            10,
            [triple_grad, in_full],
            [shape((shard_rows, width))],
            [pltpu.VMEM((shard_rows, 3 * local), bf16), *in_kernel, sum_sems],
            [key_parts],
            after=[attention_sum],
        )
    else:
        attn_input_grad = collect(
            [
                dot(
                    lax.dynamic_slice_in_dim(triple_grad, owner(i) * shard_rows, shard_rows, 1),
                    in_full,
                    0,
                    1,
                )
                for i in range(tensor_size)
            ]
        )
        key_other = swap_half(key_parts)
    key_sum = scatter_far((key_parts,), (key_other,))
    in_sum, out_sum = attention_sum[:, : 3 * local], attention_sum[:, 3 * local :]
    first_norm, _ = rms_parts(attn_sum)
    feed_norm, _ = rms_parts(middle)
    second_norm, _ = rms_parts(feed_sum)
    tanh_attn, tanh_feed = jnp.tanh(gate_attn), jnp.tanh(gate_feed)
    branch_attn_grad, branch_feed_grad = tanh_attn * middle_grad, tanh_feed * cotangent
    gate_attn_grad = middle_grad * (first_norm * gains[1]) * (1.0 - tanh_attn * tanh_attn)
    gate_feed_grad = cotangent * (second_norm * gains[3]) * (1.0 - tanh_feed * tanh_feed)
    scale_feed_grad = feed_input_grad * feed_norm * gains[2]
    scale_attn_grad = attn_input_grad * attn_norm * gains[0]
    latent_grad = middle_grad + rms_back(
        attn_norm, attn_inv, attn_input_grad * gains[0] * (1.0 + scale_attn)
    )
    shared_rows = jnp.stack(
        [
            jnp.sum(attn_input_grad * attn_norm * (1.0 + scale_attn), axis=0),
            jnp.sum(branch_attn_grad * first_norm, axis=0),
            jnp.sum(feed_input_grad * feed_norm * (1.0 + scale_feed), axis=0),
            jnp.sum(branch_feed_grad * second_norm, axis=0),
        ]
    )
    head_rows = jnp.stack(
        [own_gains[:, 0], own_gains[:, 128], text_gains[:, 128], text_gains[:, 0]]
    )
    head_full = lax.dynamic_update_slice(
        jnp.zeros((4, width), jnp.float32), head_rows, (jnp.zeros((), jnp.int32), offset)
    )
    channel_part = jnp.concatenate([shared_rows, head_full], axis=0)
    factor_tokens = jnp.concatenate(
        [scale_attn_grad, gate_attn_grad, scale_feed_grad, gate_feed_grad], axis=1
    )
    factor_image = jnp.dot(chooser.T, factor_tokens, precision=HIGH)
    factor_image = jnp.transpose(
        factor_image.reshape(per_row, dp_size, tensor_size, own_columns), (2, 1, 0, 3)
    )
    channel_blocks = jnp.transpose(channel_part.reshape(8, dp_size, -1), (1, 0, 2))
    channel_blocks = channel_blocks.reshape(dp_size, -1, own_columns)
    payload = jnp.concatenate(
        [factor_image, jnp.broadcast_to(channel_blocks, (tensor_size, *channel_blocks.shape))],
        axis=2,
    )
    blocks = payload.shape[1:]
    feed_in_parts = feed_in_both.reshape(1, 2, -1, 2 * units)
    received, feed_in_other = remote_call(
        return_kernel,
        "modulation_return",
        1,
        [payload],
        [shape(blocks)],
        exchange_scratch([payload.shape, blocks, blocks]),
        [feed_in_parts],
        everyone=True,
        after=[value_sum],
    )
    feed_in_sum = lax.dynamic_index_in_dim(
        feed_in_parts, dp_index % 2, 1, keepdims=False
    ).astype(f32) + feed_in_other.astype(f32)
    feed_in_sum = feed_in_sum[0]
    factor_grad = received[:, :per_row].reshape(images, own_columns)
    channel_sum = jnp.sum(received[:, per_row:], axis=0).reshape(channels.shape)
    modulator_sum = jnp.dot(augmented.astype(jnp.float32).T, factor_grad, precision=HIGH)

    in_sum, out_sum, feed_in_sum, feed_out_sum, key_sum, value_sum = (
        value.astype(jnp.float32)
        for value in (in_sum, out_sum, feed_in_sum, feed_out_sum, key_sum, value_sum)
    )
    squares = (
        jnp.sum(in_sum * in_sum)
        + jnp.sum(out_sum * out_sum)
        + jnp.sum(feed_in_sum * feed_in_sum)
        + jnp.sum(feed_out_sum * feed_out_sum)
        + jnp.sum(key_sum * key_sum)
        + jnp.sum(value_sum * value_sum)
        + jnp.sum(modulator_sum * modulator_sum)
        + jnp.sum(channel_sum * channel_sum) / tensor_size
    )
    in_sum = jnp.stack([in_sum[:, i * local : (i + 1) * local] for i in range(3)])
    feed_in_sum = jnp.stack([feed_in_sum[:, i * units : (i + 1) * units] for i in range(2)])
    caption_sum = jnp.stack([key_sum.T, value_sum.T])
    (squares,) = remote_call(
        total_kernel,
        "norm_exchange",
        2,
        [jnp.broadcast_to(squares, (8, 128))],
        [shape((8, 128))],
        exchange_scratch([(tensor_size, 8, 128), (dp_size, 8, 128), (8, 128)]),
        everyone=True,
    )
    grad_norm = jnp.sqrt(squares[0, 0])
    factor = CLIP / jnp.maximum(grad_norm, CLIP)
    results = [
        adamw(grad * factor, weight, moment, square, DECAY, RATE)
        for grad, weight, moment, square in (
            (in_sum, attention_in, moment_attention_in, square_attention_in),
            (out_sum.T, attention_out, moment_attention_out, square_attention_out),
            (feed_in_sum, feed_in, moment_feed_in, square_feed_in),
            (feed_out_sum.T, feed_out, moment_feed_out, square_feed_out),
            (caption_sum, caption_in, moment_caption_in, square_caption_in),
            (modulator_sum, modulator, moment_modulator, square_modulator),
        )
    ]
    results.append(
        adamw(channel_sum * factor, channels, moment_channels, square_channels, 0.0, GAIN_RATE)
    )
    return (block_out, latent_grad, grad_norm, *(part for result in results for part in result))


def solution(mesh):
    return jax.shard_map(
        body,
        mesh=mesh,
        in_specs=(
            P(("dp", "tensor"), None),
            P(("dp", "tensor"), None),
            P("dp", "tensor"),
            P(),
            P("dp", None),
            P("dp", None),
            P("dp", None),
            P("dp", None),
            P(None, "dp", "tensor"),
            P("tensor", "dp"),
            P(None, "dp", "tensor"),
            P("tensor", "dp"),
            P(None, "tensor", "dp"),
            P(None, ("dp", "tensor")),
            P(None, "dp"),
            P(None, "dp", "tensor"),
            P(None, "dp", "tensor"),
            P("tensor", "dp"),
            P("tensor", "dp"),
            P(None, "dp", "tensor"),
            P(None, "dp", "tensor"),
            P("tensor", "dp"),
            P("tensor", "dp"),
            P(None, "tensor", "dp"),
            P(None, "tensor", "dp"),
            P(None, ("dp", "tensor")),
            P(None, ("dp", "tensor")),
            P(None, "dp"),
            P(None, "dp"),
        ),
        out_specs=(
            P(("dp", "tensor"), None),
            P(("dp", "tensor"), None),
            P(),
            P(None, "dp", "tensor"),
            P(None, "dp", "tensor"),
            P(None, "dp", "tensor"),
            P("tensor", "dp"),
            P("tensor", "dp"),
            P("tensor", "dp"),
            P(None, "dp", "tensor"),
            P(None, "dp", "tensor"),
            P(None, "dp", "tensor"),
            P("tensor", "dp"),
            P("tensor", "dp"),
            P("tensor", "dp"),
            P(None, "tensor", "dp"),
            P(None, "tensor", "dp"),
            P(None, "tensor", "dp"),
            P(None, ("dp", "tensor")),
            P(None, ("dp", "tensor")),
            P(None, ("dp", "tensor")),
            P(None, "dp"),
            P(None, "dp"),
            P(None, "dp"),
        ),
        check_vma=False,
    )
```

```python
import functools
import math

import jax
import jax.numpy as jnp
from jax import lax
from jax.experimental import pallas as pl
from jax.experimental.pallas import tpu as pltpu
from jax.sharding import PartitionSpec as P

HEAD = 64
CAP = 256
STEP = 10


EPS = 1e-06
NEG = -1e30
THETA = 10000.0
BETA1 = 0.9
BETA2 = 0.95
RATE = 0.05
GAIN_RATE = 0.8
DECAY = 0.1
ADAM_EPS = 1e-08
CLIP = 1.0
HIGH = lax.Precision.HIGHEST


def half(value):
    return value.astype(jnp.bfloat16)


TILE = 256
LOG2E = 1.0 / math.log(2.0)
MESH = pl.DeviceIdType.MESH


def dot(left, right, left_dim, right_dim):
    return lax.dot_general(
        left, right, (((left_dim,), (right_dim,)), ((), ())), preferred_element_type=jnp.float32
    )


def rms_parts(value, axis=-1):
    inverse = lax.rsqrt(jnp.mean(value * value, axis=axis, keepdims=True) + EPS)
    return (value * inverse, inverse)


def rms_back(normed, inverse, grad, axis=-1):
    return inverse * (grad - normed * jnp.mean(grad * normed, axis=axis, keepdims=True))


def rope_tables(rows, columns):
    quarter = HEAD // 4
    frequency = THETA ** (-jnp.arange(quarter, dtype=jnp.float32) / quarter)
    angles = jnp.concatenate(
        [
            frequency[:, None] * rows.astype(jnp.float32)[None, :],
            frequency[:, None] * columns.astype(jnp.float32)[None, :],
        ],
        axis=0,
    )
    return (jnp.cos(angles), jnp.sin(angles))


def gate_kernel(value, after, out):
    del value, after, out


def gate(value, after):
    anywhere = pl.BlockSpec(memory_space=pl.ANY)
    return pl.pallas_call(
        gate_kernel,
        out_shape=jax.ShapeDtypeStruct(value.shape, value.dtype),
        in_specs=[anywhere, anywhere],
        out_specs=anywhere,
        input_output_aliases={0: 0},
        name="gate",
    )(value, after)


def near_swap(value):
    return lax.ppermute(value, "dp", [(i, i ^ 1) for i in range(lax.axis_size("dp"))])


def far_groups():
    count = lax.axis_size("dp")
    return [list(range(near, count, 2)) for near in range(2)]


def gather_far(value):
    return lax.all_gather(value, "dp", axis=0, tiled=True, axis_index_groups=far_groups())


def flat(blocks):
    return blocks.reshape(-1, blocks.shape[-1])


def join_near(own, other, count):
    odd = lax.axis_index("dp") % 2
    own = own.reshape(-1, count, own.shape[1])
    other = other.reshape(own.shape)
    return flat(
        jnp.stack([jnp.where(odd == 0, own, other), jnp.where(odd == 0, other, own)], axis=1)
    )


def swap_half(parts):
    odd = lax.axis_index("dp") % 2
    send = lax.dynamic_index_in_dim(parts, 1 - odd, 1, keepdims=False)
    return near_swap(send.reshape(-1, send.shape[2])).reshape(send.shape)


def sum_half(parts, other):
    odd = lax.axis_index("dp") % 2
    keep = lax.dynamic_index_in_dim(parts, odd, 1, keepdims=False)
    return flat(half(keep.astype(jnp.float32) + other.astype(jnp.float32)))


def scatter_far(value):
    return lax.psum_scatter(
        value, "dp", scatter_dimension=0, tiled=True, axis_index_groups=far_groups()
    )


def swap_tensor(value, bits):
    return lax.ppermute(value, "tensor", [(i, i ^ bits) for i in range(lax.axis_size("tensor"))])


def owner(place):
    if lax.axis_size("tensor") == 4:
        return lax.axis_index("tensor") ^ place
    return jnp.int32(place)


def spread(value):
    count = lax.axis_size("tensor")
    if count == 4:
        near = swap_tensor(value, 1)
        far = swap_tensor(value, 2)
        return [value, near, far, swap_tensor(far, 1)]
    whole = lax.all_gather(value, "tensor", axis=0, tiled=False)
    return [whole[i] for i in range(count)]


def collect_near(parts):
    if len(parts) == 4:
        rows = parts[0].shape[0]
        sent = swap_tensor(half(jnp.concatenate([parts[3], parts[1]], axis=0)), 1)
        sent = sent.astype(jnp.float32)
        return (parts[0] + sent[rows:], half(parts[2] + sent[:rows]))
    return (half(jnp.concatenate(parts, axis=0)),)


def collect_far(sums):
    if len(sums) == 2:
        return sums[0] + swap_tensor(sums[1], 2).astype(jnp.float32)
    return lax.psum_scatter(
        sums[0], "tensor", scatter_dimension=0, tiled=True
    ).astype(jnp.float32)


def collect(parts):
    return collect_far(collect_near(parts))


def in_place(blocks):
    if len(blocks) == 4:
        stacked = jnp.stack(blocks)
        mine = lax.axis_index("tensor")
        blocks = [
            lax.dynamic_index_in_dim(stacked, mine ^ i, 0, keepdims=False)
            for i in range(len(blocks))
        ]
    return jnp.concatenate(blocks, axis=0)


def dp_neighbour():
    mine = lax.axis_index("dp")
    return mine + 1 - 2 * (mine % 2)


def meet(everyone, neighbour):
    barrier = pltpu.get_barrier_semaphore()
    if everyone:
        others = [
            {axis: (lax.axis_index(axis) + step) % lax.axis_size(axis)}
            for axis in ("dp", "tensor")
            for step in range(1, lax.axis_size(axis))
        ]
    else:
        _, near, far, _ = row_peers()
        others = [{"tensor": near}, {"tensor": far}]
        if neighbour:
            others.append({"dp": dp_neighbour()})
    for other in others:
        pl.semaphore_signal(barrier, inc=1, device_id=other, device_id_type=MESH)
    pl.semaphore_wait(barrier, len(others))


def remote_call(
    kernel, name, number, operands, outs, scratch, carry=(), everyone=False, neighbour=False, after=()
):
    copies = sum(array.shape[0] if len(array.shape) == 4 else 1 for array in carry)
    traded = [
        jax.ShapeDtypeStruct(
            (array.shape[0], *array.shape[2:]) if len(array.shape) == 4 else array.shape,
            array.dtype,
        )
        for array in carry
    ]

    def run(*refs):
        refs = list(refs)
        ins = [refs.pop(0) for _ in operands]
        sources = [refs.pop(0) for _ in carry]
        del refs[: len(after)]
        results = [refs.pop(0) for _ in outs]
        targets = [refs.pop(0) for _ in carry]
        meet(everyone, neighbour or bool(carry))
        started = []
        if carry:
            sems = refs.pop()
            other = dp_neighbour()
            pairs = []
            for source, target in zip(sources, targets):
                if len(source.shape) == 2:
                    pairs.append((source, target))
                else:
                    pairs += [
                        (source.at[i, other % 2], target.at[i]) for i in range(source.shape[0])
                    ]
            for i, (source, target) in enumerate(pairs):
                copy = pltpu.make_async_remote_copy(
                    src_ref=source,
                    dst_ref=target,
                    send_sem=sems.at[0, i],
                    recv_sem=sems.at[1, i],
                    device_id={"dp": other},
                    device_id_type=MESH,
                )
                copy.start()
                started.append(copy)
        kernel(*ins, *results, *refs)
        for copy in started:
            copy.wait()

    whole = pl.BlockSpec(memory_space=pltpu.VMEM)
    anywhere = pl.BlockSpec(memory_space=pl.ANY)
    return pl.pallas_call(
        run,
        out_shape=[*outs, *traded],
        in_specs=[whole] * len(operands) + [anywhere] * (len(carry) + len(after)),
        out_specs=[whole] * len(outs) + [anywhere] * len(carry),
        scratch_shapes=[
            *scratch,
            *([pltpu.SemaphoreType.DMA((2, copies))] if carry else []),
        ],
        compiler_params=pltpu.CompilerParams(
            collective_id=number, has_side_effects=True, vmem_limit_bytes=60 * 1024 * 1024
        ),
        cost_estimate=pl.CostEstimate(flops=1 << 20, bytes_accessed=1 << 20, transcendentals=0),
        name=name,
    )(*operands, *carry, *after)


def send_blocks(axis, pick, target, send_sem, recv_sem):
    count = lax.axis_size(axis)
    mine = lax.axis_index(axis)

    def copy(other, place):
        return pltpu.make_async_remote_copy(
            src_ref=pick(other),
            dst_ref=target.at[place],
            send_sem=send_sem.at[other],
            recv_sem=recv_sem.at[place],
            device_id={axis: other},
            device_id_type=MESH,
        )

    others = [(mine + step) % count for step in range(1, count)]
    for other in others:
        copy(other, mine).start()
    for other in others:
        copy(other, mine).wait_send()
        copy(other, other).wait_recv()


def spread_kernel(source, target, middle, send_dp, recv_dp, send_tensor, recv_tensor):
    mine = lax.axis_index("dp")
    middle[mine] = source[mine]
    send_blocks("dp", lambda other: source.at[other], middle, send_dp, recv_dp)
    target[lax.axis_index("tensor")] = middle[...]
    send_blocks("tensor", lambda other: middle, target, send_tensor, recv_tensor)


def return_kernel(
    source, target, middle, summed, last, send_dp, recv_dp, send_tensor, recv_tensor
):
    place = lax.axis_index("tensor")
    middle[place] = source[place]
    send_blocks("tensor", lambda other: source.at[other], middle, send_tensor, recv_tensor)
    total = middle[0]
    for other in range(1, lax.axis_size("tensor")):
        total += middle[other]
    summed[...] = total
    mine = lax.axis_index("dp")
    last[mine] = summed[mine]
    send_blocks("dp", lambda other: summed.at[other], last, send_dp, recv_dp)
    target[...] = last[...]


def total_kernel(source, target, near, far, part, send_dp, recv_dp, send_tensor, recv_tensor):
    near[lax.axis_index("tensor")] = source[...]
    send_blocks("tensor", lambda other: source, near, send_tensor, recv_tensor)
    part[...] = jnp.sum(near[...], axis=0)
    far[lax.axis_index("dp")] = part[...]
    send_blocks("dp", lambda other: part, far, send_dp, recv_dp)
    target[...] = jnp.sum(far[...], axis=0)


def exchange_scratch(shapes):
    sizes = (lax.axis_size("dp"),) * 2 + (lax.axis_size("tensor"),) * 2
    return [pltpu.VMEM(shape, jnp.float32) for shape in shapes] + [
        pltpu.SemaphoreType.DMA((size,)) for size in sizes
    ]


CHUNKS = 4


def row_peers():
    mine = lax.axis_index("tensor")
    near = mine + 1 - 2 * (mine % 2)
    return (mine, near, (mine + 2) % 4, (near + 2) % 4)


def remote(source, target, sems, index, other):
    return pltpu.make_async_remote_copy(
        src_ref=source,
        dst_ref=target,
        send_sem=sems.at[0, index],
        recv_sem=sems.at[1, index],
        device_id={"tensor": other},
        device_id_type=MESH,
    )


def chunk_rows(total):
    size = total // CHUNKS
    return [slice(i * size, (i + 1) * size) for i in range(CHUNKS)]


def sum_blocks(partial, finish, work, sems):
    mine, near, far, both = row_peers()
    send_both, send_near, near_both, near_own, send_far, far_own, base = work
    size = base.shape[0] // 2
    chunks = chunk_rows(size)

    def terms(block, rows):
        start = pl.multiple_of((block % 2) * size + rows.start, size // CHUNKS)
        return base[pl.ds(start, size // CHUNKS), :]

    def hand_over(block, source, target, kind):
        copies = []
        for i, rows in enumerate(chunks):
            source[rows, :] = half(terms(block, rows))
            copies.append(
                remote(source.at[rows], target.at[rows], sems, CHUNKS * kind + i, near)
            )
            copies[i].start()
        return copies

    partial(far // 2, base)
    across = []
    for i, copy in enumerate(hand_over(both, send_both, near_both, 0)):
        rows = chunks[i]
        copy.wait()
        send_far[rows, :] = half(terms(far, rows) + near_both[rows, :].astype(jnp.float32))
        across.append(remote(send_far.at[rows], far_own.at[rows], sems, 2 * CHUNKS + i, far))
        across[i].start()
    partial(mine // 2, base)
    for i, copy in enumerate(hand_over(near, send_near, near_own, 1)):
        rows = chunks[i]
        copy.wait()
        across[i].wait()
        finish(
            i,
            rows,
            terms(mine, rows)
            + near_own[rows, :].astype(jnp.float32)
            + far_own[rows, :].astype(jnp.float32),
        )


SUM_SEMAPHORES = 3 * CHUNKS


def chip_rows(chip, size):
    return pl.ds(pl.multiple_of(chip * 2 * size, 2 * size), 2 * size)


def sum_scratch(rows, columns):
    narrow = pltpu.VMEM((rows, columns), jnp.bfloat16)
    return [narrow] * 6 + [pltpu.VMEM((2 * rows, columns), jnp.float32)]


class Spread:
    def __init__(self, gathered, sems, base):
        self.gathered, self.sems, self.base = gathered, sems, base
        self.mine, self.near, self.far, self.both = row_peers()
        self.chunks = chunk_rows(gathered.shape[1])
        self.started = []

    def copy(self, block, i, kind, other):
        part = self.gathered.at[block, self.chunks[i]]
        return remote(part, part, self.sems, self.base + CHUNKS * kind + i, other)

    def offer(self, i, value):
        self.gathered[self.mine, self.chunks[i], :] = value
        for kind, other in ((0, self.far), (1, self.near)):
            copy = self.copy(self.mine, i, kind, other)
            copy.start()
            self.started.append(copy)

    def settle(self):
        for i in range(CHUNKS):
            self.copy(self.far, i, 0, self.far).wait_recv()
            forward = self.copy(self.far, i, 2, self.near)
            forward.start()
            self.started.append(forward)
        for i in range(CHUNKS):
            self.copy(self.near, i, 1, self.near).wait_recv()
            self.copy(self.both, i, 2, self.near).wait_recv()
        for copy in self.started:
            copy.wait_send()


def tiles_of(total, size):
    def run(step):
        def body(index, carry):
            step(pl.ds(pl.multiple_of(index * size, size), size))
            return carry

        lax.fori_loop(0, total // size, body, 0)

    return run


def pick(chooser, factor, which, rows):
    width = factor.shape[1] // 4
    return jnp.dot(
        chooser[rows, :],
        factor[:, which * width : (which + 1) * width],
        precision=HIGH,
        preferred_element_type=jnp.float32,
    )


def add_up(place, target, value):
    target[place] += jnp.sum(value.reshape(-1, 8, value.shape[1]), axis=0)


def add_images(choose, i, place, target, value):
    target[place] += jnp.dot(
        choose[i], value, precision=HIGH, preferred_element_type=jnp.float32
    )


def enter_kernel(latents, factor, chooser, gain, gathered, sems):
    share = Spread(gathered, sems, 0)
    for i, rows in enumerate(share.chunks):
        scale = pick(chooser, factor, 0, rows)
        share.offer(i, enter_point(latents[rows, :].astype(jnp.float32), scale, gain[0:1]))
    share.settle()


def project_kernel(weight, captions, total, *rest):
    work, sems = rest[:-1], rest[-1]
    local = total.shape[0]

    def partial(chip, base):
        rows = chip_rows(chip, local)

        @tiles_of(captions.shape[0], 512)
        def _(columns):
            base[:, columns] = dot(weight[rows, :], captions[columns, :], 1, 1)

    def finish(i, rows, value):
        total[rows, :] = value

    sum_blocks(partial, finish, work, sems)


def transposed_partial(left, weight, lhs, size):
    def partial(chip, base):
        lhs[...] = half(left[:, chip_rows(chip, size)].astype(jnp.float32).T)

        @tiles_of(weight.shape[0], 512)
        def _(columns):
            base[:, columns] = dot(lhs[...], weight[columns, :], 1, 1)

    return partial


def attention_out_kernel(
    mixed, weight, latents, factor, chooser, gain, summed, middle, gathered, *rest
):
    lhs, work, sems = rest[0], rest[1:-1], rest[-1]
    share = Spread(gathered, sems, SUM_SEMAPHORES)

    def finish(i, rows, value):
        summed[rows, :] = value
        middle[rows, :], out = middle_point(
            value,
            latents[rows, :].astype(jnp.float32),
            pick(chooser, factor, 1, rows),
            pick(chooser, factor, 2, rows),
            gain[1:2],
            gain[2:3],
        )
        share.offer(i, out)

    sum_blocks(transposed_partial(mixed, weight, lhs, latents.shape[0]), finish, work, sems)
    share.settle()


def feed_kernel(
    inputs, feed, down, middle, factor, chooser, choose, cotangent, gain,
    gate_up, hidden, out, factor_grad, row_grad, gathered, *rest
):
    work, sems = rest[:-1], rest[-1]
    size = middle.shape[0]
    units = hidden.shape[1]
    factor_grad[...] = jnp.zeros_like(factor_grad)
    row_grad[...] = jnp.zeros_like(row_grad)

    def partial(chip, base):
        own = chip_rows(chip, size)

        @tiles_of(units, 512)
        def _(columns):
            other = pl.ds(pl.multiple_of(columns.start + units, 512), 512)
            first = dot(inputs[own, :], feed[:, columns], 1, 0)
            second = dot(inputs[own, :], feed[:, other], 1, 0)
            gate_up[own, columns] = first
            gate_up[own, other] = second
            hidden[own, columns] = half(first * jax.nn.sigmoid(first) * second)

        @tiles_of(down.shape[0], 512)
        def _(columns):
            base[:, columns] = dot(hidden[own, :], down[columns, :], 1, 1)

    share = Spread(gathered, sems, SUM_SEMAPHORES)

    def finish(i, rows, value):
        out[rows, :], back, gate_grad, row = end_point(
            value,
            middle[rows, :],
            pick(chooser, factor, 3, rows),
            cotangent[rows, :],
            gain[3:4],
        )
        share.offer(i, back)
        add_images(choose, i, 0, factor_grad, gate_grad)
        add_up(0, row_grad, row)

    sum_blocks(partial, finish, work, sems)
    share.settle()


def feed_back_kernel(
    back, gate_up, feed, down, summed, middle, factor, chooser, choose, cotangent, gain,
    pair, middle_grad, factor_grad, row_grad, gathered, *rest
):
    work, sems = rest[:-1], rest[-1]
    size = middle.shape[0]
    units = down.shape[1]
    factor_grad[...] = jnp.zeros_like(factor_grad)
    row_grad[...] = jnp.zeros_like(row_grad)

    def partial(chip, base):
        own = chip_rows(chip, size)

        @tiles_of(units, 512)
        def _(columns):
            other = pl.ds(pl.multiple_of(columns.start + units, 512), 512)
            grad = dot(back[own, :], down[:, columns], 1, 0)
            first, second = gate_up[own, columns], gate_up[own, other]
            pair[own, columns], pair[own, other] = pair_point(grad, first, second)

        @tiles_of(feed.shape[0], 512)
        def _(columns):
            base[:, columns] = dot(pair[own, :], feed[columns, :], 1, 1)

    share = Spread(gathered, sems, SUM_SEMAPHORES)

    def finish(i, rows, value):
        middle_grad[rows, :], out, gate_grad, scale_grad, first_row, second_row = (
            middle_back_point(
                value,
                summed[rows, :],
                middle[rows, :],
                pick(chooser, factor, 1, rows),
                pick(chooser, factor, 2, rows),
                cotangent[rows, :],
                gain[1:2],
                gain[2:3],
            )
        )
        share.offer(i, out)
        add_images(choose, i, 0, factor_grad, gate_grad)
        add_images(choose, i, 1, factor_grad, scale_grad)
        add_up(0, row_grad, first_row)
        add_up(1, row_grad, second_row)

    sum_blocks(partial, finish, work, sems)
    share.settle()


def enter_back_kernel(
    triple, weight, latents, factor, chooser, choose, middle_grad, gain,
    latent_grad, factor_grad, row_grad, *rest
):
    lhs, work, sems = rest[0], rest[1:-1], rest[-1]
    factor_grad[...] = jnp.zeros_like(factor_grad)
    row_grad[...] = jnp.zeros_like(row_grad)

    def finish(i, rows, value):
        latent_grad[rows, :], scale_grad, row = enter_back_point(
            value,
            latents[rows, :].astype(jnp.float32),
            pick(chooser, factor, 0, rows),
            middle_grad[rows, :],
            gain[0:1],
        )
        add_images(choose, i, 0, factor_grad, scale_grad)
        add_up(0, row_grad, row)

    sum_blocks(transposed_partial(triple, weight, lhs, latents.shape[0]), finish, work, sems)


def text_kernel(own, captions, summed, gathered, kept, sent, arrived, sems):
    mine, near, far, both = row_peers()
    other = dp_neighbour()
    odd = 1 - other % 2
    size = own.shape[0] // CHUNKS
    each = CHUNKS // 2
    started = []

    def part(k):
        base = (1 - odd) if k < each else odd
        return pl.ds(pl.multiple_of((base * each + k % each) * size, size), size)

    def move(block, k, kind, device):
        rows = gathered.at[block, part(k)]
        return remote(rows, rows, sems, CHUNKS * kind + k, device)

    def across(block, order, k):
        rows = pl.ds(k * size, size)
        return pltpu.make_async_remote_copy(
            src_ref=sent.at[block, rows],
            dst_ref=arrived.at[block, rows],
            send_sem=sems.at[0, 3 * CHUNKS + order * each + k],
            recv_sem=sems.at[1, 3 * CHUNKS + order * each + k],
            device_id={"dp": other},
            device_id_type=MESH,
        )

    def begin(copy):
        copy.start()
        started.append(copy)

    def work(block, order, k):
        value = dot(gathered[block, part(k), :], captions[...], 1, 0)
        rows = pl.ds((k % each) * size, size)
        if k < each:
            sent[block, rows, :] = half(value)
            begin(across(block, order, k))
        else:
            kept[block, rows, :] = value

    for k in range(CHUNKS):
        gathered[mine, part(k), :] = own[part(k), :]
        begin(move(mine, k, 0, far))
        begin(move(mine, k, 1, near))
    for k in range(CHUNKS):
        work(mine, 0, k)
    for k in range(CHUNKS):
        move(near, k, 1, near).wait_recv()
        work(near, 1, k)
    for k in range(CHUNKS):
        move(far, k, 0, far).wait_recv()
        begin(move(far, k, 2, near))
        work(far, 2, k)
        if k:
            move(both, k - 1, 2, near).wait_recv()
            work(both, 3, k - 1)
    move(both, CHUNKS - 1, 2, near).wait_recv()
    work(both, 3, CHUNKS - 1)
    for order, block in enumerate((mine, near, far, both)):
        for k in range(each):
            across(block, order, k).wait_recv()
            rows = pl.ds(k * size, size)
            summed[block, rows, :] = half(
                kept[block, rows, :] + arrived[block, rows, :].astype(jnp.float32)
            )
    for copy in started:
        copy.wait_send()


def enter_point(source, scale, gain):
    normed, _ = rms_parts(source)
    return half(normed * gain * (1.0 + scale))


def middle_point(summed, source, gate, scale, first_gain, second_gain):
    normed, _ = rms_parts(summed)
    middle = source + jnp.tanh(gate) * (normed * first_gain)
    return (middle, enter_point(middle, scale, second_gain))


def end_point(summed, middle, gate, cotangent, gain):
    normed, inverse = rms_parts(summed)
    turned = jnp.tanh(gate)
    branch = normed * gain
    grad = turned * cotangent
    return (
        middle + turned * branch,
        half(rms_back(normed, inverse, grad * gain)),
        cotangent * branch * (1.0 - turned * turned),
        grad * normed,
    )


def pair_point(grad, first, second):
    sigmoid = jax.nn.sigmoid(first)
    return (
        half(grad * second * (sigmoid + first * sigmoid * (1.0 - sigmoid))),
        half(grad * (first * sigmoid)),
    )


def middle_back_point(
    input_grad, summed, middle, gate, scale, cotangent, first_gain, second_gain
):
    normed, inverse = rms_parts(middle)
    gained = input_grad * (1.0 + scale)
    middle_grad = cotangent + rms_back(normed, inverse, gained * second_gain)
    scale_grad, second_row = input_grad * normed * second_gain, gained * normed
    normed, inverse = rms_parts(summed)
    turned = jnp.tanh(gate)
    branch = turned * middle_grad
    return (
        middle_grad,
        half(rms_back(normed, inverse, branch * first_gain)),
        middle_grad * (normed * first_gain) * (1.0 - turned * turned),
        scale_grad,
        branch * normed,
        second_row,
    )


def enter_back_point(input_grad, source, scale, middle_grad, gain):
    normed, inverse = rms_parts(source)
    gained = input_grad * (1.0 + scale)
    return (
        middle_grad + rms_back(normed, inverse, gained * gain),
        input_grad * normed * gain,
        gained * normed,
    )


def spans(heads):
    return [slice(head * HEAD, (head + 1) * HEAD) for head in range(heads)]


def head_norm(value):
    inverse = lax.rsqrt(jnp.mean(value * value, axis=0, keepdims=True) + EPS)
    return (value * inverse, inverse)


def head_back(normed, inverse, grad):
    return inverse * (grad - normed * jnp.mean(grad * normed, axis=0, keepdims=True))


def turn(value, cosine, sine):
    middle = HEAD // 2
    first, second = value[:middle], value[middle:]
    return jnp.concatenate(
        [first * cosine - second * sine, second * cosine + first * sine], axis=0
    )


def score_block(keys, query, bias):
    return jnp.exp2(dot(keys, query, 1, 0) * (HEAD ** (-0.5) * LOG2E) + bias)


def self_bias(step, ids_row, ids_column):
    start = pl.multiple_of(step * TILE, TILE)
    return jnp.where(ids_column[pl.ds(start, TILE), :] == ids_row[...], 0.0, NEG)


def cross_bias(step, ids_row, lengths):
    slots = lax.broadcasted_iota(jnp.int32, (TILE, 1), 0) < lengths[step]
    return jnp.where(slots & (ids_row[...] == step), 0.0, NEG)


def attend_tile(heads, meta, bias_of, query, key_rows, value, out, total, inv_ref):
    base = 2 * pl.program_id(0)
    out[...] = jnp.zeros_like(out)
    total[...] = jnp.zeros_like(total)

    def step(index, carry):
        bias = bias_of(index)
        rows = pl.ds(pl.multiple_of(index * TILE, TILE), TILE)
        for head, span in enumerate(spans(heads)):
            expo = score_block(key_rows[head, rows, :], query[span, :], bias)
            total[head] += jnp.sum(expo.reshape(TILE // 8, 8, TILE), axis=0)
            out[span, :] += dot(value[span, rows], half(expo), 1, 0)
        return carry

    lax.fori_loop(meta[base], meta[base + 1], step, 0)
    for head, span in enumerate(spans(heads)):
        inverse = 1.0 / jnp.sum(total[head], axis=0, keepdims=True)
        inv_ref[head] = jnp.broadcast_to(inverse, (8, TILE))
        out[span, :] = out[span, :] * inverse


def attend_back_tile(
    heads, meta, bias_of, query, key_rows, key, value_rows, inv_ref, out, back, dq, dk, dv, centre
):
    base = 2 * pl.program_id(0)
    scale = HEAD ** (-0.5)
    dq[...] = jnp.zeros_like(dq)
    for head, span in enumerate(spans(heads)):
        both = out[span, :] * back[span, :].astype(jnp.float32)
        centre[head] = jnp.broadcast_to(jnp.sum(both, axis=0, keepdims=True), (8, TILE))

    def step(index, carry):
        bias = bias_of(index)
        rows = pl.ds(pl.multiple_of(index * TILE, TILE), TILE)
        for head, span in enumerate(spans(heads)):
            probs = score_block(key_rows[head, rows, :], query[span, :], bias)
            probs = probs * inv_ref[head, 0:1, :]
            prob_grad = dot(value_rows[head, rows, :], back[span, :], 1, 0)
            score_grad = half(probs * (prob_grad - centre[head, 0:1, :]))
            dv[span, rows] += dot(back[span, :], half(probs), 1, 1)
            dk[span, rows] += dot(query[span, :], score_grad, 1, 1) * scale
            dq[span, :] += dot(key[span, rows], score_grad, 1, 0) * scale
        return carry

    lax.fori_loop(meta[base], meta[base + 1], step, 0)


def self_forward_kernel(
    heads,
    meta,
    ids_row,
    ids_column,
    gain,
    cosine,
    sine,
    cosine_all,
    sine_all,
    raw_query,
    raw_key,
    raw_value,
    query,
    key,
    key_rows,
    value_rows,
    out,
    inv_ref,
    value,
    total,
):
    local = heads * HEAD

    @pl.when(pl.program_id(0) == 0)
    def _():
        for head, span in enumerate(spans(heads)):
            normed, _ = head_norm(raw_key[span, :])
            turned = turn(normed * gain[span, 1:2], cosine_all[...], sine_all[...])
            key[span, :] = half(turned)
            key_rows[head] = half(turned.T)
            plain = raw_value[span, :]
            value[span, :] = half(plain)
            value_rows[head] = half(plain.T)

    for span in spans(heads):
        normed, _ = head_norm(raw_query[span, :])
        query[span, :] = half(turn(normed * gain[span, 0:1], cosine[...], sine[...]))
    attend_tile(
        heads,
        meta,
        lambda index: self_bias(index, ids_row, ids_column),
        query,
        key_rows,
        value,
        out,
        total,
        inv_ref,
    )


def cross_forward_kernel(
    heads,
    meta,
    lengths,
    ids_row,
    gain,
    query,
    own_out,
    raw_key,
    raw_value,
    key,
    key_rows,
    value_rows,
    out,
    inv_ref,
    mixed,
    value,
    total,
):
    @pl.when(pl.program_id(0) == 0)
    def _():
        for head, span in enumerate(spans(heads)):
            normed, _ = head_norm(raw_key[span, :])
            normed = normed * gain[span, 2:3]
            key[span, :] = half(normed)
            key_rows[head] = half(normed.T)
            plain = raw_value[span, :]
            value[span, :] = half(plain)
            value_rows[head] = half(plain.T)

    attend_tile(
        heads,
        meta,
        lambda index: cross_bias(index, ids_row, lengths),
        query,
        key_rows,
        value,
        out,
        total,
        inv_ref,
    )
    mixed[...] = half(own_out[...] + jnp.tanh(gain[:, 3:4]) * out[...])


def cross_backward_kernel(
    heads,
    meta,
    lengths,
    ids_row,
    gain,
    query,
    key_rows,
    key,
    value_rows,
    inv_ref,
    out,
    mixed_grad,
    raw_key,
    dq,
    dk,
    dv,
    gain_grad,
    back,
    centre,
    dk_sum,
    dv_sum,
    gate_sum,
):
    place = pl.program_id(0)

    @pl.when(place == 0)
    def _():
        dk_sum[...] = jnp.zeros_like(dk_sum)
        dv_sum[...] = jnp.zeros_like(dv_sum)
        gate_sum[...] = jnp.zeros_like(gate_sum)

    gate = jnp.tanh(gain[:, 3:4])
    back[...] = half(gate * mixed_grad[...])
    gate_sum[...] += mixed_grad[...] * out[...]
    attend_back_tile(
        heads,
        meta,
        lambda index: cross_bias(index, ids_row, lengths),
        query,
        key_rows,
        key,
        value_rows,
        inv_ref,
        out,
        back,
        dq,
        dk_sum,
        dv_sum,
        centre,
    )

    @pl.when(place == pl.num_programs(0) - 1)
    def _():
        dv[...] = half(dv_sum[...])
        gate_grad = jnp.sum(gate_sum[...], axis=1, keepdims=True) * (1.0 - gate * gate)
        gain_grad[:, 0:128] = jnp.broadcast_to(gate_grad, (heads * HEAD, 128))
        for span in spans(heads):
            normed, inverse = head_norm(raw_key[span, :])
            grad = dk_sum[span, :]
            summed = jnp.sum(grad * normed, axis=1, keepdims=True)
            gain_grad[span, 128:256] = jnp.broadcast_to(summed, (HEAD, 128))
            dk[span, :] = half(head_back(normed, inverse, grad * gain[span, 2:3]))


def self_backward_kernel(
    heads,
    meta,
    ids_row,
    ids_column,
    gain,
    cosine,
    sine,
    cosine_all,
    sine_all,
    query,
    key_rows,
    key,
    value_rows,
    inv_ref,
    out,
    mixed_grad,
    other_dq,
    raw_query,
    raw_key,
    triple,
    gain_grad,
    back,
    centre,
    dq,
    dk_sum,
    dv_sum,
    query_sum,
):
    place = pl.program_id(0)
    local = heads * HEAD

    @pl.when(place == 0)
    def _():
        dk_sum[...] = jnp.zeros_like(dk_sum)
        dv_sum[...] = jnp.zeros_like(dv_sum)
        query_sum[...] = jnp.zeros_like(query_sum)

    back[...] = half(mixed_grad[...])
    attend_back_tile(
        heads,
        meta,
        lambda index: self_bias(index, ids_row, ids_column),
        query,
        key_rows,
        key,
        value_rows,
        inv_ref,
        out,
        back,
        dq,
        dk_sum,
        dv_sum,
        centre,
    )
    columns = pl.ds(pl.multiple_of(place * TILE, TILE), TILE)
    for span in spans(heads):
        normed, inverse = head_norm(raw_query[span, :])
        grad = turn(dq[span, :] + other_dq[span, :], cosine[...], -sine[...])
        query_sum[span, :] += grad * normed
        triple[span, columns] = half(head_back(normed, inverse, grad * gain[span, 0:1]))

    @pl.when(place == pl.num_programs(0) - 1)
    def _():
        summed = jnp.sum(query_sum[...], axis=1, keepdims=True)
        gain_grad[:, 0:128] = jnp.broadcast_to(summed, (local, 128))
        triple[2 * local :, :] = half(dv_sum[...])
        for head, span in enumerate(spans(heads)):
            normed, inverse = head_norm(raw_key[span, :])
            grad = turn(dk_sum[span, :], cosine_all[...], -sine_all[...])
            summed = jnp.sum(grad * normed, axis=1, keepdims=True)
            gain_grad[span, 128:256] = jnp.broadcast_to(summed, (HEAD, 128))
            triple[local + head * HEAD : local + (head + 1) * HEAD, :] = half(
                head_back(normed, inverse, grad * gain[span, 1:2])
            )


def attention_call(kernel, name, scalars, operands, outs, scratch, tokens, weight, after=()):
    def block(array, tiled):
        lead = array.shape[:-1]
        if tiled is not True and tiled is not False:
            third = (lead[0] // 3, tokens if tiled else TILE)
            return pl.BlockSpec(third, lambda i, *_: (tiled, 0) if tiled else (0, i))
        if tiled:
            return pl.BlockSpec((*lead, TILE), lambda i, *_: (*([0] * len(lead)), i))
        return pl.BlockSpec(array.shape, lambda i, *_: (0,) * len(array.shape))

    count = len(scalars) + len(operands)

    def run(*refs):
        kernel(*refs[:count], *refs[count + len(after) :])

    return pl.pallas_call(
        run,
        grid_spec=pltpu.PrefetchScalarGridSpec(
            num_scalar_prefetch=len(scalars),
            grid=(tokens // TILE,),
            in_specs=[block(*operand) for operand in operands]
            + [pl.BlockSpec(memory_space=pl.ANY)] * len(after),
            out_specs=[block(*out) for out in outs],
            scratch_shapes=scratch,
        ),
        out_shape=[out for out, _ in outs],
        compiler_params=pltpu.CompilerParams(
            vmem_limit_bytes=58 * 1024 * 1024, dimension_semantics=("arbitrary",)
        ),
        cost_estimate=pl.CostEstimate(
            flops=weight, bytes_accessed=weight, transcendentals=0
        ),
        name=name,
    )(*scalars, *(operand for operand, _ in operands), *after)


def adamw(grad, weight, moment, square, decay, rate):
    moment_new = BETA1 * moment + (1.0 - BETA1) * grad
    square_new = BETA2 * square + (1.0 - BETA2) * grad * grad
    step_size = (
        moment_new / (1.0 - BETA1**STEP) / (jnp.sqrt(square_new / (1.0 - BETA2**STEP)) + ADAM_EPS)
    )
    return (moment_new, square_new, weight - rate * (step_size + decay * weight))


def body(
    latents,
    cotangent,
    captions,
    conditions,
    image_ids,
    rope_rows,
    rope_cols,
    caption_lengths,
    attention_in,
    attention_out,
    feed_in,
    feed_out,
    caption_in,
    modulator,
    channels,
    moment_attention_in,
    square_attention_in,
    moment_attention_out,
    square_attention_out,
    moment_feed_in,
    square_feed_in,
    moment_feed_out,
    square_feed_out,
    moment_caption_in,
    square_caption_in,
    moment_modulator,
    square_modulator,
    moment_channels,
    square_channels,
):
    tensor_size = lax.axis_size("tensor")
    tensor_index = lax.axis_index("tensor")
    dp_size = lax.axis_size("dp")
    dp_index = lax.axis_index("dp")
    shard_rows, width = latents.shape
    local = attention_in.shape[2]
    heads = local // HEAD
    units = feed_in.shape[2]
    segment = image_ids[0]
    row_tokens = segment.shape[0]
    images = conditions.shape[0]
    per_row = caption_lengths.shape[1]
    lengths = caption_lengths[0]
    slots = captions.shape[0]
    offset = tensor_index * local
    own_ids = lax.dynamic_slice_in_dim(segment, tensor_index * shard_rows, shard_rows)

    rows = attention_in.shape[1]
    fused = tensor_size == 4
    caption_half = half(caption_in)
    key_line = gather_far(caption_half[0].T)
    value_line = gather_far(caption_half[1].T)
    in_half = half(attention_in)
    attention_line = gather_far(jnp.concatenate([in_half[0], in_half[1], in_half[2]], axis=1))
    out_own = half(attention_out).T
    down_line = gather_far(half(feed_out).T)
    feed_half = half(feed_in)
    feed_own = jnp.concatenate([feed_half[0], feed_half[1]], axis=1)

    augmented = half(
        jnp.concatenate([jax.nn.silu(conditions), jnp.ones((images, 1), jnp.float32)], axis=1)
    )
    factor_part = jnp.dot(augmented, half(modulator), preferred_element_type=jnp.float32)
    own_columns = factor_part.shape[1]
    payload = jnp.concatenate(
        [
            factor_part.reshape(dp_size, per_row, own_columns),
            jnp.broadcast_to(
                lax.reduce_precision(channels, 8, 7).reshape(-1, own_columns),
                (dp_size, channels.size // own_columns, own_columns),
            ),
        ],
        axis=1,
    )
    received, out_other = remote_call(
        spread_kernel,
        "modulation_exchange",
        0,
        [payload],
        [jax.ShapeDtypeStruct((tensor_size, *payload.shape), jnp.float32)],
        exchange_scratch([payload.shape]),
        [out_own],
        everyone=True,
    )
    out_full = gather_far(join_near(out_own, out_other, rows))
    factor_row = jnp.transpose(received[:, :, :per_row], (2, 1, 0, 3)).reshape(per_row, -1)
    gains = received[0, :, per_row:].reshape(dp_size, 8, -1)
    gains = jnp.transpose(gains, (1, 0, 2)).reshape(8, width)
    local_gains = lax.dynamic_slice_in_dim(gains[4:], offset, local, 1).T
    chooser = (own_ids[:, None] == jnp.arange(per_row, dtype=jnp.int32)[None, :]).astype(
        jnp.float32
    )
    choose = jnp.transpose(chooser.reshape(CHUNKS, -1, per_row), (0, 2, 1))

    def token_factor(which):
        return pick(chooser, factor_row, which, slice(None))

    def split(value):
        return [value[i * shard_rows : (i + 1) * shard_rows] for i in range(tensor_size)]

    def by_image(*grads):
        return jnp.stack([jnp.dot(chooser.T, grad, precision=HIGH) for grad in grads])

    f32, bf16 = jnp.float32, jnp.bfloat16

    def shape(dims, dtype=f32):
        return jax.ShapeDtypeStruct(dims, dtype)

    gathered = shape((tensor_size, shard_rows, width), bf16)
    in_kernel = sum_scratch(shard_rows, width)

    def semaphores(count):
        return pltpu.SemaphoreType.DMA((2, count))

    sum_sems, all_sems = semaphores(SUM_SEMAPHORES), semaphores(SUM_SEMAPHORES + 3 * CHUNKS)
    source = latents.astype(f32)

    def caption_project(weight, carry, number):
        if fused:
            return remote_call(
                project_kernel,
                "project",
                number,
                [weight, captions],
                [shape((local, slots))],
                [*sum_scratch(local, slots), sum_sems],
                carry,
            )
        total = collect(
            [
                dot(
                    lax.dynamic_slice_in_dim(weight, owner(i) * local, local), captions, 1, 1
                )
                for i in range(tensor_size)
            ]
        )
        return (total, *(near_swap(array) for array in carry))

    if fused:
        attn_full, key_other = remote_call(
            enter_kernel,
            "enter",
            3,
            [latents, factor_row, chooser, gains],
            [gathered],
            [semaphores(3 * CHUNKS)],
            [key_line],
        )
        attn_full = attn_full.reshape(row_tokens, width)
    else:
        attn_full = in_place(spread(enter_point(source, token_factor(0), gains[0])))
        key_other = near_swap(key_line)
    text_key_raw, value_other, feed_other = caption_project(
        join_near(key_line, key_other, rows), [value_line, feed_own], 4
    )
    feed_full = gather_far(join_near(feed_own, feed_other, rows))
    text_value_raw, attention_other = caption_project(
        join_near(value_line, value_other, rows), [attention_line], 11
    )
    in_full = join_near(attention_line, attention_other, rows)
    projected = dot(in_full, attn_full, 0, 1)
    cosine, sine = rope_tables(rope_rows[0], rope_cols[0])

    tiles = row_tokens // TILE
    first_id = segment.reshape(tiles, TILE)[:, 0]
    last_id = segment.reshape(tiles, TILE)[:, TILE - 1]
    low = jnp.sum((segment[None] < first_id[:, None]).astype(jnp.int32), axis=1) // TILE
    high = (
        jnp.sum((segment[None] <= last_id[:, None]).astype(jnp.int32), axis=1) + TILE - 1
    ) // TILE
    self_meta = jnp.stack([low, high], axis=1).reshape(-1)
    cross_meta = jnp.stack([first_id, last_id + 1], axis=1).reshape(-1)
    ids_row = image_ids
    ids_column = segment[:, None]
    wide = jax.ShapeDtypeStruct((local, row_tokens), jnp.float32)
    narrow = jax.ShapeDtypeStruct((local, row_tokens), jnp.bfloat16)
    sums = jax.ShapeDtypeStruct((heads, 8, row_tokens), jnp.float32)
    by_rows = jax.ShapeDtypeStruct((heads, row_tokens, HEAD), jnp.bfloat16)
    text_narrow = jax.ShapeDtypeStruct((local, slots), jnp.bfloat16)
    text_rows = jax.ShapeDtypeStruct((heads, slots, HEAD), jnp.bfloat16)
    gain_shape = jax.ShapeDtypeStruct((local, 256), jnp.float32)
    tile_sums = pltpu.VMEM((heads, 8, TILE), jnp.float32)
    tables = [(cosine, True), (sine, True), (cosine, False), (sine, False)]
    queries, keys, key_rows, value_rows, own_out, own_inv = attention_call(
        functools.partial(self_forward_kernel, heads),
        "self_forward",
        [self_meta],
        [
            (ids_row, True),
            (ids_column, False),
            (local_gains, False),
            *tables,
            (projected, 0),
            (projected, 1),
            (projected, 2),
        ],
        [
            (narrow, True),
            (narrow, False),
            (by_rows, False),
            (by_rows, False),
            (wide, True),
            (sums, True),
        ],
        [pltpu.VMEM((local, row_tokens), jnp.bfloat16), tile_sums],
        row_tokens,
        15000,
    )
    text_keys, text_key_rows, text_value_rows, other_out, other_inv, mixed = attention_call(
        functools.partial(cross_forward_kernel, heads),
        "cross_forward",
        [cross_meta, lengths],
        [
            (ids_row, True),
            (local_gains, False),
            (queries, True),
            (own_out, True),
            (text_key_raw, False),
            (text_value_raw, False),
        ],
        [
            (text_narrow, False),
            (text_rows, False),
            (text_rows, False),
            (wide, True),
            (sums, True),
            (narrow, True),
        ],
        [pltpu.VMEM((local, slots), jnp.bfloat16), tile_sums],
        row_tokens,
        18000,
    )
    norm_gains = gains
    if fused:
        attn_sum, middle, feed_all, down_other = remote_call(
            attention_out_kernel,
            "attention_out",
            5,
            [mixed, out_full, latents, factor_row, chooser, norm_gains],
            [shape((shard_rows, width)), shape((shard_rows, width)), gathered],
            [pltpu.VMEM((2 * shard_rows, local), bf16), *in_kernel, all_sems],
            [down_line],
        )
        feed_all = feed_all.reshape(row_tokens, width)
        down_full = join_near(down_line, down_other, rows)
        gate_up, hidden, block_out, end_factor, end_row, feed_sum_grad = remote_call(
            feed_kernel,
            "feed_forward",
            6,
            [
                feed_all,
                feed_full,
                down_full,
                middle,
                factor_row,
                chooser,
                choose,
                cotangent,
                norm_gains,
            ],
            [
                shape((row_tokens, 2 * units)),
                shape((row_tokens, units), bf16),
                shape((shard_rows, width)),
                shape((1, per_row, width)),
                shape((1, 8, width)),
                gathered,
            ],
            [*in_kernel, all_sems],
        )
        feed_sum_grad = feed_sum_grad.reshape(row_tokens, width)
    else:
        attn_sum = collect(
            [
                dot(
                    lax.dynamic_slice_in_dim(mixed, owner(i) * shard_rows, shard_rows, 1),
                    out_full,
                    0,
                    1,
                )
                for i in range(tensor_size)
            ]
        )
        middle, feed_block = middle_point(
            attn_sum, source, token_factor(1), token_factor(2), gains[1], gains[2]
        )
        feed_all = in_place(spread(feed_block))
        down_full = join_near(down_line, near_swap(down_line), rows)
        gate_up = dot(feed_all, feed_full, 1, 0)
        hidden = half(jax.nn.silu(gate_up[:, :units]) * gate_up[:, units:])
        feed_sum = collect(split(dot(hidden, down_full, 1, 1)))
        block_out, feed_block_grad, *grads = end_point(
            feed_sum, middle, token_factor(3), cotangent, gains[3]
        )
        end_factor, end_row = by_image(grads[0]), grads[1][None]
        feed_sum_grad = in_place(spread(feed_block_grad))
    feed_out_grad = half(dot(feed_sum_grad, hidden, 0, 0))
    feed_out_parts = feed_out_grad.reshape(dp_size // 2, 2, -1, units)
    if fused:
        (
            pair_grad,
            middle_grad,
            middle_factor,
            middle_row,
            attn_sum_grad,
            feed_out_other,
        ) = remote_call(
            feed_back_kernel,
            "feed_backward",
            7,
            [
                feed_sum_grad,
                gate_up,
                feed_full,
                down_full,
                attn_sum,
                middle,
                factor_row,
                chooser,
                choose,
                cotangent,
                norm_gains,
            ],
            [
                shape((row_tokens, 2 * units), bf16),
                shape((shard_rows, width)),
                shape((2, per_row, width)),
                shape((2, 8, width)),
                gathered,
            ],
            [*in_kernel, all_sems],
            [feed_out_parts],
        )
        attn_sum_grad = attn_sum_grad.reshape(row_tokens, width)
    else:
        hidden_grad = dot(feed_sum_grad, down_full, 1, 0)
        pair_grad = jnp.concatenate(
            pair_point(hidden_grad, gate_up[:, :units], gate_up[:, units:]), axis=1
        )
        feed_input_grad = collect(split(dot(pair_grad, feed_full, 1, 1)))
        middle_grad, attn_block_grad, *grads = middle_back_point(
            feed_input_grad,
            attn_sum,
            middle,
            token_factor(1),
            token_factor(2),
            cotangent,
            gains[1],
            gains[2],
        )
        middle_factor, middle_row = by_image(*grads[:2]), jnp.stack(grads[2:])
        attn_sum_grad = in_place(spread(attn_block_grad))
        feed_out_other = swap_half(feed_out_parts)
    feed_out_sum = scatter_far(sum_half(feed_out_parts, feed_out_other))
    outer_grad = half(dot(feed_all, pair_grad, 0, 0))
    outer_both = lax.psum_scatter(
        outer_grad, "dp", scatter_dimension=0, tiled=True, axis_index_groups=far_groups()
    )
    mixed_grad = dot(out_full, gate(attn_sum_grad, outer_grad), 0, 1)
    out_parts = half(dot(attn_sum_grad, mixed, 0, 1)).reshape(dp_size // 2, 2, -1, local)
    query_two, text_key_grad, text_value_grad, text_gains = attention_call(
        functools.partial(cross_backward_kernel, heads),
        "cross_backward",
        [cross_meta, lengths],
        [
            (ids_row, True),
            (local_gains, False),
            (queries, True),
            (text_key_rows, False),
            (text_keys, False),
            (text_value_rows, False),
            (other_inv, True),
            (other_out, True),
            (mixed_grad, True),
            (text_key_raw, False),
        ],
        [(wide, True), (text_narrow, False), (text_narrow, False), (gain_shape, False)],
        [
            pltpu.VMEM((local, TILE), jnp.bfloat16),
            tile_sums,
            pltpu.VMEM((local, slots), jnp.float32),
            pltpu.VMEM((local, slots), jnp.float32),
            pltpu.VMEM((local, TILE), jnp.float32),
        ],
        row_tokens,
        25000,
    )
    triple_grad, own_gains = attention_call(
        functools.partial(self_backward_kernel, heads),
        "self_backward",
        [self_meta],
        [
            (ids_row, True),
            (ids_column, False),
            (local_gains, False),
            *tables,
            (queries, True),
            (key_rows, False),
            (keys, False),
            (value_rows, False),
            (own_inv, True),
            (own_out, True),
            (mixed_grad, True),
            (query_two, True),
            (projected, 0),
            (projected, 1),
        ],
        [
            (jax.ShapeDtypeStruct((3 * local, row_tokens), jnp.bfloat16), False),
            (gain_shape, False),
        ],
        [
            pltpu.VMEM((local, TILE), jnp.bfloat16),
            tile_sums,
            pltpu.VMEM((local, TILE), jnp.float32),
            pltpu.VMEM((local, row_tokens), jnp.float32),
            pltpu.VMEM((local, row_tokens), jnp.float32),
            pltpu.VMEM((local, TILE), jnp.float32),
        ],
        row_tokens,
        25000,
        [feed_out_sum],
    )
    in_parts = half(dot(attn_full, triple_grad, 0, 1)).reshape(dp_size // 2, 2, -1, 3 * local)

    if fused:
        latent_grad, enter_factor, enter_row, in_other = remote_call(
            enter_back_kernel,
            "enter_backward",
            10,
            [
                triple_grad,
                in_full,
                latents,
                factor_row,
                chooser,
                choose,
                middle_grad,
                norm_gains,
            ],
            [
                shape((shard_rows, width)),
                shape((1, per_row, width)),
                shape((1, 8, width)),
            ],
            [pltpu.VMEM((2 * shard_rows, 3 * local), bf16), *in_kernel, sum_sems],
            [in_parts],
        )
    else:
        attn_input_grad = collect(
            [
                dot(
                    lax.dynamic_slice_in_dim(triple_grad, owner(i) * shard_rows, shard_rows, 1),
                    in_full,
                    0,
                    1,
                )
                for i in range(tensor_size)
            ]
        )
        in_other = swap_half(in_parts)
        latent_grad, *grads = enter_back_point(
            attn_input_grad, source, token_factor(0), middle_grad, gains[0]
        )
        enter_factor, enter_row = by_image(grads[0]), grads[1][None]
    in_sum = scatter_far(sum_half(in_parts, in_other))

    columns = captions.shape[1]

    def caption_back(grad, carry, number, after):
        if not fused:
            parts = half(dot(in_place(spread(grad)), captions, 1, 0))
            parts = parts.reshape(dp_size // 2, 2, -1, columns)
            return (sum_half(parts, swap_half(parts)), *(swap_half(array) for array in carry))
        kept = (tensor_size, local // 2, columns)
        summed, _, *others = remote_call(
            text_kernel,
            "text_gradient",
            number,
            [grad, captions],
            [shape(kept, bf16), shape((tensor_size, local, slots), bf16)],
            [
                pltpu.VMEM(kept, f32),
                pltpu.VMEM(kept, bf16),
                pltpu.VMEM(kept, bf16),
                semaphores(5 * CHUNKS),
            ],
            carry,
            neighbour=True,
            after=after,
        )
        return (flat(summed), *others)

    value_grad, out_other = caption_back(text_value_grad, [out_parts], 8, [latent_grad])
    value_sum = scatter_far(
        jnp.concatenate([value_grad, sum_half(out_parts, out_other)], axis=1)
    )
    (key_grad,) = caption_back(text_key_grad, [], 9, [outer_both, value_grad])
    key_sum = scatter_far(key_grad)
    value_sum, out_sum = value_sum[:, :columns], value_sum[:, columns:]
    shared_rows = jnp.sum(
        jnp.concatenate([enter_row, middle_row, end_row]), axis=1
    )
    head_rows = jnp.stack(
        [own_gains[:, 0], own_gains[:, 128], text_gains[:, 128], text_gains[:, 0]]
    )
    head_full = lax.dynamic_update_slice(
        jnp.zeros((4, width), jnp.float32), head_rows, (jnp.zeros((), jnp.int32), offset)
    )
    channel_part = jnp.concatenate([shared_rows, head_full], axis=0)
    factor_image = jnp.concatenate([enter_factor, middle_factor, end_factor])
    factor_image = jnp.transpose(factor_image, (1, 0, 2))
    factor_image = jnp.transpose(
        factor_image.reshape(per_row, dp_size, tensor_size, own_columns), (2, 1, 0, 3)
    )
    channel_blocks = jnp.transpose(channel_part.reshape(8, dp_size, -1), (1, 0, 2))
    channel_blocks = channel_blocks.reshape(dp_size, -1, own_columns)
    payload = jnp.concatenate(
        [factor_image, jnp.broadcast_to(channel_blocks, (tensor_size, *channel_blocks.shape))],
        axis=2,
    )
    blocks = payload.shape[1:]
    outer_parts = outer_both.reshape(1, 2, -1, outer_both.shape[1])
    received, outer_other = remote_call(
        return_kernel,
        "modulation_return",
        1,
        [payload],
        [shape(blocks)],
        exchange_scratch([payload.shape, blocks, blocks]),
        [outer_parts],
        everyone=True,
        after=[in_sum],
    )
    feed_in_sum = lax.dynamic_index_in_dim(outer_parts, dp_index % 2, 1, keepdims=False)[0]
    feed_in_sum = feed_in_sum.astype(f32) + outer_other[0].astype(f32)
    factor_grad = received[:, :per_row].reshape(images, own_columns)
    channel_sum = jnp.sum(received[:, per_row:], axis=0).reshape(channels.shape)
    modulator_sum = jnp.dot(augmented.astype(jnp.float32).T, factor_grad, precision=HIGH)

    in_sum, out_sum, feed_in_sum, feed_out_sum, key_sum, value_sum = (
        value.astype(jnp.float32)
        for value in (in_sum, out_sum, feed_in_sum, feed_out_sum, key_sum, value_sum)
    )
    squares = (
        jnp.sum(in_sum * in_sum)
        + jnp.sum(out_sum * out_sum)
        + jnp.sum(feed_in_sum * feed_in_sum)
        + jnp.sum(feed_out_sum * feed_out_sum)
        + jnp.sum(key_sum * key_sum)
        + jnp.sum(value_sum * value_sum)
        + jnp.sum(modulator_sum * modulator_sum)
        + jnp.sum(channel_sum * channel_sum) / tensor_size
    )
    in_sum = jnp.stack([in_sum[:, i * local : (i + 1) * local] for i in range(3)])
    feed_in_sum = jnp.stack([feed_in_sum[:, i * units : (i + 1) * units] for i in range(2)])
    caption_sum = jnp.stack([key_sum.T, value_sum.T])
    (squares,) = remote_call(
        total_kernel,
        "norm_exchange",
        2,
        [jnp.broadcast_to(squares, (8, 128))],
        [shape((8, 128))],
        exchange_scratch([(tensor_size, 8, 128), (dp_size, 8, 128), (8, 128)]),
        everyone=True,
    )
    grad_norm = jnp.sqrt(squares[0, 0])
    factor = CLIP / jnp.maximum(grad_norm, CLIP)
    results = [
        adamw(grad * factor, weight, moment, square, DECAY, RATE)
        for grad, weight, moment, square in (
            (in_sum, attention_in, moment_attention_in, square_attention_in),
            (out_sum.T, attention_out, moment_attention_out, square_attention_out),
            (feed_in_sum, feed_in, moment_feed_in, square_feed_in),
            (feed_out_sum.T, feed_out, moment_feed_out, square_feed_out),
            (caption_sum, caption_in, moment_caption_in, square_caption_in),
            (modulator_sum, modulator, moment_modulator, square_modulator),
        )
    ]
    results.append(
        adamw(channel_sum * factor, channels, moment_channels, square_channels, 0.0, GAIN_RATE)
    )
    return (block_out, latent_grad, grad_norm, *(part for result in results for part in result))


def solution(mesh):
    return jax.shard_map(
        body,
        mesh=mesh,
        in_specs=(
            P(("dp", "tensor"), None),
            P(("dp", "tensor"), None),
            P("dp", "tensor"),
            P(),
            P("dp", None),
            P("dp", None),
            P("dp", None),
            P("dp", None),
            P(None, "dp", "tensor"),
            P("tensor", "dp"),
            P(None, "dp", "tensor"),
            P("tensor", "dp"),
            P(None, "tensor", "dp"),
            P(None, ("dp", "tensor")),
            P(None, "dp"),
            P(None, "dp", "tensor"),
            P(None, "dp", "tensor"),
            P("tensor", "dp"),
            P("tensor", "dp"),
            P(None, "dp", "tensor"),
            P(None, "dp", "tensor"),
            P("tensor", "dp"),
            P("tensor", "dp"),
            P(None, "tensor", "dp"),
            P(None, "tensor", "dp"),
            P(None, ("dp", "tensor")),
            P(None, ("dp", "tensor")),
            P(None, "dp"),
            P(None, "dp"),
        ),
        out_specs=(
            P(("dp", "tensor"), None),
            P(("dp", "tensor"), None),
            P(),
            P(None, "dp", "tensor"),
            P(None, "dp", "tensor"),
            P(None, "dp", "tensor"),
            P("tensor", "dp"),
            P("tensor", "dp"),
            P("tensor", "dp"),
            P(None, "dp", "tensor"),
            P(None, "dp", "tensor"),
            P(None, "dp", "tensor"),
            P("tensor", "dp"),
            P("tensor", "dp"),
            P("tensor", "dp"),
            P(None, "tensor", "dp"),
            P(None, "tensor", "dp"),
            P(None, "tensor", "dp"),
            P(None, ("dp", "tensor")),
            P(None, ("dp", "tensor")),
            P(None, ("dp", "tensor")),
            P(None, "dp"),
            P(None, "dp"),
            P(None, "dp"),
        ),
        check_vma=False,
    )
```

```python
import functools
import math

import jax
import jax.numpy as jnp
from jax import lax
from jax.experimental import pallas as pl
from jax.experimental.pallas import tpu as pltpu
from jax.sharding import PartitionSpec as P

HEAD = 64
CAP = 256
STEP = 10


EPS = 1e-06
NEG = -1e30
THETA = 10000.0
BETA1 = 0.9
BETA2 = 0.95
RATE = 0.05
GAIN_RATE = 0.8
DECAY = 0.1
ADAM_EPS = 1e-08
CLIP = 1.0
HIGH = lax.Precision.HIGHEST


def half(value):
    return value.astype(jnp.bfloat16)


TILE = 256
AHEAD = 2
LOG2E = 1.0 / math.log(2.0)
MESH = pl.DeviceIdType.MESH


def dot(left, right, left_dim, right_dim):
    return lax.dot_general(
        left, right, (((left_dim,), (right_dim,)), ((), ())), preferred_element_type=jnp.float32
    )


def rms_parts(value, axis=-1):
    inverse = lax.rsqrt(jnp.mean(value * value, axis=axis, keepdims=True) + EPS)
    return (value * inverse, inverse)


def rms_back(normed, inverse, grad, axis=-1):
    return inverse * (grad - normed * jnp.mean(grad * normed, axis=axis, keepdims=True))


def rope_tables(rows, columns):
    quarter = HEAD // 4
    frequency = THETA ** (-jnp.arange(quarter, dtype=jnp.float32) / quarter)
    angles = jnp.concatenate(
        [
            frequency[:, None] * rows.astype(jnp.float32)[None, :],
            frequency[:, None] * columns.astype(jnp.float32)[None, :],
        ],
        axis=0,
    )
    return (jnp.cos(angles), jnp.sin(angles))


def gate_kernel(value, after, out):
    del value, after, out


def gate(value, after):
    anywhere = pl.BlockSpec(memory_space=pl.ANY)
    return pl.pallas_call(
        gate_kernel,
        out_shape=jax.ShapeDtypeStruct(value.shape, value.dtype),
        in_specs=[anywhere, anywhere],
        out_specs=anywhere,
        input_output_aliases={0: 0},
        name="gate",
    )(value, after)


def near_swap(value):
    return lax.ppermute(value, "dp", [(i, i ^ 1) for i in range(lax.axis_size("dp"))])


def far_groups():
    count = lax.axis_size("dp")
    return [list(range(near, count, 2)) for near in range(2)]


def gather_far(value):
    return lax.all_gather(value, "dp", axis=0, tiled=True, axis_index_groups=far_groups())


def flat(blocks):
    return blocks.reshape(-1, blocks.shape[-1])


def join_near(own, other, count):
    odd = lax.axis_index("dp") % 2
    own = own.reshape(-1, count, own.shape[1])
    other = other.reshape(own.shape)
    return flat(
        jnp.stack([jnp.where(odd == 0, own, other), jnp.where(odd == 0, other, own)], axis=1)
    )


def swap_half(parts):
    odd = lax.axis_index("dp") % 2
    send = lax.dynamic_index_in_dim(parts, 1 - odd, 1, keepdims=False)
    return near_swap(send.reshape(-1, send.shape[2])).reshape(send.shape)


def sum_half(parts, other):
    odd = lax.axis_index("dp") % 2
    keep = lax.dynamic_index_in_dim(parts, odd, 1, keepdims=False)
    return flat(half(keep.astype(jnp.float32) + other.astype(jnp.float32)))


def scatter_far(value):
    return lax.psum_scatter(
        value, "dp", scatter_dimension=0, tiled=True, axis_index_groups=far_groups()
    )


def swap_tensor(value, bits):
    return lax.ppermute(value, "tensor", [(i, i ^ bits) for i in range(lax.axis_size("tensor"))])


def owner(place):
    if lax.axis_size("tensor") == 4:
        return lax.axis_index("tensor") ^ place
    return jnp.int32(place)


def spread(value):
    count = lax.axis_size("tensor")
    if count == 4:
        near = swap_tensor(value, 1)
        far = swap_tensor(value, 2)
        return [value, near, far, swap_tensor(far, 1)]
    whole = lax.all_gather(value, "tensor", axis=0, tiled=False)
    return [whole[i] for i in range(count)]


def collect_near(parts):
    if len(parts) == 4:
        rows = parts[0].shape[0]
        sent = swap_tensor(half(jnp.concatenate([parts[3], parts[1]], axis=0)), 1)
        sent = sent.astype(jnp.float32)
        return (parts[0] + sent[rows:], half(parts[2] + sent[:rows]))
    return (half(jnp.concatenate(parts, axis=0)),)


def collect_far(sums):
    if len(sums) == 2:
        return sums[0] + swap_tensor(sums[1], 2).astype(jnp.float32)
    return lax.psum_scatter(
        sums[0], "tensor", scatter_dimension=0, tiled=True
    ).astype(jnp.float32)


def collect(parts):
    return collect_far(collect_near(parts))


def in_place(blocks):
    if len(blocks) == 4:
        stacked = jnp.stack(blocks)
        mine = lax.axis_index("tensor")
        blocks = [
            lax.dynamic_index_in_dim(stacked, mine ^ i, 0, keepdims=False)
            for i in range(len(blocks))
        ]
    return jnp.concatenate(blocks, axis=0)


def dp_neighbour():
    mine = lax.axis_index("dp")
    return mine + 1 - 2 * (mine % 2)


def meet(everyone, neighbour):
    barrier = pltpu.get_barrier_semaphore()
    if everyone:
        others = [
            {axis: (lax.axis_index(axis) + step) % lax.axis_size(axis)}
            for axis in ("dp", "tensor")
            for step in range(1, lax.axis_size(axis))
        ]
    else:
        _, near, far, _ = row_peers()
        others = [{"tensor": near}, {"tensor": far}]
        if neighbour:
            others.append({"dp": dp_neighbour()})
    for other in others:
        pl.semaphore_signal(barrier, inc=1, device_id=other, device_id_type=MESH)
    pl.semaphore_wait(barrier, len(others))


def remote_call(
    kernel, name, number, operands, outs, scratch, carry=(), everyone=False, neighbour=False, after=()
):
    copies = sum(array.shape[0] if len(array.shape) == 4 else 1 for array in carry)
    traded = [
        jax.ShapeDtypeStruct(
            (array.shape[0], *array.shape[2:]) if len(array.shape) == 4 else array.shape,
            array.dtype,
        )
        for array in carry
    ]

    def run(*refs):
        refs = list(refs)
        ins = [refs.pop(0) for _ in operands]
        sources = [refs.pop(0) for _ in carry]
        del refs[: len(after)]
        results = [refs.pop(0) for _ in outs]
        targets = [refs.pop(0) for _ in carry]
        meet(everyone, neighbour or bool(carry))
        started = []
        if carry:
            sems = refs.pop()
            other = dp_neighbour()
            pairs = []
            for source, target in zip(sources, targets):
                if len(source.shape) == 2:
                    pairs.append((source, target))
                else:
                    pairs += [
                        (source.at[i, other % 2], target.at[i]) for i in range(source.shape[0])
                    ]
            for i, (source, target) in enumerate(pairs):
                copy = pltpu.make_async_remote_copy(
                    src_ref=source,
                    dst_ref=target,
                    send_sem=sems.at[0, i],
                    recv_sem=sems.at[1, i],
                    device_id={"dp": other},
                    device_id_type=MESH,
                )
                copy.start()
                started.append(copy)
        kernel(*ins, *results, *refs)
        for copy in started:
            copy.wait()

    whole = pl.BlockSpec(memory_space=pltpu.VMEM)
    anywhere = pl.BlockSpec(memory_space=pl.ANY)
    return pl.pallas_call(
        run,
        out_shape=[*outs, *traded],
        in_specs=[whole] * len(operands) + [anywhere] * (len(carry) + len(after)),
        out_specs=[whole] * len(outs) + [anywhere] * len(carry),
        scratch_shapes=[
            *scratch,
            *([pltpu.SemaphoreType.DMA((2, copies))] if carry else []),
        ],
        compiler_params=pltpu.CompilerParams(
            collective_id=number, has_side_effects=True, vmem_limit_bytes=60 * 1024 * 1024
        ),
        cost_estimate=pl.CostEstimate(flops=1 << 20, bytes_accessed=1 << 20, transcendentals=0),
        name=name,
    )(*operands, *carry, *after)


def send_blocks(axis, pick, target, send_sem, recv_sem):
    count = lax.axis_size(axis)
    mine = lax.axis_index(axis)

    def copy(other, place):
        return pltpu.make_async_remote_copy(
            src_ref=pick(other),
            dst_ref=target.at[place],
            send_sem=send_sem.at[other],
            recv_sem=recv_sem.at[place],
            device_id={axis: other},
            device_id_type=MESH,
        )

    others = [(mine + step) % count for step in range(1, count)]
    for other in others:
        copy(other, mine).start()
    for other in others:
        copy(other, mine).wait_send()
        copy(other, other).wait_recv()


def spread_kernel(source, target, middle, send_dp, recv_dp, send_tensor, recv_tensor):
    mine = lax.axis_index("dp")
    middle[mine] = source[mine]
    send_blocks("dp", lambda other: source.at[other], middle, send_dp, recv_dp)
    target[lax.axis_index("tensor")] = middle[...]
    send_blocks("tensor", lambda other: middle, target, send_tensor, recv_tensor)


def return_kernel(
    source, target, middle, summed, last, send_dp, recv_dp, send_tensor, recv_tensor
):
    place = lax.axis_index("tensor")
    middle[place] = source[place]
    send_blocks("tensor", lambda other: source.at[other], middle, send_tensor, recv_tensor)
    total = middle[0]
    for other in range(1, lax.axis_size("tensor")):
        total += middle[other]
    summed[...] = total
    mine = lax.axis_index("dp")
    last[mine] = summed[mine]
    send_blocks("dp", lambda other: summed.at[other], last, send_dp, recv_dp)
    target[...] = last[...]


def total_kernel(source, target, near, far, part, send_dp, recv_dp, send_tensor, recv_tensor):
    near[lax.axis_index("tensor")] = source[...]
    send_blocks("tensor", lambda other: source, near, send_tensor, recv_tensor)
    part[...] = jnp.sum(near[...], axis=0)
    far[lax.axis_index("dp")] = part[...]
    send_blocks("dp", lambda other: part, far, send_dp, recv_dp)
    target[...] = jnp.sum(far[...], axis=0)


def exchange_scratch(shapes):
    sizes = (lax.axis_size("dp"),) * 2 + (lax.axis_size("tensor"),) * 2
    return [pltpu.VMEM(shape, jnp.float32) for shape in shapes] + [
        pltpu.SemaphoreType.DMA((size,)) for size in sizes
    ]


CHUNKS = 4


def row_peers():
    mine = lax.axis_index("tensor")
    near = mine + 1 - 2 * (mine % 2)
    return (mine, near, (mine + 2) % 4, (near + 2) % 4)


def remote(source, target, sems, index, other):
    return pltpu.make_async_remote_copy(
        src_ref=source,
        dst_ref=target,
        send_sem=sems.at[0, index],
        recv_sem=sems.at[1, index],
        device_id={"tensor": other},
        device_id_type=MESH,
    )


def chunk_rows(total):
    size = total // CHUNKS
    return [slice(i * size, (i + 1) * size) for i in range(CHUNKS)]


def sum_blocks(partial, finish, work, sems, by_columns=False):
    mine, near, far, both = row_peers()
    send_both, send_near, near_both, near_own, send_far, far_own, base = work
    size, width = base.shape[0] // 2, base.shape[1]
    step = width // CHUNKS
    if by_columns:
        chunks = [(slice(None), slice(i * step, (i + 1) * step)) for i in range(CHUNKS)]
    else:
        chunks = [(rows, slice(None)) for rows in chunk_rows(size)]

    def terms(block, place):
        rows, columns = place
        first, count = rows.start or 0, size if by_columns else size // CHUNKS
        start = pl.multiple_of((block % 2) * size + first, count)
        return base[pl.ds(start, count), columns]

    def hand_over(chip, block, source, target, kind):
        copies = []
        if not by_columns:
            partial(chip, base, None)
        for i, place in enumerate(chunks):
            if by_columns:
                partial(chip, base, place[1])
            source[place] = half(terms(block, place))
            copies.append(
                remote(source.at[place], target.at[place], sems, CHUNKS * kind + i, near)
            )
            copies[i].start()
            if by_columns and i:
                yield i - 1, copies[i - 1]
        for i in range(CHUNKS - 1 if by_columns else 0, CHUNKS):
            yield i, copies[i]

    across = []
    for i, copy in hand_over(far // 2, both, send_both, near_both, 0):
        place = chunks[i]
        copy.wait()
        send_far[place] = half(terms(far, place) + near_both[place].astype(jnp.float32))
        across.append(
            remote(send_far.at[place], far_own.at[place], sems, 2 * CHUNKS + i, far)
        )
        across[i].start()
    for i, copy in hand_over(mine // 2, near, send_near, near_own, 1):
        place = chunks[i]
        copy.wait()
        across[i].wait()
        finish(
            i,
            place[1] if by_columns else place[0],
            terms(mine, place)
            + near_own[place].astype(jnp.float32)
            + far_own[place].astype(jnp.float32),
        )


SUM_SEMAPHORES = 3 * CHUNKS


def chip_rows(chip, size):
    return pl.ds(pl.multiple_of(chip * 2 * size, 2 * size), 2 * size)


def sum_scratch(rows, columns):
    narrow = pltpu.VMEM((rows, columns), jnp.bfloat16)
    return [narrow] * 6 + [pltpu.VMEM((2 * rows, columns), jnp.float32)]


class Spread:
    def __init__(self, gathered, sems, base):
        self.gathered, self.sems, self.base = gathered, sems, base
        self.mine, self.near, self.far, self.both = row_peers()
        self.chunks = chunk_rows(gathered.shape[1])
        self.started = []

    def copy(self, block, i, kind, other):
        part = self.gathered.at[block, self.chunks[i]]
        return remote(part, part, self.sems, self.base + CHUNKS * kind + i, other)

    def offer(self, i, value):
        self.gathered[self.mine, self.chunks[i], :] = value
        for kind, other in ((0, self.far), (1, self.near)):
            copy = self.copy(self.mine, i, kind, other)
            copy.start()
            self.started.append(copy)

    def settle(self):
        for i in range(CHUNKS):
            self.copy(self.far, i, 0, self.far).wait_recv()
            forward = self.copy(self.far, i, 2, self.near)
            forward.start()
            self.started.append(forward)
        for i in range(CHUNKS):
            self.copy(self.near, i, 1, self.near).wait_recv()
            self.copy(self.both, i, 2, self.near).wait_recv()
        for copy in self.started:
            copy.wait_send()


def tiles_of(total, size):
    def run(step):
        def body(index, carry):
            step(pl.ds(pl.multiple_of(index * size, size), size))
            return carry

        lax.fori_loop(0, total // size, body, 0)

    return run


def pick(chooser, factor, which, rows):
    width = factor.shape[1] // 4
    return jnp.dot(
        chooser[rows, :],
        factor[:, which * width : (which + 1) * width],
        precision=HIGH,
        preferred_element_type=jnp.float32,
    )


def add_up(place, target, value):
    target[place] += jnp.sum(value.reshape(-1, 8, value.shape[1]), axis=0)


def add_images(choose, i, place, target, value):
    target[place] += jnp.dot(
        choose[i], value, precision=HIGH, preferred_element_type=jnp.float32
    )


def enter_kernel(latents, factor, chooser, gain, gathered, sems):
    share = Spread(gathered, sems, 0)
    for i, rows in enumerate(share.chunks):
        scale = pick(chooser, factor, 0, rows)
        share.offer(i, enter_point(latents[rows, :].astype(jnp.float32), scale, gain[0:1]))
    share.settle()


def project_kernel(weight, captions, total, *rest):
    work, sems = rest[:-1], rest[-1]
    local = total.shape[0]

    def partial(chip, base, columns):
        base[:, columns] = dot(weight[chip_rows(chip, local), :], captions[columns, :], 1, 1)

    def finish(i, columns, value):
        total[:, columns] = value

    sum_blocks(partial, finish, work, sems, by_columns=True)


def transposed_partial(left, weight, lhs, size):
    def partial(chip, base, _):
        lhs[...] = half(left[:, chip_rows(chip, size)].astype(jnp.float32).T)

        @tiles_of(weight.shape[0], 512)
        def _(columns):
            base[:, columns] = dot(lhs[...], weight[columns, :], 1, 1)

    return partial


def attention_out_kernel(
    mixed, weight, latents, factor, chooser, gain, summed, middle, gathered, *rest
):
    lhs, work, sems = rest[0], rest[1:-1], rest[-1]
    share = Spread(gathered, sems, SUM_SEMAPHORES)

    def finish(i, rows, value):
        summed[rows, :] = value
        middle[rows, :], out = middle_point(
            value,
            latents[rows, :].astype(jnp.float32),
            pick(chooser, factor, 1, rows),
            pick(chooser, factor, 2, rows),
            gain[1:2],
            gain[2:3],
        )
        share.offer(i, out)

    sum_blocks(transposed_partial(mixed, weight, lhs, latents.shape[0]), finish, work, sems)
    share.settle()


def feed_kernel(
    inputs, feed, down, middle, factor, chooser, choose, cotangent, gain,
    gate_up, hidden, out, factor_grad, row_grad, gathered, *rest
):
    work, sems = rest[:-1], rest[-1]
    size = middle.shape[0]
    units = hidden.shape[1]
    factor_grad[...] = jnp.zeros_like(factor_grad)
    row_grad[...] = jnp.zeros_like(row_grad)

    def partial(chip, base, _):
        own = chip_rows(chip, size)

        @tiles_of(units, 512)
        def _(columns):
            other = pl.ds(pl.multiple_of(columns.start + units, 512), 512)
            first = dot(inputs[own, :], feed[:, columns], 1, 0)
            second = dot(inputs[own, :], feed[:, other], 1, 0)
            gate_up[own, columns] = first
            gate_up[own, other] = second
            hidden[own, columns] = half(first * jax.nn.sigmoid(first) * second)

        @tiles_of(down.shape[0], 512)
        def _(columns):
            base[:, columns] = dot(hidden[own, :], down[columns, :], 1, 1)

    share = Spread(gathered, sems, SUM_SEMAPHORES)

    def finish(i, rows, value):
        out[rows, :], back, gate_grad, row = end_point(
            value,
            middle[rows, :],
            pick(chooser, factor, 3, rows),
            cotangent[rows, :],
            gain[3:4],
        )
        share.offer(i, back)
        add_images(choose, i, 0, factor_grad, gate_grad)
        add_up(0, row_grad, row)

    sum_blocks(partial, finish, work, sems)
    share.settle()


def feed_back_kernel(
    back, gate_up, feed, down, summed, middle, factor, chooser, choose, cotangent, gain,
    pair, middle_grad, factor_grad, row_grad, gathered, *rest
):
    work, sems = rest[:-1], rest[-1]
    size = middle.shape[0]
    units = down.shape[1]
    factor_grad[...] = jnp.zeros_like(factor_grad)
    row_grad[...] = jnp.zeros_like(row_grad)

    def partial(chip, base, _):
        own = chip_rows(chip, size)

        @tiles_of(units, 512)
        def _(columns):
            other = pl.ds(pl.multiple_of(columns.start + units, 512), 512)
            grad = dot(back[own, :], down[:, columns], 1, 0)
            first, second = gate_up[own, columns], gate_up[own, other]
            pair[own, columns], pair[own, other] = pair_point(grad, first, second)

        @tiles_of(feed.shape[0], 512)
        def _(columns):
            base[:, columns] = dot(pair[own, :], feed[columns, :], 1, 1)

    share = Spread(gathered, sems, SUM_SEMAPHORES)

    def finish(i, rows, value):
        middle_grad[rows, :], out, gate_grad, scale_grad, first_row, second_row = (
            middle_back_point(
                value,
                summed[rows, :],
                middle[rows, :],
                pick(chooser, factor, 1, rows),
                pick(chooser, factor, 2, rows),
                cotangent[rows, :],
                gain[1:2],
                gain[2:3],
            )
        )
        share.offer(i, out)
        add_images(choose, i, 0, factor_grad, gate_grad)
        add_images(choose, i, 1, factor_grad, scale_grad)
        add_up(0, row_grad, first_row)
        add_up(1, row_grad, second_row)

    sum_blocks(partial, finish, work, sems)
    share.settle()


def enter_back_kernel(
    triple, weight, latents, factor, chooser, choose, middle_grad, gain,
    latent_grad, factor_grad, row_grad, *rest
):
    lhs, work, sems = rest[0], rest[1:-1], rest[-1]
    factor_grad[...] = jnp.zeros_like(factor_grad)
    row_grad[...] = jnp.zeros_like(row_grad)

    def finish(i, rows, value):
        latent_grad[rows, :], scale_grad, row = enter_back_point(
            value,
            latents[rows, :].astype(jnp.float32),
            pick(chooser, factor, 0, rows),
            middle_grad[rows, :],
            gain[0:1],
        )
        add_images(choose, i, 0, factor_grad, scale_grad)
        add_up(0, row_grad, row)

    sum_blocks(transposed_partial(triple, weight, lhs, latents.shape[0]), finish, work, sems)


def text_kernel(own, captions, summed, gathered, kept, sent, arrived, sems):
    mine, near, far, both = row_peers()
    other = dp_neighbour()
    odd = 1 - other % 2
    size = own.shape[0] // CHUNKS
    each = CHUNKS // 2
    started = []

    def part(k):
        base = (1 - odd) if k < each else odd
        return pl.ds(pl.multiple_of((base * each + k % each) * size, size), size)

    def move(block, k, kind, device):
        rows = gathered.at[block, part(k)]
        return remote(rows, rows, sems, CHUNKS * kind + k, device)

    def across(block, order, k):
        rows = pl.ds(k * size, size)
        return pltpu.make_async_remote_copy(
            src_ref=sent.at[block, rows],
            dst_ref=arrived.at[block, rows],
            send_sem=sems.at[0, 3 * CHUNKS + order * each + k],
            recv_sem=sems.at[1, 3 * CHUNKS + order * each + k],
            device_id={"dp": other},
            device_id_type=MESH,
        )

    def begin(copy):
        copy.start()
        started.append(copy)

    def work(block, order, k):
        value = dot(gathered[block, part(k), :], captions[...], 1, 0)
        rows = pl.ds((k % each) * size, size)
        if k < each:
            sent[block, rows, :] = half(value)
            begin(across(block, order, k))
        else:
            kept[block, rows, :] = value

    for k in range(CHUNKS):
        gathered[mine, part(k), :] = own[part(k), :]
        begin(move(mine, k, 0, far))
        begin(move(mine, k, 1, near))
    for k in range(CHUNKS):
        work(mine, 0, k)
    for k in range(CHUNKS):
        move(near, k, 1, near).wait_recv()
        work(near, 1, k)
    for k in range(CHUNKS):
        move(far, k, 0, far).wait_recv()
        begin(move(far, k, 2, near))
        work(far, 2, k)
        if k:
            move(both, k - 1, 2, near).wait_recv()
            work(both, 3, k - 1)
    move(both, CHUNKS - 1, 2, near).wait_recv()
    work(both, 3, CHUNKS - 1)
    for order, block in enumerate((mine, near, far, both)):
        for k in range(each):
            across(block, order, k).wait_recv()
            rows = pl.ds(k * size, size)
            summed[block, rows, :] = half(
                kept[block, rows, :] + arrived[block, rows, :].astype(jnp.float32)
            )
    for copy in started:
        copy.wait_send()


def enter_point(source, scale, gain):
    normed, _ = rms_parts(source)
    return half(normed * gain * (1.0 + scale))


def middle_point(summed, source, gate, scale, first_gain, second_gain):
    normed, _ = rms_parts(summed)
    middle = source + jnp.tanh(gate) * (normed * first_gain)
    return (middle, enter_point(middle, scale, second_gain))


def end_point(summed, middle, gate, cotangent, gain):
    normed, inverse = rms_parts(summed)
    turned = jnp.tanh(gate)
    branch = normed * gain
    grad = turned * cotangent
    return (
        middle + turned * branch,
        half(rms_back(normed, inverse, grad * gain)),
        cotangent * branch * (1.0 - turned * turned),
        grad * normed,
    )


def pair_point(grad, first, second):
    sigmoid = jax.nn.sigmoid(first)
    return (
        half(grad * second * (sigmoid + first * sigmoid * (1.0 - sigmoid))),
        half(grad * (first * sigmoid)),
    )


def middle_back_point(
    input_grad, summed, middle, gate, scale, cotangent, first_gain, second_gain
):
    normed, inverse = rms_parts(middle)
    gained = input_grad * (1.0 + scale)
    middle_grad = cotangent + rms_back(normed, inverse, gained * second_gain)
    scale_grad, second_row = input_grad * normed * second_gain, gained * normed
    normed, inverse = rms_parts(summed)
    turned = jnp.tanh(gate)
    branch = turned * middle_grad
    return (
        middle_grad,
        half(rms_back(normed, inverse, branch * first_gain)),
        middle_grad * (normed * first_gain) * (1.0 - turned * turned),
        scale_grad,
        branch * normed,
        second_row,
    )


def enter_back_point(input_grad, source, scale, middle_grad, gain):
    normed, inverse = rms_parts(source)
    gained = input_grad * (1.0 + scale)
    return (
        middle_grad + rms_back(normed, inverse, gained * gain),
        input_grad * normed * gain,
        gained * normed,
    )


def spans(heads):
    return [slice(head * HEAD, (head + 1) * HEAD) for head in range(heads)]


def head_norm(value):
    inverse = lax.rsqrt(jnp.mean(value * value, axis=0, keepdims=True) + EPS)
    return (value * inverse, inverse)


def head_back(normed, inverse, grad):
    return inverse * (grad - normed * jnp.mean(grad * normed, axis=0, keepdims=True))


def turn(value, cosine, sine):
    middle = HEAD // 2
    first, second = value[:middle], value[middle:]
    return jnp.concatenate(
        [first * cosine - second * sine, second * cosine + first * sine], axis=0
    )


def self_bias(step, ids_row, ids_column):
    start = pl.multiple_of(step * TILE, TILE)
    return jnp.where(ids_column[pl.ds(start, TILE), :] == ids_row[...], 0.0, NEG)


def cross_bias(step, ids_row, lengths):
    slots = lax.broadcasted_iota(jnp.int32, (TILE, 1), 0) < lengths[step]
    return jnp.where(slots & (ids_row[...] == step), 0.0, NEG)


def attend_tile(heads, meta, bias_of, query, key_rows, value, out, total, inv_ref):
    base = 2 * pl.program_id(0)
    factor = HEAD ** (-0.5) * LOG2E
    out[...] = jnp.zeros_like(out)
    total[...] = jnp.zeros_like(total)

    def step(index, carry):
        bias = bias_of(index)
        rows = pl.ds(pl.multiple_of(index * TILE, TILE), TILE)
        scores = [
            dot(key_rows[head, rows, :], query[span, :], 1, 0)
            for head, span in enumerate(spans(heads))
        ]
        for head, span in enumerate(spans(heads)):
            expo = jnp.exp2(scores[head] * factor + bias)
            total[head] += jnp.sum(expo.reshape(TILE // 8, 8, TILE), axis=0)
            out[span, :] += dot(value[span, rows], half(expo), 1, 0)
        return carry

    lax.fori_loop(meta[base], meta[base + 1], step, 0)
    for head, span in enumerate(spans(heads)):
        inverse = 1.0 / jnp.sum(total[head], axis=0, keepdims=True)
        inv_ref[head] = jnp.broadcast_to(inverse, (8, TILE))
        out[span, :] = out[span, :] * inverse


def attend_back_tile(
    heads, meta, bias_of, query, key_rows, key, value_rows, inv_ref, out, back, dq, dk, dv, centre
):
    base = 2 * pl.program_id(0)
    scale = HEAD ** (-0.5)
    dq[...] = jnp.zeros_like(dq)
    for head, span in enumerate(spans(heads)):
        both = out[span, :] * back[span, :].astype(jnp.float32)
        centre[head] = jnp.broadcast_to(jnp.sum(both, axis=0, keepdims=True), (8, TILE))

    def step(index, carry):
        bias = bias_of(index)
        rows = pl.ds(pl.multiple_of(index * TILE, TILE), TILE)
        def products(head):
            span = spans(heads)[head]
            return (
                dot(key_rows[head, rows, :], query[span, :], 1, 0),
                dot(value_rows[head, rows, :], back[span, :], 1, 0),
            )

        ahead = [products(head) for head in range(min(AHEAD, heads))]
        for head, span in enumerate(spans(heads)):
            scores, prob_grad = ahead.pop(0)
            if head + AHEAD < heads:
                ahead.append(products(head + AHEAD))
            probs = jnp.exp2(scores * (scale * LOG2E) + bias)
            probs = probs * inv_ref[head, 0:1, :]
            score_grad = half(probs * (prob_grad - centre[head, 0:1, :]))
            dv[span, rows] += dot(back[span, :], half(probs), 1, 1)
            dk[span, rows] += dot(query[span, :], score_grad, 1, 1) * scale
            dq[span, :] += dot(key[span, rows], score_grad, 1, 0) * scale
        return carry

    lax.fori_loop(meta[base], meta[base + 1], step, 0)


def self_forward_kernel(
    heads,
    meta,
    ids_row,
    ids_column,
    gain,
    cosine,
    sine,
    cosine_all,
    sine_all,
    raw_query,
    raw_key,
    raw_value,
    query,
    key,
    key_rows,
    value_rows,
    out,
    inv_ref,
    value,
    total,
):
    local = heads * HEAD

    @pl.when(pl.program_id(0) == 0)
    def _():
        for head, span in enumerate(spans(heads)):
            normed, _ = head_norm(raw_key[span, :])
            turned = turn(normed * gain[span, 1:2], cosine_all[...], sine_all[...])
            key[span, :] = half(turned)
            key_rows[head] = half(turned.T)
            plain = raw_value[span, :]
            value[span, :] = half(plain)
            value_rows[head] = half(plain.T)

    for span in spans(heads):
        normed, _ = head_norm(raw_query[span, :])
        query[span, :] = half(turn(normed * gain[span, 0:1], cosine[...], sine[...]))
    attend_tile(
        heads,
        meta,
        lambda index: self_bias(index, ids_row, ids_column),
        query,
        key_rows,
        value,
        out,
        total,
        inv_ref,
    )


def cross_forward_kernel(
    heads,
    meta,
    lengths,
    ids_row,
    gain,
    query,
    own_out,
    raw_key,
    raw_value,
    key,
    key_rows,
    value_rows,
    out,
    inv_ref,
    mixed,
    value,
    total,
):
    @pl.when(pl.program_id(0) == 0)
    def _():
        for head, span in enumerate(spans(heads)):
            normed, _ = head_norm(raw_key[span, :])
            normed = normed * gain[span, 2:3]
            key[span, :] = half(normed)
            key_rows[head] = half(normed.T)
            plain = raw_value[span, :]
            value[span, :] = half(plain)
            value_rows[head] = half(plain.T)

    attend_tile(
        heads,
        meta,
        lambda index: cross_bias(index, ids_row, lengths),
        query,
        key_rows,
        value,
        out,
        total,
        inv_ref,
    )
    mixed[...] = half(own_out[...] + jnp.tanh(gain[:, 3:4]) * out[...])


def cross_backward_kernel(
    heads,
    meta,
    lengths,
    ids_row,
    gain,
    query,
    key_rows,
    key,
    value_rows,
    inv_ref,
    out,
    mixed_grad,
    raw_key,
    dq,
    dk,
    dv,
    gain_grad,
    back,
    centre,
    dk_sum,
    dv_sum,
    gate_sum,
):
    place = pl.program_id(0)

    @pl.when(place == 0)
    def _():
        dk_sum[...] = jnp.zeros_like(dk_sum)
        dv_sum[...] = jnp.zeros_like(dv_sum)
        gate_sum[...] = jnp.zeros_like(gate_sum)

    gate = jnp.tanh(gain[:, 3:4])
    back[...] = half(gate * mixed_grad[...])
    gate_sum[...] += mixed_grad[...] * out[...]
    attend_back_tile(
        heads,
        meta,
        lambda index: cross_bias(index, ids_row, lengths),
        query,
        key_rows,
        key,
        value_rows,
        inv_ref,
        out,
        back,
        dq,
        dk_sum,
        dv_sum,
        centre,
    )

    @pl.when(place == pl.num_programs(0) - 1)
    def _():
        dv[...] = half(dv_sum[...])
        gate_grad = jnp.sum(gate_sum[...], axis=1, keepdims=True) * (1.0 - gate * gate)
        gain_grad[:, 0:128] = jnp.broadcast_to(gate_grad, (heads * HEAD, 128))
        for span in spans(heads):
            normed, inverse = head_norm(raw_key[span, :])
            grad = dk_sum[span, :]
            summed = jnp.sum(grad * normed, axis=1, keepdims=True)
            gain_grad[span, 128:256] = jnp.broadcast_to(summed, (HEAD, 128))
            dk[span, :] = half(head_back(normed, inverse, grad * gain[span, 2:3]))


def self_backward_kernel(
    heads,
    meta,
    ids_row,
    ids_column,
    gain,
    cosine,
    sine,
    cosine_all,
    sine_all,
    query,
    key_rows,
    key,
    value_rows,
    inv_ref,
    out,
    mixed_grad,
    other_dq,
    raw_query,
    raw_key,
    triple,
    gain_grad,
    back,
    centre,
    dq,
    dk_sum,
    dv_sum,
    query_sum,
):
    place = pl.program_id(0)
    local = heads * HEAD

    @pl.when(place == 0)
    def _():
        dk_sum[...] = jnp.zeros_like(dk_sum)
        dv_sum[...] = jnp.zeros_like(dv_sum)
        query_sum[...] = jnp.zeros_like(query_sum)

    back[...] = half(mixed_grad[...])
    attend_back_tile(
        heads,
        meta,
        lambda index: self_bias(index, ids_row, ids_column),
        query,
        key_rows,
        key,
        value_rows,
        inv_ref,
        out,
        back,
        dq,
        dk_sum,
        dv_sum,
        centre,
    )
    columns = pl.ds(pl.multiple_of(place * TILE, TILE), TILE)
    for span in spans(heads):
        normed, inverse = head_norm(raw_query[span, :])
        grad = turn(dq[span, :] + other_dq[span, :], cosine[...], -sine[...])
        query_sum[span, :] += grad * normed
        triple[span, columns] = half(head_back(normed, inverse, grad * gain[span, 0:1]))

    @pl.when(place == pl.num_programs(0) - 1)
    def _():
        summed = jnp.sum(query_sum[...], axis=1, keepdims=True)
        gain_grad[:, 0:128] = jnp.broadcast_to(summed, (local, 128))
        triple[2 * local :, :] = half(dv_sum[...])
        for head, span in enumerate(spans(heads)):
            normed, inverse = head_norm(raw_key[span, :])
            grad = turn(dk_sum[span, :], cosine_all[...], -sine_all[...])
            summed = jnp.sum(grad * normed, axis=1, keepdims=True)
            gain_grad[span, 128:256] = jnp.broadcast_to(summed, (HEAD, 128))
            triple[local + head * HEAD : local + (head + 1) * HEAD, :] = half(
                head_back(normed, inverse, grad * gain[span, 1:2])
            )


def attention_call(kernel, name, scalars, operands, outs, scratch, tokens, weight, after=()):
    def block(array, tiled):
        lead = array.shape[:-1]
        if tiled is not True and tiled is not False:
            third = (lead[0] // 3, tokens if tiled else TILE)
            return pl.BlockSpec(third, lambda i, *_: (tiled, 0) if tiled else (0, i))
        if tiled:
            return pl.BlockSpec((*lead, TILE), lambda i, *_: (*([0] * len(lead)), i))
        return pl.BlockSpec(array.shape, lambda i, *_: (0,) * len(array.shape))

    count = len(scalars) + len(operands)

    def run(*refs):
        kernel(*refs[:count], *refs[count + len(after) :])

    return pl.pallas_call(
        run,
        grid_spec=pltpu.PrefetchScalarGridSpec(
            num_scalar_prefetch=len(scalars),
            grid=(tokens // TILE,),
            in_specs=[block(*operand) for operand in operands]
            + [pl.BlockSpec(memory_space=pl.ANY)] * len(after),
            out_specs=[block(*out) for out in outs],
            scratch_shapes=scratch,
        ),
        out_shape=[out for out, _ in outs],
        compiler_params=pltpu.CompilerParams(
            vmem_limit_bytes=58 * 1024 * 1024, dimension_semantics=("arbitrary",)
        ),
        cost_estimate=pl.CostEstimate(
            flops=weight, bytes_accessed=weight, transcendentals=0
        ),
        name=name,
    )(*scalars, *(operand for operand, _ in operands), *after)


def adamw(grad, weight, moment, square, decay, rate):
    moment_new = BETA1 * moment + (1.0 - BETA1) * grad
    square_new = BETA2 * square + (1.0 - BETA2) * grad * grad
    step_size = (
        moment_new / (1.0 - BETA1**STEP) / (jnp.sqrt(square_new / (1.0 - BETA2**STEP)) + ADAM_EPS)
    )
    return (moment_new, square_new, weight - rate * (step_size + decay * weight))


def body(
    latents,
    cotangent,
    captions,
    conditions,
    image_ids,
    rope_rows,
    rope_cols,
    caption_lengths,
    attention_in,
    attention_out,
    feed_in,
    feed_out,
    caption_in,
    modulator,
    channels,
    moment_attention_in,
    square_attention_in,
    moment_attention_out,
    square_attention_out,
    moment_feed_in,
    square_feed_in,
    moment_feed_out,
    square_feed_out,
    moment_caption_in,
    square_caption_in,
    moment_modulator,
    square_modulator,
    moment_channels,
    square_channels,
):
    tensor_size = lax.axis_size("tensor")
    tensor_index = lax.axis_index("tensor")
    dp_size = lax.axis_size("dp")
    dp_index = lax.axis_index("dp")
    shard_rows, width = latents.shape
    local = attention_in.shape[2]
    heads = local // HEAD
    units = feed_in.shape[2]
    segment = image_ids[0]
    row_tokens = segment.shape[0]
    images = conditions.shape[0]
    per_row = caption_lengths.shape[1]
    lengths = caption_lengths[0]
    slots = captions.shape[0]
    offset = tensor_index * local
    own_ids = lax.dynamic_slice_in_dim(segment, tensor_index * shard_rows, shard_rows)

    rows = attention_in.shape[1]
    fused = tensor_size == 4
    caption_half = half(caption_in)
    key_line = gather_far(caption_half[0].T)
    value_line = gather_far(
        jnp.concatenate([caption_half[1].T, half(attention_out).T], axis=1)
    )
    in_half = half(attention_in)
    attention_line = gather_far(jnp.concatenate([in_half[0], in_half[1], in_half[2]], axis=1))
    down_line = gather_far(half(feed_out).T)
    feed_half = half(feed_in)
    feed_own = jnp.concatenate([feed_half[0], feed_half[1]], axis=1)

    augmented = half(
        jnp.concatenate([jax.nn.silu(conditions), jnp.ones((images, 1), jnp.float32)], axis=1)
    )
    factor_part = jnp.dot(augmented, half(modulator), preferred_element_type=jnp.float32)
    own_columns = factor_part.shape[1]
    payload = jnp.concatenate(
        [
            factor_part.reshape(dp_size, per_row, own_columns),
            jnp.broadcast_to(
                lax.reduce_precision(channels, 8, 7).reshape(-1, own_columns),
                (dp_size, channels.size // own_columns, own_columns),
            ),
        ],
        axis=1,
    )
    received, feed_other = remote_call(
        spread_kernel,
        "modulation_exchange",
        0,
        [payload],
        [jax.ShapeDtypeStruct((tensor_size, *payload.shape), jnp.float32)],
        exchange_scratch([payload.shape]),
        [feed_own],
        everyone=True,
    )
    feed_full = gather_far(join_near(feed_own, feed_other, rows))
    factor_row = jnp.transpose(received[:, :, :per_row], (2, 1, 0, 3)).reshape(per_row, -1)
    gains = received[0, :, per_row:].reshape(dp_size, 8, -1)
    gains = jnp.transpose(gains, (1, 0, 2)).reshape(8, width)
    local_gains = lax.dynamic_slice_in_dim(gains[4:], offset, local, 1).T
    chooser = (own_ids[:, None] == jnp.arange(per_row, dtype=jnp.int32)[None, :]).astype(
        jnp.float32
    )
    choose = jnp.transpose(chooser.reshape(CHUNKS, -1, per_row), (0, 2, 1))

    def token_factor(which):
        return pick(chooser, factor_row, which, slice(None))

    def split(value):
        return [value[i * shard_rows : (i + 1) * shard_rows] for i in range(tensor_size)]

    def by_image(*grads):
        return jnp.stack([jnp.dot(chooser.T, grad, precision=HIGH) for grad in grads])

    f32, bf16 = jnp.float32, jnp.bfloat16

    def shape(dims, dtype=f32):
        return jax.ShapeDtypeStruct(dims, dtype)

    gathered = shape((tensor_size, shard_rows, width), bf16)
    in_kernel = sum_scratch(shard_rows, width)

    def semaphores(count):
        return pltpu.SemaphoreType.DMA((2, count))

    sum_sems, all_sems = semaphores(SUM_SEMAPHORES), semaphores(SUM_SEMAPHORES + 3 * CHUNKS)
    source = latents.astype(f32)

    def caption_project(weight, carry, number):
        if fused:
            return remote_call(
                project_kernel,
                "project",
                number,
                [weight, captions],
                [shape((local, slots))],
                [*sum_scratch(local, slots), sum_sems],
                carry,
            )
        total = collect(
            [
                dot(
                    lax.dynamic_slice_in_dim(weight, owner(i) * local, local), captions, 1, 1
                )
                for i in range(tensor_size)
            ]
        )
        return (total, *(near_swap(array) for array in carry))

    if fused:
        attn_full, key_other = remote_call(
            enter_kernel,
            "enter",
            3,
            [latents, factor_row, chooser, gains],
            [gathered],
            [semaphores(3 * CHUNKS)],
            [key_line],
        )
        attn_full = attn_full.reshape(row_tokens, width)
    else:
        attn_full = in_place(spread(enter_point(source, token_factor(0), gains[0])))
        key_other = near_swap(key_line)
    text_key_raw, value_other = caption_project(
        join_near(key_line, key_other, rows), [value_line], 4
    )
    features = captions.shape[1]
    value_full, out_full = (
        join_near(value_line[:, part], value_other[:, part], rows)
        for part in (slice(0, features), slice(features, None))
    )
    text_value_raw, attention_other = caption_project(value_full, [attention_line], 11)
    in_full = join_near(attention_line, attention_other, rows)
    projected = dot(in_full, attn_full, 0, 1)
    cosine, sine = rope_tables(rope_rows[0], rope_cols[0])

    tiles = row_tokens // TILE
    first_id = segment.reshape(tiles, TILE)[:, 0]
    last_id = segment.reshape(tiles, TILE)[:, TILE - 1]
    low = jnp.sum((segment[None] < first_id[:, None]).astype(jnp.int32), axis=1) // TILE
    high = (
        jnp.sum((segment[None] <= last_id[:, None]).astype(jnp.int32), axis=1) + TILE - 1
    ) // TILE
    self_meta = jnp.stack([low, high], axis=1).reshape(-1)
    cross_meta = jnp.stack([first_id, last_id + 1], axis=1).reshape(-1)
    ids_row = image_ids
    ids_column = segment[:, None]
    wide = jax.ShapeDtypeStruct((local, row_tokens), jnp.float32)
    narrow = jax.ShapeDtypeStruct((local, row_tokens), jnp.bfloat16)
    sums = jax.ShapeDtypeStruct((heads, 8, row_tokens), jnp.float32)
    by_rows = jax.ShapeDtypeStruct((heads, row_tokens, HEAD), jnp.bfloat16)
    text_narrow = jax.ShapeDtypeStruct((local, slots), jnp.bfloat16)
    text_rows = jax.ShapeDtypeStruct((heads, slots, HEAD), jnp.bfloat16)
    gain_shape = jax.ShapeDtypeStruct((local, 256), jnp.float32)
    tile_sums = pltpu.VMEM((heads, 8, TILE), jnp.float32)
    tables = [(cosine, True), (sine, True), (cosine, False), (sine, False)]
    queries, keys, key_rows, value_rows, own_out, own_inv = attention_call(
        functools.partial(self_forward_kernel, heads),
        "self_forward",
        [self_meta],
        [
            (ids_row, True),
            (ids_column, False),
            (local_gains, False),
            *tables,
            (projected, 0),
            (projected, 1),
            (projected, 2),
        ],
        [
            (narrow, True),
            (narrow, False),
            (by_rows, False),
            (by_rows, False),
            (wide, True),
            (sums, True),
        ],
        [pltpu.VMEM((local, row_tokens), jnp.bfloat16), tile_sums],
        row_tokens,
        15000,
    )
    text_keys, text_key_rows, text_value_rows, other_out, other_inv, mixed = attention_call(
        functools.partial(cross_forward_kernel, heads),
        "cross_forward",
        [cross_meta, lengths],
        [
            (ids_row, True),
            (local_gains, False),
            (queries, True),
            (own_out, True),
            (text_key_raw, False),
            (text_value_raw, False),
        ],
        [
            (text_narrow, False),
            (text_rows, False),
            (text_rows, False),
            (wide, True),
            (sums, True),
            (narrow, True),
        ],
        [pltpu.VMEM((local, slots), jnp.bfloat16), tile_sums],
        row_tokens,
        18000,
    )
    norm_gains = gains
    if fused:
        attn_sum, middle, feed_all, down_other = remote_call(
            attention_out_kernel,
            "attention_out",
            5,
            [mixed, out_full, latents, factor_row, chooser, norm_gains],
            [shape((shard_rows, width)), shape((shard_rows, width)), gathered],
            [pltpu.VMEM((2 * shard_rows, local), bf16), *in_kernel, all_sems],
            [down_line],
        )
        feed_all = feed_all.reshape(row_tokens, width)
        down_full = join_near(down_line, down_other, rows)
        gate_up, hidden, block_out, end_factor, end_row, feed_sum_grad = remote_call(
            feed_kernel,
            "feed_forward",
            6,
            [
                feed_all,
                feed_full,
                down_full,
                middle,
                factor_row,
                chooser,
                choose,
                cotangent,
                norm_gains,
            ],
            [
                shape((row_tokens, 2 * units)),
                shape((row_tokens, units), bf16),
                shape((shard_rows, width)),
                shape((1, per_row, width)),
                shape((1, 8, width)),
                gathered,
            ],
            [*in_kernel, all_sems],
        )
        feed_sum_grad = feed_sum_grad.reshape(row_tokens, width)
    else:
        attn_sum = collect(
            [
                dot(
                    lax.dynamic_slice_in_dim(mixed, owner(i) * shard_rows, shard_rows, 1),
                    out_full,
                    0,
                    1,
                )
                for i in range(tensor_size)
            ]
        )
        middle, feed_block = middle_point(
            attn_sum, source, token_factor(1), token_factor(2), gains[1], gains[2]
        )
        feed_all = in_place(spread(feed_block))
        down_full = join_near(down_line, near_swap(down_line), rows)
        gate_up = dot(feed_all, feed_full, 1, 0)
        hidden = half(jax.nn.silu(gate_up[:, :units]) * gate_up[:, units:])
        feed_sum = collect(split(dot(hidden, down_full, 1, 1)))
        block_out, feed_block_grad, *grads = end_point(
            feed_sum, middle, token_factor(3), cotangent, gains[3]
        )
        end_factor, end_row = by_image(grads[0]), grads[1][None]
        feed_sum_grad = in_place(spread(feed_block_grad))
    feed_out_grad = half(dot(feed_sum_grad, hidden, 0, 0))
    feed_out_parts = feed_out_grad.reshape(dp_size // 2, 2, -1, units)
    if fused:
        (
            pair_grad,
            middle_grad,
            middle_factor,
            middle_row,
            attn_sum_grad,
            feed_out_other,
        ) = remote_call(
            feed_back_kernel,
            "feed_backward",
            7,
            [
                feed_sum_grad,
                gate_up,
                feed_full,
                down_full,
                attn_sum,
                middle,
                factor_row,
                chooser,
                choose,
                cotangent,
                norm_gains,
            ],
            [
                shape((row_tokens, 2 * units), bf16),
                shape((shard_rows, width)),
                shape((2, per_row, width)),
                shape((2, 8, width)),
                gathered,
            ],
            [*in_kernel, all_sems],
            [feed_out_parts],
        )
        attn_sum_grad = attn_sum_grad.reshape(row_tokens, width)
    else:
        hidden_grad = dot(feed_sum_grad, down_full, 1, 0)
        pair_grad = jnp.concatenate(
            pair_point(hidden_grad, gate_up[:, :units], gate_up[:, units:]), axis=1
        )
        feed_input_grad = collect(split(dot(pair_grad, feed_full, 1, 1)))
        middle_grad, attn_block_grad, *grads = middle_back_point(
            feed_input_grad,
            attn_sum,
            middle,
            token_factor(1),
            token_factor(2),
            cotangent,
            gains[1],
            gains[2],
        )
        middle_factor, middle_row = by_image(*grads[:2]), jnp.stack(grads[2:])
        attn_sum_grad = in_place(spread(attn_block_grad))
        feed_out_other = swap_half(feed_out_parts)
    feed_out_sum = scatter_far(sum_half(feed_out_parts, feed_out_other))
    outer_grad = half(dot(feed_all, pair_grad, 0, 0))
    outer_both = lax.psum_scatter(
        outer_grad, "dp", scatter_dimension=0, tiled=True, axis_index_groups=far_groups()
    )
    mixed_grad = dot(out_full, gate(attn_sum_grad, outer_grad), 0, 1)
    out_parts = half(dot(attn_sum_grad, mixed, 0, 1)).reshape(dp_size // 2, 2, -1, local)
    query_two, text_key_grad, text_value_grad, text_gains = attention_call(
        functools.partial(cross_backward_kernel, heads),
        "cross_backward",
        [cross_meta, lengths],
        [
            (ids_row, True),
            (local_gains, False),
            (queries, True),
            (text_key_rows, False),
            (text_keys, False),
            (text_value_rows, False),
            (other_inv, True),
            (other_out, True),
            (mixed_grad, True),
            (text_key_raw, False),
        ],
        [(wide, True), (text_narrow, False), (text_narrow, False), (gain_shape, False)],
        [
            pltpu.VMEM((local, TILE), jnp.bfloat16),
            tile_sums,
            pltpu.VMEM((local, slots), jnp.float32),
            pltpu.VMEM((local, slots), jnp.float32),
            pltpu.VMEM((local, TILE), jnp.float32),
        ],
        row_tokens,
        25000,
    )
    triple_grad, own_gains = attention_call(
        functools.partial(self_backward_kernel, heads),
        "self_backward",
        [self_meta],
        [
            (ids_row, True),
            (ids_column, False),
            (local_gains, False),
            *tables,
            (queries, True),
            (key_rows, False),
            (keys, False),
            (value_rows, False),
            (own_inv, True),
            (own_out, True),
            (mixed_grad, True),
            (query_two, True),
            (projected, 0),
            (projected, 1),
        ],
        [
            (jax.ShapeDtypeStruct((3 * local, row_tokens), jnp.bfloat16), False),
            (gain_shape, False),
        ],
        [
            pltpu.VMEM((local, TILE), jnp.bfloat16),
            tile_sums,
            pltpu.VMEM((local, TILE), jnp.float32),
            pltpu.VMEM((local, row_tokens), jnp.float32),
            pltpu.VMEM((local, row_tokens), jnp.float32),
            pltpu.VMEM((local, TILE), jnp.float32),
        ],
        row_tokens,
        25000,
        [feed_out_sum],
    )
    in_parts = half(dot(attn_full, triple_grad, 0, 1)).reshape(dp_size // 2, 2, -1, 3 * local)

    if fused:
        latent_grad, enter_factor, enter_row, in_other = remote_call(
            enter_back_kernel,
            "enter_backward",
            10,
            [
                triple_grad,
                in_full,
                latents,
                factor_row,
                chooser,
                choose,
                middle_grad,
                norm_gains,
            ],
            [
                shape((shard_rows, width)),
                shape((1, per_row, width)),
                shape((1, 8, width)),
            ],
            [pltpu.VMEM((2 * shard_rows, 3 * local), bf16), *in_kernel, sum_sems],
            [in_parts],
        )
    else:
        attn_input_grad = collect(
            [
                dot(
                    lax.dynamic_slice_in_dim(triple_grad, owner(i) * shard_rows, shard_rows, 1),
                    in_full,
                    0,
                    1,
                )
                for i in range(tensor_size)
            ]
        )
        in_other = swap_half(in_parts)
        latent_grad, *grads = enter_back_point(
            attn_input_grad, source, token_factor(0), middle_grad, gains[0]
        )
        enter_factor, enter_row = by_image(grads[0]), grads[1][None]
    in_sum = scatter_far(sum_half(in_parts, in_other))

    columns = captions.shape[1]

    def caption_back(grad, carry, number, after):
        if not fused:
            parts = half(dot(in_place(spread(grad)), captions, 1, 0))
            parts = parts.reshape(dp_size // 2, 2, -1, columns)
            return (sum_half(parts, swap_half(parts)), *(swap_half(array) for array in carry))
        kept = (tensor_size, local // 2, columns)
        summed, _, *others = remote_call(
            text_kernel,
            "text_gradient",
            number,
            [grad, captions],
            [shape(kept, bf16), shape((tensor_size, local, slots), bf16)],
            [
                pltpu.VMEM(kept, f32),
                pltpu.VMEM(kept, bf16),
                pltpu.VMEM(kept, bf16),
                semaphores(5 * CHUNKS),
            ],
            carry,
            neighbour=True,
            after=after,
        )
        return (flat(summed), *others)

    value_grad, out_other = caption_back(text_value_grad, [out_parts], 8, [latent_grad])
    value_sum = scatter_far(
        jnp.concatenate([value_grad, sum_half(out_parts, out_other)], axis=1)
    )
    (key_grad,) = caption_back(text_key_grad, [], 9, [outer_both, value_grad])
    key_sum = scatter_far(key_grad)
    shared_rows = jnp.sum(
        jnp.concatenate([enter_row, middle_row, end_row]), axis=1
    )
    head_rows = jnp.stack(
        [own_gains[:, 0], own_gains[:, 128], text_gains[:, 128], text_gains[:, 0]]
    )
    head_full = lax.dynamic_update_slice(
        jnp.zeros((4, width), jnp.float32), head_rows, (jnp.zeros((), jnp.int32), offset)
    )
    channel_part = jnp.concatenate([shared_rows, head_full], axis=0)
    factor_image = jnp.concatenate([enter_factor, middle_factor, end_factor])
    factor_image = jnp.transpose(factor_image, (1, 0, 2))
    factor_image = jnp.transpose(
        factor_image.reshape(per_row, dp_size, tensor_size, own_columns), (2, 1, 0, 3)
    )
    channel_blocks = jnp.transpose(channel_part.reshape(8, dp_size, -1), (1, 0, 2))
    channel_blocks = channel_blocks.reshape(dp_size, -1, own_columns)
    payload = jnp.concatenate(
        [factor_image, jnp.broadcast_to(channel_blocks, (tensor_size, *channel_blocks.shape))],
        axis=2,
    )
    blocks = payload.shape[1:]
    outer_parts = outer_both.reshape(1, 2, -1, outer_both.shape[1])
    received, outer_other = remote_call(
        return_kernel,
        "modulation_return",
        1,
        [payload],
        [shape(blocks)],
        exchange_scratch([payload.shape, blocks, blocks]),
        [outer_parts],
        everyone=True,
        after=[in_sum],
    )
    in_sum, value_sum = gate(in_sum, received), gate(value_sum, received)
    feed_out_sum = gate(feed_out_sum, received)
    value_sum, out_sum = value_sum[:, :columns], value_sum[:, columns:]
    feed_in_sum = lax.dynamic_index_in_dim(outer_parts, dp_index % 2, 1, keepdims=False)[0]
    feed_in_sum = feed_in_sum.astype(f32) + outer_other[0].astype(f32)
    factor_grad = received[:, :per_row].reshape(images, own_columns)
    channel_sum = jnp.sum(received[:, per_row:], axis=0).reshape(channels.shape)
    modulator_sum = jnp.dot(augmented.astype(jnp.float32).T, factor_grad, precision=HIGH)

    def square(value):
        value = value.astype(f32)
        return jnp.sum(value * value)

    squares = (
        square(in_sum)
        + square(out_sum)
        + square(feed_in_sum)
        + square(feed_out_sum)
        + square(key_sum)
        + square(value_sum)
        + square(modulator_sum)
        + square(channel_sum) / tensor_size
    )
    in_sum = jnp.stack([in_sum[:, i * local : (i + 1) * local] for i in range(3)])
    feed_in_sum = jnp.stack([feed_in_sum[:, i * units : (i + 1) * units] for i in range(2)])
    caption_sum = jnp.stack([key_sum.T, value_sum.T])
    (squares,) = remote_call(
        total_kernel,
        "norm_exchange",
        2,
        [jnp.broadcast_to(squares, (8, 128))],
        [shape((8, 128))],
        exchange_scratch([(tensor_size, 8, 128), (dp_size, 8, 128), (8, 128)]),
        everyone=True,
    )
    grad_norm = jnp.sqrt(squares[0, 0])
    factor = CLIP / jnp.maximum(grad_norm, CLIP)
    results = [
        adamw(grad.astype(f32) * factor, weight, moment, second, DECAY, RATE)
        for grad, weight, moment, second in (
            (in_sum, attention_in, moment_attention_in, square_attention_in),
            (out_sum.T, attention_out, moment_attention_out, square_attention_out),
            (feed_in_sum, feed_in, moment_feed_in, square_feed_in),
            (feed_out_sum.T, feed_out, moment_feed_out, square_feed_out),
            (caption_sum, caption_in, moment_caption_in, square_caption_in),
            (modulator_sum, modulator, moment_modulator, square_modulator),
        )
    ]
    results.append(
        adamw(channel_sum * factor, channels, moment_channels, square_channels, 0.0, GAIN_RATE)
    )
    return (block_out, latent_grad, grad_norm, *(part for result in results for part in result))


def solution(mesh):
    return jax.shard_map(
        body,
        mesh=mesh,
        in_specs=(
            P(("dp", "tensor"), None),
            P(("dp", "tensor"), None),
            P("dp", "tensor"),
            P(),
            P("dp", None),
            P("dp", None),
            P("dp", None),
            P("dp", None),
            P(None, "dp", "tensor"),
            P("tensor", "dp"),
            P(None, "dp", "tensor"),
            P("tensor", "dp"),
            P(None, "tensor", "dp"),
            P(None, ("dp", "tensor")),
            P(None, "dp"),
            P(None, "dp", "tensor"),
            P(None, "dp", "tensor"),
            P("tensor", "dp"),
            P("tensor", "dp"),
            P(None, "dp", "tensor"),
            P(None, "dp", "tensor"),
            P("tensor", "dp"),
            P("tensor", "dp"),
            P(None, "tensor", "dp"),
            P(None, "tensor", "dp"),
            P(None, ("dp", "tensor")),
            P(None, ("dp", "tensor")),
            P(None, "dp"),
            P(None, "dp"),
        ),
        out_specs=(
            P(("dp", "tensor"), None),
            P(("dp", "tensor"), None),
            P(),
            P(None, "dp", "tensor"),
            P(None, "dp", "tensor"),
            P(None, "dp", "tensor"),
            P("tensor", "dp"),
            P("tensor", "dp"),
            P("tensor", "dp"),
            P(None, "dp", "tensor"),
            P(None, "dp", "tensor"),
            P(None, "dp", "tensor"),
            P("tensor", "dp"),
            P("tensor", "dp"),
            P("tensor", "dp"),
            P(None, "tensor", "dp"),
            P(None, "tensor", "dp"),
            P(None, "tensor", "dp"),
            P(None, ("dp", "tensor")),
            P(None, ("dp", "tensor")),
            P(None, ("dp", "tensor")),
            P(None, "dp"),
            P(None, "dp"),
            P(None, "dp"),
        ),
        check_vma=False,
    )
```

```python
import functools
import math

import jax
import jax.numpy as jnp
from jax import lax
from jax.experimental import pallas as pl
from jax.experimental.pallas import tpu as pltpu
from jax.sharding import PartitionSpec as P

HEAD = 64
CAP = 256
STEP = 10


EPS = 1e-06
NEG = -1e30
THETA = 10000.0
BETA1 = 0.9
BETA2 = 0.95
RATE = 0.05
GAIN_RATE = 0.8
DECAY = 0.1
ADAM_EPS = 1e-08
CLIP = 1.0
HIGH = lax.Precision.HIGHEST


def half(value):
    return value.astype(jnp.bfloat16)


TILE = 256
AHEAD = 2
LOG2E = 1.0 / math.log(2.0)
MESH = pl.DeviceIdType.MESH


def dot(left, right, left_dim, right_dim):
    return lax.dot_general(
        left, right, (((left_dim,), (right_dim,)), ((), ())), preferred_element_type=jnp.float32
    )


def rms_parts(value, axis=-1):
    inverse = lax.rsqrt(jnp.mean(value * value, axis=axis, keepdims=True) + EPS)
    return (value * inverse, inverse)


def rms_back(normed, inverse, grad, axis=-1):
    return inverse * (grad - normed * jnp.mean(grad * normed, axis=axis, keepdims=True))


def rope_tables(rows, columns):
    quarter = HEAD // 4
    frequency = THETA ** (-jnp.arange(quarter, dtype=jnp.float32) / quarter)
    angles = jnp.concatenate(
        [
            frequency[:, None] * rows.astype(jnp.float32)[None, :],
            frequency[:, None] * columns.astype(jnp.float32)[None, :],
        ],
        axis=0,
    )
    return (jnp.cos(angles), jnp.sin(angles))


def gate_kernel(value, after, out):
    del value, after, out


def gate(value, after):
    anywhere = pl.BlockSpec(memory_space=pl.ANY)
    return pl.pallas_call(
        gate_kernel,
        out_shape=jax.ShapeDtypeStruct(value.shape, value.dtype),
        in_specs=[anywhere, anywhere],
        out_specs=anywhere,
        input_output_aliases={0: 0},
        name="gate",
    )(value, after)


def near_swap(value):
    return lax.ppermute(value, "dp", [(i, i ^ 1) for i in range(lax.axis_size("dp"))])


def far_groups():
    count = lax.axis_size("dp")
    return [list(range(near, count, 2)) for near in range(2)]


def gather_far(value):
    return lax.all_gather(value, "dp", axis=0, tiled=True, axis_index_groups=far_groups())


def flat(blocks):
    return blocks.reshape(-1, blocks.shape[-1])


def join_near(own, other, count):
    odd = lax.axis_index("dp") % 2
    own = own.reshape(-1, count, own.shape[1])
    other = other.reshape(own.shape)
    return flat(
        jnp.stack([jnp.where(odd == 0, own, other), jnp.where(odd == 0, other, own)], axis=1)
    )


def swap_half(parts):
    odd = lax.axis_index("dp") % 2
    send = lax.dynamic_index_in_dim(parts, 1 - odd, 1, keepdims=False)
    return near_swap(send.reshape(-1, send.shape[2])).reshape(send.shape)


def sum_half(parts, other):
    odd = lax.axis_index("dp") % 2
    keep = lax.dynamic_index_in_dim(parts, odd, 1, keepdims=False)
    return flat(half(keep.astype(jnp.float32) + other.astype(jnp.float32)))


def scatter_far(value):
    return lax.psum_scatter(
        value, "dp", scatter_dimension=0, tiled=True, axis_index_groups=far_groups()
    )


def swap_tensor(value, bits):
    return lax.ppermute(value, "tensor", [(i, i ^ bits) for i in range(lax.axis_size("tensor"))])


def owner(place):
    if lax.axis_size("tensor") == 4:
        return lax.axis_index("tensor") ^ place
    return jnp.int32(place)


def spread(value):
    count = lax.axis_size("tensor")
    if count == 4:
        near = swap_tensor(value, 1)
        far = swap_tensor(value, 2)
        return [value, near, far, swap_tensor(far, 1)]
    whole = lax.all_gather(value, "tensor", axis=0, tiled=False)
    return [whole[i] for i in range(count)]


def collect_near(parts):
    if len(parts) == 4:
        rows = parts[0].shape[0]
        sent = swap_tensor(half(jnp.concatenate([parts[3], parts[1]], axis=0)), 1)
        sent = sent.astype(jnp.float32)
        return (parts[0] + sent[rows:], half(parts[2] + sent[:rows]))
    return (half(jnp.concatenate(parts, axis=0)),)


def collect_far(sums):
    if len(sums) == 2:
        return sums[0] + swap_tensor(sums[1], 2).astype(jnp.float32)
    return lax.psum_scatter(
        sums[0], "tensor", scatter_dimension=0, tiled=True
    ).astype(jnp.float32)


def collect(parts):
    return collect_far(collect_near(parts))


def in_place(blocks):
    if len(blocks) == 4:
        stacked = jnp.stack(blocks)
        mine = lax.axis_index("tensor")
        blocks = [
            lax.dynamic_index_in_dim(stacked, mine ^ i, 0, keepdims=False)
            for i in range(len(blocks))
        ]
    return jnp.concatenate(blocks, axis=0)


def dp_neighbour():
    mine = lax.axis_index("dp")
    return mine + 1 - 2 * (mine % 2)


def meet(everyone, neighbour):
    barrier = pltpu.get_barrier_semaphore()
    if everyone:
        others = [
            {axis: (lax.axis_index(axis) + step) % lax.axis_size(axis)}
            for axis in ("dp", "tensor")
            for step in range(1, lax.axis_size(axis))
        ]
    else:
        _, near, far, _ = row_peers()
        others = [{"tensor": near}, {"tensor": far}]
        if neighbour:
            others.append({"dp": dp_neighbour()})
    for other in others:
        pl.semaphore_signal(barrier, inc=1, device_id=other, device_id_type=MESH)
    pl.semaphore_wait(barrier, len(others))


def remote_call(
    kernel,
    name,
    number,
    operands,
    outs,
    scratch,
    carry=(),
    everyone=False,
    neighbour=False,
    after=(),
    late=(),
    late_outs=(),
):
    copies = sum(array.shape[0] if len(array.shape) == 4 else 1 for array in carry)
    traded = [
        jax.ShapeDtypeStruct(
            (array.shape[0], *array.shape[2:]) if len(array.shape) == 4 else array.shape,
            array.dtype,
        )
        for array in carry
    ]

    def run(*refs):
        refs = list(refs)
        ins = [refs.pop(0) for _ in (*operands, *late)]
        sources = [refs.pop(0) for _ in carry]
        del refs[: len(after)]
        results = [refs.pop(0) for _ in (*outs, *late_outs)]
        targets = [refs.pop(0) for _ in carry]
        meet(everyone, neighbour or bool(carry))
        started = []
        if carry:
            sems = refs.pop()
            other = dp_neighbour()
            pairs = []
            for source, target in zip(sources, targets):
                if len(source.shape) == 2:
                    pairs.append((source, target))
                else:
                    pairs += [
                        (source.at[i, other % 2], target.at[i]) for i in range(source.shape[0])
                    ]
            for i, (source, target) in enumerate(pairs):
                copy = pltpu.make_async_remote_copy(
                    src_ref=source,
                    dst_ref=target,
                    send_sem=sems.at[0, i],
                    recv_sem=sems.at[1, i],
                    device_id={"dp": other},
                    device_id_type=MESH,
                )
                copy.start()
                started.append(copy)
        kernel(*ins, *results, *refs)
        for copy in started:
            copy.wait()

    whole = pl.BlockSpec(memory_space=pltpu.VMEM)
    anywhere = pl.BlockSpec(memory_space=pl.ANY)
    return pl.pallas_call(
        run,
        out_shape=[*outs, *late_outs, *traded],
        in_specs=[whole] * len(operands) + [anywhere] * (len(late) + len(carry) + len(after)),
        out_specs=[whole] * len(outs) + [anywhere] * (len(late_outs) + len(carry)),
        scratch_shapes=[
            *scratch,
            *([pltpu.SemaphoreType.DMA((2, copies))] if carry else []),
        ],
        compiler_params=pltpu.CompilerParams(
            collective_id=number, has_side_effects=True, vmem_limit_bytes=60 * 1024 * 1024
        ),
        cost_estimate=pl.CostEstimate(flops=1 << 20, bytes_accessed=1 << 20, transcendentals=0),
        name=name,
    )(*operands, *late, *carry, *after)


def send_blocks(axis, pick, target, send_sem, recv_sem):
    count = lax.axis_size(axis)
    mine = lax.axis_index(axis)

    def copy(other, place):
        return pltpu.make_async_remote_copy(
            src_ref=pick(other),
            dst_ref=target.at[place],
            send_sem=send_sem.at[other],
            recv_sem=recv_sem.at[place],
            device_id={axis: other},
            device_id_type=MESH,
        )

    others = [(mine + step) % count for step in range(1, count)]
    for other in others:
        copy(other, mine).start()
    for other in others:
        copy(other, mine).wait_send()
        copy(other, other).wait_recv()


def spread_kernel(source, target, middle, send_dp, recv_dp, send_tensor, recv_tensor):
    mine = lax.axis_index("dp")
    middle[mine] = source[mine]
    send_blocks("dp", lambda other: source.at[other], middle, send_dp, recv_dp)
    target[lax.axis_index("tensor")] = middle[...]
    send_blocks("tensor", lambda other: middle, target, send_tensor, recv_tensor)


def return_kernel(
    source, target, middle, summed, last, send_dp, recv_dp, send_tensor, recv_tensor
):
    place = lax.axis_index("tensor")
    middle[place] = source[place]
    send_blocks("tensor", lambda other: source.at[other], middle, send_tensor, recv_tensor)
    total = middle[0]
    for other in range(1, lax.axis_size("tensor")):
        total += middle[other]
    summed[...] = total
    mine = lax.axis_index("dp")
    last[mine] = summed[mine]
    send_blocks("dp", lambda other: summed.at[other], last, send_dp, recv_dp)
    target[...] = last[...]


def total_kernel(source, target, near, far, part, send_dp, recv_dp, send_tensor, recv_tensor):
    near[lax.axis_index("tensor")] = source[...]
    send_blocks("tensor", lambda other: source, near, send_tensor, recv_tensor)
    part[...] = jnp.sum(near[...], axis=0)
    far[lax.axis_index("dp")] = part[...]
    send_blocks("dp", lambda other: part, far, send_dp, recv_dp)
    target[...] = jnp.sum(far[...], axis=0)


def exchange_scratch(shapes):
    sizes = (lax.axis_size("dp"),) * 2 + (lax.axis_size("tensor"),) * 2
    return [pltpu.VMEM(shape, jnp.float32) for shape in shapes] + [
        pltpu.SemaphoreType.DMA((size,)) for size in sizes
    ]


CHUNKS = 4


def row_peers():
    mine = lax.axis_index("tensor")
    near = mine + 1 - 2 * (mine % 2)
    return (mine, near, (mine + 2) % 4, (near + 2) % 4)


def remote(source, target, sems, index, other):
    return pltpu.make_async_remote_copy(
        src_ref=source,
        dst_ref=target,
        send_sem=sems.at[0, index],
        recv_sem=sems.at[1, index],
        device_id={"tensor": other},
        device_id_type=MESH,
    )


def chunk_rows(total):
    size = total // CHUNKS
    return [slice(i * size, (i + 1) * size) for i in range(CHUNKS)]


def sum_blocks(partial, finish, work, sems, by_columns=False):
    mine, near, far, both = row_peers()
    send_both, send_near, near_both, near_own, send_far, far_own, base = work
    size, width = base.shape[0] // 2, base.shape[1]
    step = width // CHUNKS
    if by_columns:
        chunks = [(slice(None), slice(i * step, (i + 1) * step)) for i in range(CHUNKS)]
    else:
        chunks = [(rows, slice(None)) for rows in chunk_rows(size)]

    def terms(block, place):
        rows, columns = place
        first, count = rows.start or 0, size if by_columns else size // CHUNKS
        start = pl.multiple_of((block % 2) * size + first, count)
        return base[pl.ds(start, count), columns]

    def hand_over(chip, block, source, target, kind):
        copies = []
        if not by_columns:
            partial(chip, base, None)
        for i, place in enumerate(chunks):
            if by_columns:
                partial(chip, base, place[1])
            source[place] = half(terms(block, place))
            copies.append(
                remote(source.at[place], target.at[place], sems, CHUNKS * kind + i, near)
            )
            copies[i].start()
            if by_columns and i:
                yield i - 1, copies[i - 1]
        for i in range(CHUNKS - 1 if by_columns else 0, CHUNKS):
            yield i, copies[i]

    across = []
    for i, copy in hand_over(far // 2, both, send_both, near_both, 0):
        place = chunks[i]
        copy.wait()
        send_far[place] = half(terms(far, place) + near_both[place].astype(jnp.float32))
        across.append(
            remote(send_far.at[place], far_own.at[place], sems, 2 * CHUNKS + i, far)
        )
        across[i].start()
    for i, copy in hand_over(mine // 2, near, send_near, near_own, 1):
        place = chunks[i]
        copy.wait()
        across[i].wait()
        finish(
            i,
            place[1] if by_columns else place[0],
            terms(mine, place)
            + near_own[place].astype(jnp.float32)
            + far_own[place].astype(jnp.float32),
        )


SUM_SEMAPHORES = 3 * CHUNKS


def chip_rows(chip, size):
    return pl.ds(pl.multiple_of(chip * 2 * size, 2 * size), 2 * size)


def sum_scratch(rows, columns):
    narrow = pltpu.VMEM((rows, columns), jnp.bfloat16)
    return [narrow] * 6 + [pltpu.VMEM((2 * rows, columns), jnp.float32)]


class Spread:
    def __init__(self, gathered, sems, base):
        self.gathered, self.sems, self.base = gathered, sems, base
        self.mine, self.near, self.far, self.both = row_peers()
        self.chunks = chunk_rows(gathered.shape[1])
        self.started = []

    def copy(self, block, i, kind, other):
        part = self.gathered.at[block, self.chunks[i]]
        return remote(part, part, self.sems, self.base + CHUNKS * kind + i, other)

    def offer(self, i, value):
        self.gathered[self.mine, self.chunks[i], :] = value
        for kind, other in ((0, self.far), (1, self.near)):
            copy = self.copy(self.mine, i, kind, other)
            copy.start()
            self.started.append(copy)

    def settle(self):
        for i in range(CHUNKS):
            self.copy(self.far, i, 0, self.far).wait_recv()
            forward = self.copy(self.far, i, 2, self.near)
            forward.start()
            self.started.append(forward)
        for i in range(CHUNKS):
            self.copy(self.near, i, 1, self.near).wait_recv()
            self.copy(self.both, i, 2, self.near).wait_recv()
        for copy in self.started:
            copy.wait_send()


def tiles_of(total, size):
    def run(step):
        def body(index, carry):
            step(pl.ds(pl.multiple_of(index * size, size), size))
            return carry

        lax.fori_loop(0, total // size, body, 0)

    return run


def pick(chooser, factor, which, rows):
    width = factor.shape[1] // 4
    return jnp.dot(
        chooser[rows, :],
        factor[:, which * width : (which + 1) * width],
        precision=HIGH,
        preferred_element_type=jnp.float32,
    )


def add_up(place, target, value):
    target[place] += jnp.sum(value.reshape(-1, 8, value.shape[1]), axis=0)


def add_images(choose, i, place, target, value):
    target[place] += jnp.dot(
        choose[i], value, precision=HIGH, preferred_element_type=jnp.float32
    )


def enter_kernel(latents, factor, chooser, gain, gathered, sems):
    share = Spread(gathered, sems, 0)
    for i, rows in enumerate(share.chunks):
        scale = pick(chooser, factor, 0, rows)
        share.offer(i, enter_point(latents[rows, :].astype(jnp.float32), scale, gain[0:1]))
    share.settle()


def project_kernel(weight, captions, total, *rest):
    work, sems = rest[:-1], rest[-1]
    local = total.shape[0]

    def partial(chip, base, columns):
        base[:, columns] = dot(weight[chip_rows(chip, local), :], captions[columns, :], 1, 1)

    def finish(i, columns, value):
        total[:, columns] = value

    sum_blocks(partial, finish, work, sems, by_columns=True)


def transposed_partial(left, weight, lhs, size):
    def partial(chip, base, _):
        lhs[...] = half(left[:, chip_rows(chip, size)].astype(jnp.float32).T)

        @tiles_of(weight.shape[0], 512)
        def _(columns):
            base[:, columns] = dot(lhs[...], weight[columns, :], 1, 1)

    return partial


def attention_out_kernel(
    mixed, weight, latents, factor, chooser, gain, summed, middle, gathered, *rest
):
    lhs, work, sems = rest[0], rest[1:-1], rest[-1]
    share = Spread(gathered, sems, SUM_SEMAPHORES)

    def finish(i, rows, value):
        summed[rows, :] = value
        middle[rows, :], out = middle_point(
            value,
            latents[rows, :].astype(jnp.float32),
            pick(chooser, factor, 1, rows),
            pick(chooser, factor, 2, rows),
            gain[1:2],
            gain[2:3],
        )
        share.offer(i, out)

    sum_blocks(transposed_partial(mixed, weight, lhs, latents.shape[0]), finish, work, sems)
    share.settle()


def begin_copies(pairs, sems):
    copies = [
        pltpu.make_async_copy(source, target, sems.at[i])
        for i, (source, target) in enumerate(pairs)
    ]
    for copy in copies:
        copy.start()
    return copies


def feed_kernel(
    inputs, feed, factor, chooser, choose, gain, down_far, middle_far, cotangent_far,
    hidden, out, factor_grad, row_grad, gathered, gate_far, *rest
):
    gate_up, down, middle, cotangent, moves = rest[:5]
    work, sems = rest[5:-1], rest[-1]
    size = middle.shape[0]
    units = hidden.shape[1]
    loads = begin_copies(
        [(down_far, down), (middle_far, middle), (cotangent_far, cotangent)], moves
    )
    saves = []
    factor_grad[...] = jnp.zeros_like(factor_grad)
    row_grad[...] = jnp.zeros_like(row_grad)

    def partial(chip, base, _):
        own = chip_rows(chip, size)

        @tiles_of(units, 512)
        def _(columns):
            other = pl.ds(pl.multiple_of(columns.start + units, 512), 512)
            first = dot(inputs[own, :], feed[:, columns], 1, 0)
            second = dot(inputs[own, :], feed[:, other], 1, 0)
            gate_up[own, columns] = first
            gate_up[own, other] = second
            hidden[own, columns] = half(first * jax.nn.sigmoid(first) * second)

        save = pltpu.make_async_copy(
            gate_up.at[own], gate_far.at[own], moves.at[3 + len(saves)]
        )
        save.start()
        saves.append(save)
        for load in loads[:1] if len(saves) == 1 else loads[1:]:
            load.wait()

        @tiles_of(down.shape[0], 512)
        def _(columns):
            base[:, columns] = dot(hidden[own, :], down[columns, :], 1, 1)

    share = Spread(gathered, sems, SUM_SEMAPHORES)

    def finish(i, rows, value):
        out[rows, :], back, gate_grad, row = end_point(
            value,
            middle[rows, :],
            pick(chooser, factor, 3, rows),
            cotangent[rows, :],
            gain[3:4],
        )
        share.offer(i, back)
        add_images(choose, i, 0, factor_grad, gate_grad)
        add_up(0, row_grad, row)

    sum_blocks(partial, finish, work, sems)
    share.settle()
    for save in saves:
        save.wait()


def feed_back_kernel(
    back, down, factor, chooser, choose, gain, gate_far, feed_far, summed_far, middle_far,
    cotangent_far, middle_grad, factor_grad, row_grad, gathered, pair_far, *rest
):
    gate_up, feed, summed, middle, cotangent, pair, moves = rest[:7]
    work, sems = rest[7:-1], rest[-1]
    size = middle.shape[0]
    units = down.shape[1]
    mine, _, far, _ = row_peers()
    first_rows, last_rows = chip_rows(far // 2, size), chip_rows(mine // 2, size)
    loads = begin_copies(
        [
            (gate_far.at[first_rows], gate_up.at[first_rows]),
            (feed_far, feed),
            (gate_far.at[last_rows], gate_up.at[last_rows]),
            (summed_far, summed),
            (middle_far, middle),
            (cotangent_far, cotangent),
        ],
        moves,
    )
    saves = []
    factor_grad[...] = jnp.zeros_like(factor_grad)
    row_grad[...] = jnp.zeros_like(row_grad)

    def partial(chip, base, _):
        own = chip_rows(chip, size)
        loads[2 if saves else 0].wait()

        @tiles_of(units, 512)
        def _(columns):
            other = pl.ds(pl.multiple_of(columns.start + units, 512), 512)
            grad = dot(back[own, :], down[:, columns], 1, 0)
            first, second = gate_up[own, columns], gate_up[own, other]
            pair[own, columns], pair[own, other] = pair_point(grad, first, second)

        save = pltpu.make_async_copy(pair.at[own], pair_far.at[own], moves.at[6 + len(saves)])
        save.start()
        saves.append(save)
        for load in loads[1:2] if len(saves) == 1 else loads[3:]:
            load.wait()

        @tiles_of(feed.shape[0], 512)
        def _(columns):
            base[:, columns] = dot(pair[own, :], feed[columns, :], 1, 1)

    share = Spread(gathered, sems, SUM_SEMAPHORES)

    def finish(i, rows, value):
        middle_grad[rows, :], out, gate_grad, scale_grad, first_row, second_row = (
            middle_back_point(
                value,
                summed[rows, :],
                middle[rows, :],
                pick(chooser, factor, 1, rows),
                pick(chooser, factor, 2, rows),
                cotangent[rows, :],
                gain[1:2],
                gain[2:3],
            )
        )
        share.offer(i, out)
        add_images(choose, i, 0, factor_grad, gate_grad)
        add_images(choose, i, 1, factor_grad, scale_grad)
        add_up(0, row_grad, first_row)
        add_up(1, row_grad, second_row)

    sum_blocks(partial, finish, work, sems)
    share.settle()
    for save in saves:
        save.wait()


def enter_back_kernel(
    triple, weight, latents, factor, chooser, choose, middle_grad, gain,
    latent_grad, factor_grad, row_grad, *rest
):
    lhs, work, sems = rest[0], rest[1:-1], rest[-1]
    factor_grad[...] = jnp.zeros_like(factor_grad)
    row_grad[...] = jnp.zeros_like(row_grad)

    def finish(i, rows, value):
        latent_grad[rows, :], scale_grad, row = enter_back_point(
            value,
            latents[rows, :].astype(jnp.float32),
            pick(chooser, factor, 0, rows),
            middle_grad[rows, :],
            gain[0:1],
        )
        add_images(choose, i, 0, factor_grad, scale_grad)
        add_up(0, row_grad, row)

    sum_blocks(transposed_partial(triple, weight, lhs, latents.shape[0]), finish, work, sems)


def text_kernel(own, captions, summed, gathered, kept, sent, arrived, sems):
    mine, near, far, both = row_peers()
    other = dp_neighbour()
    odd = 1 - other % 2
    size = own.shape[0] // CHUNKS
    each = CHUNKS // 2
    started = []

    def part(k):
        base = (1 - odd) if k < each else odd
        return pl.ds(pl.multiple_of((base * each + k % each) * size, size), size)

    def move(block, k, kind, device):
        rows = gathered.at[block, part(k)]
        return remote(rows, rows, sems, CHUNKS * kind + k, device)

    def across(block, order, k):
        rows = pl.ds(k * size, size)
        return pltpu.make_async_remote_copy(
            src_ref=sent.at[block, rows],
            dst_ref=arrived.at[block, rows],
            send_sem=sems.at[0, 3 * CHUNKS + order * each + k],
            recv_sem=sems.at[1, 3 * CHUNKS + order * each + k],
            device_id={"dp": other},
            device_id_type=MESH,
        )

    def begin(copy):
        copy.start()
        started.append(copy)

    def work(block, order, k):
        value = dot(gathered[block, part(k), :], captions[...], 1, 0)
        rows = pl.ds((k % each) * size, size)
        if k < each:
            sent[block, rows, :] = half(value)
            begin(across(block, order, k))
        else:
            kept[block, rows, :] = value

    for k in range(CHUNKS):
        gathered[mine, part(k), :] = own[part(k), :]
        begin(move(mine, k, 0, far))
        begin(move(mine, k, 1, near))
    for k in range(CHUNKS):
        work(mine, 0, k)
    for k in range(CHUNKS):
        move(near, k, 1, near).wait_recv()
        work(near, 1, k)
    for k in range(CHUNKS):
        move(far, k, 0, far).wait_recv()
        begin(move(far, k, 2, near))
        work(far, 2, k)
        if k:
            move(both, k - 1, 2, near).wait_recv()
            work(both, 3, k - 1)
    move(both, CHUNKS - 1, 2, near).wait_recv()
    work(both, 3, CHUNKS - 1)
    for order, block in enumerate((mine, near, far, both)):
        for k in range(each):
            across(block, order, k).wait_recv()
            rows = pl.ds(k * size, size)
            summed[block, rows, :] = half(
                kept[block, rows, :] + arrived[block, rows, :].astype(jnp.float32)
            )
    for copy in started:
        copy.wait_send()


def enter_point(source, scale, gain):
    normed, _ = rms_parts(source)
    return half(normed * gain * (1.0 + scale))


def middle_point(summed, source, gate, scale, first_gain, second_gain):
    normed, _ = rms_parts(summed)
    middle = source + jnp.tanh(gate) * (normed * first_gain)
    return (middle, enter_point(middle, scale, second_gain))


def end_point(summed, middle, gate, cotangent, gain):
    normed, inverse = rms_parts(summed)
    turned = jnp.tanh(gate)
    branch = normed * gain
    grad = turned * cotangent
    return (
        middle + turned * branch,
        half(rms_back(normed, inverse, grad * gain)),
        cotangent * branch * (1.0 - turned * turned),
        grad * normed,
    )


def pair_point(grad, first, second):
    sigmoid = jax.nn.sigmoid(first)
    return (
        half(grad * second * (sigmoid + first * sigmoid * (1.0 - sigmoid))),
        half(grad * (first * sigmoid)),
    )


def middle_back_point(
    input_grad, summed, middle, gate, scale, cotangent, first_gain, second_gain
):
    normed, inverse = rms_parts(middle)
    gained = input_grad * (1.0 + scale)
    middle_grad = cotangent + rms_back(normed, inverse, gained * second_gain)
    scale_grad, second_row = input_grad * normed * second_gain, gained * normed
    normed, inverse = rms_parts(summed)
    turned = jnp.tanh(gate)
    branch = turned * middle_grad
    return (
        middle_grad,
        half(rms_back(normed, inverse, branch * first_gain)),
        middle_grad * (normed * first_gain) * (1.0 - turned * turned),
        scale_grad,
        branch * normed,
        second_row,
    )


def enter_back_point(input_grad, source, scale, middle_grad, gain):
    normed, inverse = rms_parts(source)
    gained = input_grad * (1.0 + scale)
    return (
        middle_grad + rms_back(normed, inverse, gained * gain),
        input_grad * normed * gain,
        gained * normed,
    )


def spans(heads):
    return [slice(head * HEAD, (head + 1) * HEAD) for head in range(heads)]


def head_norm(value):
    inverse = lax.rsqrt(jnp.mean(value * value, axis=0, keepdims=True) + EPS)
    return (value * inverse, inverse)


def head_back(normed, inverse, grad):
    return inverse * (grad - normed * jnp.mean(grad * normed, axis=0, keepdims=True))


def turn(value, cosine, sine):
    middle = HEAD // 2
    first, second = value[:middle], value[middle:]
    return jnp.concatenate(
        [first * cosine - second * sine, second * cosine + first * sine], axis=0
    )


def self_bias(step, ids_row, ids_column):
    start = pl.multiple_of(step * TILE, TILE)
    return jnp.where(ids_column[pl.ds(start, TILE), :] == ids_row[...], 0.0, NEG)


def cross_bias(step, ids_row, lengths):
    slots = lax.broadcasted_iota(jnp.int32, (TILE, 1), 0) < lengths[step]
    return jnp.where(slots & (ids_row[...] == step), 0.0, NEG)


def attend_tile(heads, meta, bias_of, query, key_rows, value, out, total, inv_ref):
    base = 2 * pl.program_id(0)
    factor = HEAD ** (-0.5) * LOG2E
    out[...] = jnp.zeros_like(out)
    total[...] = jnp.zeros_like(total)

    def step(index, carry):
        bias = bias_of(index)
        rows = pl.ds(pl.multiple_of(index * TILE, TILE), TILE)
        scores = [
            dot(key_rows[head, rows, :], query[span, :], 1, 0)
            for head, span in enumerate(spans(heads))
        ]
        for head, span in enumerate(spans(heads)):
            expo = jnp.exp2(scores[head] * factor + bias)
            total[head] += jnp.sum(expo.reshape(TILE // 8, 8, TILE), axis=0)
            out[span, :] += dot(value[span, rows], half(expo), 1, 0)
        return carry

    lax.fori_loop(meta[base], meta[base + 1], step, 0)
    for head, span in enumerate(spans(heads)):
        inverse = 1.0 / jnp.sum(total[head], axis=0, keepdims=True)
        inv_ref[head] = jnp.broadcast_to(inverse, (8, TILE))
        out[span, :] = out[span, :] * inverse


def attend_back_tile(
    heads, meta, bias_of, query, key_rows, key, value_rows, inv_ref, out, back, dq, dk, dv, centre
):
    base = 2 * pl.program_id(0)
    scale = HEAD ** (-0.5)
    dq[...] = jnp.zeros_like(dq)
    for head, span in enumerate(spans(heads)):
        both = out[span, :] * back[span, :].astype(jnp.float32)
        centre[head] = jnp.broadcast_to(jnp.sum(both, axis=0, keepdims=True), (8, TILE))

    def step(index, carry):
        bias = bias_of(index)
        rows = pl.ds(pl.multiple_of(index * TILE, TILE), TILE)
        def products(head):
            span = spans(heads)[head]
            return (
                dot(key_rows[head, rows, :], query[span, :], 1, 0),
                dot(value_rows[head, rows, :], back[span, :], 1, 0),
            )

        ahead = [products(head) for head in range(min(AHEAD, heads))]
        for head, span in enumerate(spans(heads)):
            scores, prob_grad = ahead.pop(0)
            if head + AHEAD < heads:
                ahead.append(products(head + AHEAD))
            probs = jnp.exp2(scores * (scale * LOG2E) + bias)
            probs = probs * inv_ref[head, 0:1, :]
            score_grad = half(probs * (prob_grad - centre[head, 0:1, :]))
            dv[span, rows] += dot(back[span, :], half(probs), 1, 1)
            dk[span, rows] += dot(query[span, :], score_grad, 1, 1) * scale
            dq[span, :] += dot(key[span, rows], score_grad, 1, 0) * scale
        return carry

    lax.fori_loop(meta[base], meta[base + 1], step, 0)


def self_forward_kernel(
    heads,
    meta,
    ids_row,
    ids_column,
    gain,
    cosine,
    sine,
    cosine_all,
    sine_all,
    raw_query,
    raw_key,
    raw_value,
    query,
    key,
    key_rows,
    value_rows,
    out,
    inv_ref,
    value,
    total,
):
    local = heads * HEAD

    @pl.when(pl.program_id(0) == 0)
    def _():
        for head, span in enumerate(spans(heads)):
            normed, _ = head_norm(raw_key[span, :])
            turned = turn(normed * gain[span, 1:2], cosine_all[...], sine_all[...])
            key[span, :] = half(turned)
            key_rows[head] = half(turned.T)
            plain = raw_value[span, :]
            value[span, :] = half(plain)
            value_rows[head] = half(plain.T)

    for span in spans(heads):
        normed, _ = head_norm(raw_query[span, :])
        query[span, :] = half(turn(normed * gain[span, 0:1], cosine[...], sine[...]))
    attend_tile(
        heads,
        meta,
        lambda index: self_bias(index, ids_row, ids_column),
        query,
        key_rows,
        value,
        out,
        total,
        inv_ref,
    )


def cross_forward_kernel(
    heads,
    meta,
    lengths,
    ids_row,
    gain,
    query,
    own_out,
    raw_key,
    raw_value,
    key,
    key_rows,
    value_rows,
    out,
    inv_ref,
    mixed,
    value,
    total,
):
    @pl.when(pl.program_id(0) == 0)
    def _():
        for head, span in enumerate(spans(heads)):
            normed, _ = head_norm(raw_key[span, :])
            normed = normed * gain[span, 2:3]
            key[span, :] = half(normed)
            key_rows[head] = half(normed.T)
            plain = raw_value[span, :]
            value[span, :] = half(plain)
            value_rows[head] = half(plain.T)

    attend_tile(
        heads,
        meta,
        lambda index: cross_bias(index, ids_row, lengths),
        query,
        key_rows,
        value,
        out,
        total,
        inv_ref,
    )
    mixed[...] = half(own_out[...] + jnp.tanh(gain[:, 3:4]) * out[...])


def cross_backward_kernel(
    heads,
    meta,
    lengths,
    ids_row,
    gain,
    query,
    key_rows,
    key,
    value_rows,
    inv_ref,
    out,
    mixed_grad,
    raw_key,
    dq,
    dk,
    dv,
    gain_grad,
    back,
    centre,
    dk_sum,
    dv_sum,
    gate_sum,
):
    place = pl.program_id(0)

    @pl.when(place == 0)
    def _():
        dk_sum[...] = jnp.zeros_like(dk_sum)
        dv_sum[...] = jnp.zeros_like(dv_sum)
        gate_sum[...] = jnp.zeros_like(gate_sum)

    gate = jnp.tanh(gain[:, 3:4])
    back[...] = half(gate * mixed_grad[...])
    gate_sum[...] += mixed_grad[...] * out[...]
    attend_back_tile(
        heads,
        meta,
        lambda index: cross_bias(index, ids_row, lengths),
        query,
        key_rows,
        key,
        value_rows,
        inv_ref,
        out,
        back,
        dq,
        dk_sum,
        dv_sum,
        centre,
    )

    @pl.when(place == pl.num_programs(0) - 1)
    def _():
        dv[...] = half(dv_sum[...])
        gate_grad = jnp.sum(gate_sum[...], axis=1, keepdims=True) * (1.0 - gate * gate)
        gain_grad[:, 0:128] = jnp.broadcast_to(gate_grad, (heads * HEAD, 128))
        for span in spans(heads):
            normed, inverse = head_norm(raw_key[span, :])
            grad = dk_sum[span, :]
            summed = jnp.sum(grad * normed, axis=1, keepdims=True)
            gain_grad[span, 128:256] = jnp.broadcast_to(summed, (HEAD, 128))
            dk[span, :] = half(head_back(normed, inverse, grad * gain[span, 2:3]))


def self_backward_kernel(
    heads,
    meta,
    ids_row,
    ids_column,
    gain,
    cosine,
    sine,
    cosine_all,
    sine_all,
    query,
    key_rows,
    key,
    value_rows,
    inv_ref,
    out,
    mixed_grad,
    other_dq,
    raw_query,
    raw_key,
    triple,
    gain_grad,
    back,
    centre,
    dq,
    dk_sum,
    dv_sum,
    query_sum,
):
    place = pl.program_id(0)
    local = heads * HEAD

    @pl.when(place == 0)
    def _():
        dk_sum[...] = jnp.zeros_like(dk_sum)
        dv_sum[...] = jnp.zeros_like(dv_sum)
        query_sum[...] = jnp.zeros_like(query_sum)

    back[...] = half(mixed_grad[...])
    attend_back_tile(
        heads,
        meta,
        lambda index: self_bias(index, ids_row, ids_column),
        query,
        key_rows,
        key,
        value_rows,
        inv_ref,
        out,
        back,
        dq,
        dk_sum,
        dv_sum,
        centre,
    )
    columns = pl.ds(pl.multiple_of(place * TILE, TILE), TILE)
    for span in spans(heads):
        normed, inverse = head_norm(raw_query[span, :])
        grad = turn(dq[span, :] + other_dq[span, :], cosine[...], -sine[...])
        query_sum[span, :] += grad * normed
        triple[span, columns] = half(head_back(normed, inverse, grad * gain[span, 0:1]))

    @pl.when(place == pl.num_programs(0) - 1)
    def _():
        summed = jnp.sum(query_sum[...], axis=1, keepdims=True)
        gain_grad[:, 0:128] = jnp.broadcast_to(summed, (local, 128))
        triple[2 * local :, :] = half(dv_sum[...])
        for head, span in enumerate(spans(heads)):
            normed, inverse = head_norm(raw_key[span, :])
            grad = turn(dk_sum[span, :], cosine_all[...], -sine_all[...])
            summed = jnp.sum(grad * normed, axis=1, keepdims=True)
            gain_grad[span, 128:256] = jnp.broadcast_to(summed, (HEAD, 128))
            triple[local + head * HEAD : local + (head + 1) * HEAD, :] = half(
                head_back(normed, inverse, grad * gain[span, 1:2])
            )


def attention_call(kernel, name, scalars, operands, outs, scratch, tokens, weight, after=()):
    def block(array, tiled):
        lead = array.shape[:-1]
        if tiled is not True and tiled is not False:
            third = (lead[0] // 3, tokens if tiled else TILE)
            return pl.BlockSpec(third, lambda i, *_: (tiled, 0) if tiled else (0, i))
        if tiled:
            return pl.BlockSpec((*lead, TILE), lambda i, *_: (*([0] * len(lead)), i))
        return pl.BlockSpec(array.shape, lambda i, *_: (0,) * len(array.shape))

    count = len(scalars) + len(operands)

    def run(*refs):
        kernel(*refs[:count], *refs[count + len(after) :])

    return pl.pallas_call(
        run,
        grid_spec=pltpu.PrefetchScalarGridSpec(
            num_scalar_prefetch=len(scalars),
            grid=(tokens // TILE,),
            in_specs=[block(*operand) for operand in operands]
            + [pl.BlockSpec(memory_space=pl.ANY)] * len(after),
            out_specs=[block(*out) for out in outs],
            scratch_shapes=scratch,
        ),
        out_shape=[out for out, _ in outs],
        compiler_params=pltpu.CompilerParams(
            vmem_limit_bytes=58 * 1024 * 1024, dimension_semantics=("arbitrary",)
        ),
        cost_estimate=pl.CostEstimate(
            flops=weight, bytes_accessed=weight, transcendentals=0
        ),
        name=name,
    )(*scalars, *(operand for operand, _ in operands), *after)


def adamw(grad, weight, moment, square, decay, rate):
    moment_new = BETA1 * moment + (1.0 - BETA1) * grad
    square_new = BETA2 * square + (1.0 - BETA2) * grad * grad
    step_size = (
        moment_new / (1.0 - BETA1**STEP) / (jnp.sqrt(square_new / (1.0 - BETA2**STEP)) + ADAM_EPS)
    )
    return (moment_new, square_new, weight - rate * (step_size + decay * weight))


def body(
    latents,
    cotangent,
    captions,
    conditions,
    image_ids,
    rope_rows,
    rope_cols,
    caption_lengths,
    attention_in,
    attention_out,
    feed_in,
    feed_out,
    caption_in,
    modulator,
    channels,
    moment_attention_in,
    square_attention_in,
    moment_attention_out,
    square_attention_out,
    moment_feed_in,
    square_feed_in,
    moment_feed_out,
    square_feed_out,
    moment_caption_in,
    square_caption_in,
    moment_modulator,
    square_modulator,
    moment_channels,
    square_channels,
):
    tensor_size = lax.axis_size("tensor")
    tensor_index = lax.axis_index("tensor")
    dp_size = lax.axis_size("dp")
    dp_index = lax.axis_index("dp")
    shard_rows, width = latents.shape
    local = attention_in.shape[2]
    heads = local // HEAD
    units = feed_in.shape[2]
    segment = image_ids[0]
    row_tokens = segment.shape[0]
    images = conditions.shape[0]
    per_row = caption_lengths.shape[1]
    lengths = caption_lengths[0]
    slots = captions.shape[0]
    offset = tensor_index * local
    own_ids = lax.dynamic_slice_in_dim(segment, tensor_index * shard_rows, shard_rows)

    rows = attention_in.shape[1]
    fused = tensor_size == 4
    caption_half = half(caption_in)
    key_line = gather_far(caption_half[0].T)
    value_line = gather_far(
        jnp.concatenate([caption_half[1].T, half(attention_out).T], axis=1)
    )
    in_half = half(attention_in)
    attention_line = gather_far(jnp.concatenate([in_half[0], in_half[1], in_half[2]], axis=1))
    down_line = gather_far(half(feed_out).T)
    feed_half = half(feed_in)
    feed_own = jnp.concatenate([feed_half[0], feed_half[1]], axis=1)

    augmented = half(
        jnp.concatenate([jax.nn.silu(conditions), jnp.ones((images, 1), jnp.float32)], axis=1)
    )
    factor_part = jnp.dot(augmented, half(modulator), preferred_element_type=jnp.float32)
    own_columns = factor_part.shape[1]
    payload = jnp.concatenate(
        [
            factor_part.reshape(dp_size, per_row, own_columns),
            jnp.broadcast_to(
                lax.reduce_precision(channels, 8, 7).reshape(-1, own_columns),
                (dp_size, channels.size // own_columns, own_columns),
            ),
        ],
        axis=1,
    )
    received, feed_other = remote_call(
        spread_kernel,
        "modulation_exchange",
        0,
        [payload],
        [jax.ShapeDtypeStruct((tensor_size, *payload.shape), jnp.float32)],
        exchange_scratch([payload.shape]),
        [feed_own],
        everyone=True,
    )
    feed_full = gather_far(join_near(feed_own, feed_other, rows))
    factor_row = jnp.transpose(received[:, :, :per_row], (2, 1, 0, 3)).reshape(per_row, -1)
    gains = received[0, :, per_row:].reshape(dp_size, 8, -1)
    gains = jnp.transpose(gains, (1, 0, 2)).reshape(8, width)
    local_gains = lax.dynamic_slice_in_dim(gains[4:], offset, local, 1).T
    chooser = (own_ids[:, None] == jnp.arange(per_row, dtype=jnp.int32)[None, :]).astype(
        jnp.float32
    )
    choose = jnp.transpose(chooser.reshape(CHUNKS, -1, per_row), (0, 2, 1))

    def token_factor(which):
        return pick(chooser, factor_row, which, slice(None))

    def split(value):
        return [value[i * shard_rows : (i + 1) * shard_rows] for i in range(tensor_size)]

    def by_image(*grads):
        return jnp.stack([jnp.dot(chooser.T, grad, precision=HIGH) for grad in grads])

    f32, bf16 = jnp.float32, jnp.bfloat16

    def shape(dims, dtype=f32):
        return jax.ShapeDtypeStruct(dims, dtype)

    gathered = shape((tensor_size, shard_rows, width), bf16)
    in_kernel = sum_scratch(shard_rows, width)

    def semaphores(count):
        return pltpu.SemaphoreType.DMA((2, count))

    sum_sems, all_sems = semaphores(SUM_SEMAPHORES), semaphores(SUM_SEMAPHORES + 3 * CHUNKS)
    source = latents.astype(f32)

    def caption_project(weight, carry, number):
        if fused:
            return remote_call(
                project_kernel,
                "project",
                number,
                [weight, captions],
                [shape((local, slots))],
                [*sum_scratch(local, slots), sum_sems],
                carry,
            )
        total = collect(
            [
                dot(
                    lax.dynamic_slice_in_dim(weight, owner(i) * local, local), captions, 1, 1
                )
                for i in range(tensor_size)
            ]
        )
        return (total, *(near_swap(array) for array in carry))

    if fused:
        attn_full, key_other = remote_call(
            enter_kernel,
            "enter",
            3,
            [latents, factor_row, chooser, gains],
            [gathered],
            [semaphores(3 * CHUNKS)],
            [key_line],
        )
        attn_full = attn_full.reshape(row_tokens, width)
    else:
        attn_full = in_place(spread(enter_point(source, token_factor(0), gains[0])))
        key_other = near_swap(key_line)
    text_key_raw, value_other = caption_project(
        join_near(key_line, key_other, rows), [value_line], 4
    )
    features = captions.shape[1]
    value_full, out_full = (
        join_near(value_line[:, part], value_other[:, part], rows)
        for part in (slice(0, features), slice(features, None))
    )
    text_value_raw, attention_other = caption_project(value_full, [attention_line], 11)
    in_full = join_near(attention_line, attention_other, rows)
    projected = dot(in_full, attn_full, 0, 1)
    cosine, sine = rope_tables(rope_rows[0], rope_cols[0])

    tiles = row_tokens // TILE
    first_id = segment.reshape(tiles, TILE)[:, 0]
    last_id = segment.reshape(tiles, TILE)[:, TILE - 1]
    low = jnp.sum((segment[None] < first_id[:, None]).astype(jnp.int32), axis=1) // TILE
    high = (
        jnp.sum((segment[None] <= last_id[:, None]).astype(jnp.int32), axis=1) + TILE - 1
    ) // TILE
    self_meta = jnp.stack([low, high], axis=1).reshape(-1)
    cross_meta = jnp.stack([first_id, last_id + 1], axis=1).reshape(-1)
    ids_row = image_ids
    ids_column = segment[:, None]
    wide = jax.ShapeDtypeStruct((local, row_tokens), jnp.float32)
    narrow = jax.ShapeDtypeStruct((local, row_tokens), jnp.bfloat16)
    sums = jax.ShapeDtypeStruct((heads, 8, row_tokens), jnp.float32)
    by_rows = jax.ShapeDtypeStruct((heads, row_tokens, HEAD), jnp.bfloat16)
    text_narrow = jax.ShapeDtypeStruct((local, slots), jnp.bfloat16)
    text_rows = jax.ShapeDtypeStruct((heads, slots, HEAD), jnp.bfloat16)
    gain_shape = jax.ShapeDtypeStruct((local, 256), jnp.float32)
    tile_sums = pltpu.VMEM((heads, 8, TILE), jnp.float32)
    tables = [(cosine, True), (sine, True), (cosine, False), (sine, False)]
    queries, keys, key_rows, value_rows, own_out, own_inv = attention_call(
        functools.partial(self_forward_kernel, heads),
        "self_forward",
        [self_meta],
        [
            (ids_row, True),
            (ids_column, False),
            (local_gains, False),
            *tables,
            (projected, 0),
            (projected, 1),
            (projected, 2),
        ],
        [
            (narrow, True),
            (narrow, False),
            (by_rows, False),
            (by_rows, False),
            (wide, True),
            (sums, True),
        ],
        [pltpu.VMEM((local, row_tokens), jnp.bfloat16), tile_sums],
        row_tokens,
        15000,
    )
    text_keys, text_key_rows, text_value_rows, other_out, other_inv, mixed = attention_call(
        functools.partial(cross_forward_kernel, heads),
        "cross_forward",
        [cross_meta, lengths],
        [
            (ids_row, True),
            (local_gains, False),
            (queries, True),
            (own_out, True),
            (text_key_raw, False),
            (text_value_raw, False),
        ],
        [
            (text_narrow, False),
            (text_rows, False),
            (text_rows, False),
            (wide, True),
            (sums, True),
            (narrow, True),
        ],
        [pltpu.VMEM((local, slots), jnp.bfloat16), tile_sums],
        row_tokens,
        18000,
    )
    norm_gains = gains
    if fused:
        attn_sum, middle, feed_all, down_other = remote_call(
            attention_out_kernel,
            "attention_out",
            5,
            [mixed, out_full, latents, factor_row, chooser, norm_gains],
            [shape((shard_rows, width)), shape((shard_rows, width)), gathered],
            [pltpu.VMEM((2 * shard_rows, local), bf16), *in_kernel, all_sems],
            [down_line],
        )
        feed_all = feed_all.reshape(row_tokens, width)
        down_full = join_near(down_line, down_other, rows)
        block = pltpu.VMEM((shard_rows, width), f32)
        hidden, block_out, end_factor, end_row, feed_sum_grad, gate_up = remote_call(
            feed_kernel,
            "feed_forward",
            6,
            [feed_all, feed_full, factor_row, chooser, choose, norm_gains],
            [
                shape((row_tokens, units), bf16),
                shape((shard_rows, width)),
                shape((1, per_row, width)),
                shape((1, 8, width)),
                gathered,
            ],
            [
                pltpu.VMEM((row_tokens, 2 * units), f32),
                pltpu.VMEM((width, units), bf16),
                block,
                block,
                pltpu.SemaphoreType.DMA((5,)),
                *in_kernel,
                all_sems,
            ],
            late=[down_full, middle, cotangent],
            late_outs=[shape((row_tokens, 2 * units))],
        )
        feed_sum_grad = feed_sum_grad.reshape(row_tokens, width)
    else:
        attn_sum = collect(
            [
                dot(
                    lax.dynamic_slice_in_dim(mixed, owner(i) * shard_rows, shard_rows, 1),
                    out_full,
                    0,
                    1,
                )
                for i in range(tensor_size)
            ]
        )
        middle, feed_block = middle_point(
            attn_sum, source, token_factor(1), token_factor(2), gains[1], gains[2]
        )
        feed_all = in_place(spread(feed_block))
        down_full = join_near(down_line, near_swap(down_line), rows)
        gate_up = dot(feed_all, feed_full, 1, 0)
        hidden = half(jax.nn.silu(gate_up[:, :units]) * gate_up[:, units:])
        feed_sum = collect(split(dot(hidden, down_full, 1, 1)))
        block_out, feed_block_grad, *grads = end_point(
            feed_sum, middle, token_factor(3), cotangent, gains[3]
        )
        end_factor, end_row = by_image(grads[0]), grads[1][None]
        feed_sum_grad = in_place(spread(feed_block_grad))
    feed_out_grad = half(dot(feed_sum_grad, hidden, 0, 0))
    feed_out_parts = feed_out_grad.reshape(dp_size // 2, 2, -1, units)
    if fused:
        (
            middle_grad,
            middle_factor,
            middle_row,
            attn_sum_grad,
            pair_grad,
            feed_out_other,
        ) = remote_call(
            feed_back_kernel,
            "feed_backward",
            7,
            [feed_sum_grad, down_full, factor_row, chooser, choose, norm_gains],
            [
                shape((shard_rows, width)),
                shape((2, per_row, width)),
                shape((2, 8, width)),
                gathered,
            ],
            [
                pltpu.VMEM((row_tokens, 2 * units), f32),
                pltpu.VMEM((width, 2 * units), bf16),
                block,
                block,
                block,
                pltpu.VMEM((row_tokens, 2 * units), bf16),
                pltpu.SemaphoreType.DMA((8,)),
                *in_kernel,
                all_sems,
            ],
            [feed_out_parts],
            late=[gate_up, feed_full, attn_sum, middle, cotangent],
            late_outs=[shape((row_tokens, 2 * units), bf16)],
        )
        attn_sum_grad = attn_sum_grad.reshape(row_tokens, width)
    else:
        hidden_grad = dot(feed_sum_grad, down_full, 1, 0)
        pair_grad = jnp.concatenate(
            pair_point(hidden_grad, gate_up[:, :units], gate_up[:, units:]), axis=1
        )
        feed_input_grad = collect(split(dot(pair_grad, feed_full, 1, 1)))
        middle_grad, attn_block_grad, *grads = middle_back_point(
            feed_input_grad,
            attn_sum,
            middle,
            token_factor(1),
            token_factor(2),
            cotangent,
            gains[1],
            gains[2],
        )
        middle_factor, middle_row = by_image(*grads[:2]), jnp.stack(grads[2:])
        attn_sum_grad = in_place(spread(attn_block_grad))
        feed_out_other = swap_half(feed_out_parts)
    feed_out_sum = scatter_far(sum_half(feed_out_parts, feed_out_other))
    outer_grad = half(dot(feed_all, pair_grad, 0, 0))
    outer_both = lax.psum_scatter(
        outer_grad, "dp", scatter_dimension=0, tiled=True, axis_index_groups=far_groups()
    )
    mixed_grad = dot(out_full, gate(attn_sum_grad, outer_grad), 0, 1)
    out_parts = half(dot(attn_sum_grad, mixed, 0, 1)).reshape(dp_size // 2, 2, -1, local)
    query_two, text_key_grad, text_value_grad, text_gains = attention_call(
        functools.partial(cross_backward_kernel, heads),
        "cross_backward",
        [cross_meta, lengths],
        [
            (ids_row, True),
            (local_gains, False),
            (queries, True),
            (text_key_rows, False),
            (text_keys, False),
            (text_value_rows, False),
            (other_inv, True),
            (other_out, True),
            (mixed_grad, True),
            (text_key_raw, False),
        ],
        [(wide, True), (text_narrow, False), (text_narrow, False), (gain_shape, False)],
        [
            pltpu.VMEM((local, TILE), jnp.bfloat16),
            tile_sums,
            pltpu.VMEM((local, slots), jnp.float32),
            pltpu.VMEM((local, slots), jnp.float32),
            pltpu.VMEM((local, TILE), jnp.float32),
        ],
        row_tokens,
        25000,
    )
    triple_grad, own_gains = attention_call(
        functools.partial(self_backward_kernel, heads),
        "self_backward",
        [self_meta],
        [
            (ids_row, True),
            (ids_column, False),
            (local_gains, False),
            *tables,
            (queries, True),
            (key_rows, False),
            (keys, False),
            (value_rows, False),
            (own_inv, True),
            (own_out, True),
            (mixed_grad, True),
            (query_two, True),
            (projected, 0),
            (projected, 1),
        ],
        [
            (jax.ShapeDtypeStruct((3 * local, row_tokens), jnp.bfloat16), False),
            (gain_shape, False),
        ],
        [
            pltpu.VMEM((local, TILE), jnp.bfloat16),
            tile_sums,
            pltpu.VMEM((local, TILE), jnp.float32),
            pltpu.VMEM((local, row_tokens), jnp.float32),
            pltpu.VMEM((local, row_tokens), jnp.float32),
            pltpu.VMEM((local, TILE), jnp.float32),
        ],
        row_tokens,
        25000,
        [feed_out_sum],
    )
    in_parts = half(dot(attn_full, triple_grad, 0, 1)).reshape(dp_size // 2, 2, -1, 3 * local)

    if fused:
        latent_grad, enter_factor, enter_row, in_other = remote_call(
            enter_back_kernel,
            "enter_backward",
            10,
            [
                triple_grad,
                in_full,
                latents,
                factor_row,
                chooser,
                choose,
                middle_grad,
                norm_gains,
            ],
            [
                shape((shard_rows, width)),
                shape((1, per_row, width)),
                shape((1, 8, width)),
            ],
            [pltpu.VMEM((2 * shard_rows, 3 * local), bf16), *in_kernel, sum_sems],
            [in_parts],
        )
    else:
        attn_input_grad = collect(
            [
                dot(
                    lax.dynamic_slice_in_dim(triple_grad, owner(i) * shard_rows, shard_rows, 1),
                    in_full,
                    0,
                    1,
                )
                for i in range(tensor_size)
            ]
        )
        in_other = swap_half(in_parts)
        latent_grad, *grads = enter_back_point(
            attn_input_grad, source, token_factor(0), middle_grad, gains[0]
        )
        enter_factor, enter_row = by_image(grads[0]), grads[1][None]
    in_sum = scatter_far(sum_half(in_parts, in_other))

    columns = captions.shape[1]

    def caption_back(grad, carry, number, after):
        if not fused:
            parts = half(dot(in_place(spread(grad)), captions, 1, 0))
            parts = parts.reshape(dp_size // 2, 2, -1, columns)
            return (sum_half(parts, swap_half(parts)), *(swap_half(array) for array in carry))
        kept = (tensor_size, local // 2, columns)
        summed, _, *others = remote_call(
            text_kernel,
            "text_gradient",
            number,
            [grad, captions],
            [shape(kept, bf16), shape((tensor_size, local, slots), bf16)],
            [
                pltpu.VMEM(kept, f32),
                pltpu.VMEM(kept, bf16),
                pltpu.VMEM(kept, bf16),
                semaphores(5 * CHUNKS),
            ],
            carry,
            neighbour=True,
            after=after,
        )
        return (flat(summed), *others)

    value_grad, out_other = caption_back(text_value_grad, [out_parts], 8, [latent_grad])
    value_sum = scatter_far(
        jnp.concatenate([value_grad, sum_half(out_parts, out_other)], axis=1)
    )
    (key_grad,) = caption_back(text_key_grad, [], 9, [outer_both, value_grad])
    key_sum = scatter_far(key_grad)
    shared_rows = jnp.sum(
        jnp.concatenate([enter_row, middle_row, end_row]), axis=1
    )
    head_rows = jnp.stack(
        [own_gains[:, 0], own_gains[:, 128], text_gains[:, 128], text_gains[:, 0]]
    )
    head_full = lax.dynamic_update_slice(
        jnp.zeros((4, width), jnp.float32), head_rows, (jnp.zeros((), jnp.int32), offset)
    )
    channel_part = jnp.concatenate([shared_rows, head_full], axis=0)
    factor_image = jnp.concatenate([enter_factor, middle_factor, end_factor])
    factor_image = jnp.transpose(factor_image, (1, 0, 2))
    factor_image = jnp.transpose(
        factor_image.reshape(per_row, dp_size, tensor_size, own_columns), (2, 1, 0, 3)
    )
    channel_blocks = jnp.transpose(channel_part.reshape(8, dp_size, -1), (1, 0, 2))
    channel_blocks = channel_blocks.reshape(dp_size, -1, own_columns)
    payload = jnp.concatenate(
        [factor_image, jnp.broadcast_to(channel_blocks, (tensor_size, *channel_blocks.shape))],
        axis=2,
    )
    blocks = payload.shape[1:]
    outer_parts = outer_both.reshape(1, 2, -1, outer_both.shape[1])
    received, outer_other = remote_call(
        return_kernel,
        "modulation_return",
        1,
        [payload],
        [shape(blocks)],
        exchange_scratch([payload.shape, blocks, blocks]),
        [outer_parts],
        everyone=True,
        after=[in_sum],
    )
    in_sum, value_sum = gate(in_sum, received), gate(value_sum, received)
    feed_out_sum = gate(feed_out_sum, received)
    value_sum, out_sum = value_sum[:, :columns], value_sum[:, columns:]
    feed_in_sum = lax.dynamic_index_in_dim(outer_parts, dp_index % 2, 1, keepdims=False)[0]
    feed_in_sum = feed_in_sum.astype(f32) + outer_other[0].astype(f32)
    factor_grad = received[:, :per_row].reshape(images, own_columns)
    channel_sum = jnp.sum(received[:, per_row:], axis=0).reshape(channels.shape)
    modulator_sum = jnp.dot(augmented.astype(jnp.float32).T, factor_grad, precision=HIGH)

    def square(value):
        value = value.astype(f32)
        return jnp.sum(value * value)

    squares = (
        square(in_sum)
        + square(out_sum)
        + square(feed_in_sum)
        + square(feed_out_sum)
        + square(key_sum)
        + square(value_sum)
        + square(modulator_sum)
        + square(channel_sum) / tensor_size
    )
    in_sum = jnp.stack([in_sum[:, i * local : (i + 1) * local] for i in range(3)])
    feed_in_sum = jnp.stack([feed_in_sum[:, i * units : (i + 1) * units] for i in range(2)])
    caption_sum = jnp.stack([key_sum.T, value_sum.T])
    (squares,) = remote_call(
        total_kernel,
        "norm_exchange",
        2,
        [jnp.broadcast_to(squares, (8, 128))],
        [shape((8, 128))],
        exchange_scratch([(tensor_size, 8, 128), (dp_size, 8, 128), (8, 128)]),
        everyone=True,
    )
    grad_norm = jnp.sqrt(squares[0, 0])
    factor = CLIP / jnp.maximum(grad_norm, CLIP)
    results = [
        adamw(grad.astype(f32) * factor, weight, moment, second, DECAY, RATE)
        for grad, weight, moment, second in (
            (in_sum, attention_in, moment_attention_in, square_attention_in),
            (out_sum.T, attention_out, moment_attention_out, square_attention_out),
            (feed_in_sum, feed_in, moment_feed_in, square_feed_in),
            (feed_out_sum.T, feed_out, moment_feed_out, square_feed_out),
            (caption_sum, caption_in, moment_caption_in, square_caption_in),
            (modulator_sum, modulator, moment_modulator, square_modulator),
        )
    ]
    results.append(
        adamw(channel_sum * factor, channels, moment_channels, square_channels, 0.0, GAIN_RATE)
    )
    return (block_out, latent_grad, grad_norm, *(part for result in results for part in result))


def solution(mesh):
    return jax.shard_map(
        body,
        mesh=mesh,
        in_specs=(
            P(("dp", "tensor"), None),
            P(("dp", "tensor"), None),
            P("dp", "tensor"),
            P(),
            P("dp", None),
            P("dp", None),
            P("dp", None),
            P("dp", None),
            P(None, "dp", "tensor"),
            P("tensor", "dp"),
            P(None, "dp", "tensor"),
            P("tensor", "dp"),
            P(None, "tensor", "dp"),
            P(None, ("dp", "tensor")),
            P(None, "dp"),
            P(None, "dp", "tensor"),
            P(None, "dp", "tensor"),
            P("tensor", "dp"),
            P("tensor", "dp"),
            P(None, "dp", "tensor"),
            P(None, "dp", "tensor"),
            P("tensor", "dp"),
            P("tensor", "dp"),
            P(None, "tensor", "dp"),
            P(None, "tensor", "dp"),
            P(None, ("dp", "tensor")),
            P(None, ("dp", "tensor")),
            P(None, "dp"),
            P(None, "dp"),
        ),
        out_specs=(
            P(("dp", "tensor"), None),
            P(("dp", "tensor"), None),
            P(),
            P(None, "dp", "tensor"),
            P(None, "dp", "tensor"),
            P(None, "dp", "tensor"),
            P("tensor", "dp"),
            P("tensor", "dp"),
            P("tensor", "dp"),
            P(None, "dp", "tensor"),
            P(None, "dp", "tensor"),
            P(None, "dp", "tensor"),
            P("tensor", "dp"),
            P("tensor", "dp"),
            P("tensor", "dp"),
            P(None, "tensor", "dp"),
            P(None, "tensor", "dp"),
            P(None, "tensor", "dp"),
            P(None, ("dp", "tensor")),
            P(None, ("dp", "tensor")),
            P(None, ("dp", "tensor")),
            P(None, "dp"),
            P(None, "dp"),
            P(None, "dp"),
        ),
        check_vma=False,
    )
```

```python
import functools
import math

import jax
import jax.numpy as jnp
from jax import lax
from jax.experimental import pallas as pl
from jax.experimental.pallas import tpu as pltpu
from jax.sharding import PartitionSpec as P

HEAD = 64
CAP = 256
STEP = 10


EPS = 1e-06
NEG = -1e30
THETA = 10000.0
BETA1 = 0.9
BETA2 = 0.95
RATE = 0.05
GAIN_RATE = 0.8
DECAY = 0.1
ADAM_EPS = 1e-08
CLIP = 1.0
HIGH = lax.Precision.HIGHEST


def half(value):
    return value.astype(jnp.bfloat16)


TILE = 256
AHEAD = 2
LOG2E = 1.0 / math.log(2.0)
MESH = pl.DeviceIdType.MESH


def dot(left, right, left_dim, right_dim):
    return lax.dot_general(
        left, right, (((left_dim,), (right_dim,)), ((), ())), preferred_element_type=jnp.float32
    )


def rms_parts(value, axis=-1):
    inverse = lax.rsqrt(jnp.mean(value * value, axis=axis, keepdims=True) + EPS)
    return (value * inverse, inverse)


def rms_back(normed, inverse, grad, axis=-1):
    return inverse * (grad - normed * jnp.mean(grad * normed, axis=axis, keepdims=True))


def rope_tables(rows, columns):
    quarter = HEAD // 4
    frequency = THETA ** (-jnp.arange(quarter, dtype=jnp.float32) / quarter)
    angles = jnp.concatenate(
        [
            frequency[:, None] * rows.astype(jnp.float32)[None, :],
            frequency[:, None] * columns.astype(jnp.float32)[None, :],
        ],
        axis=0,
    )
    return (jnp.cos(angles), jnp.sin(angles))


def gate_kernel(value, after, out):
    del value, after, out


def gate(value, after):
    anywhere = pl.BlockSpec(memory_space=pl.ANY)
    return pl.pallas_call(
        gate_kernel,
        out_shape=jax.ShapeDtypeStruct(value.shape, value.dtype),
        in_specs=[anywhere, anywhere],
        out_specs=anywhere,
        input_output_aliases={0: 0},
        name="gate",
    )(value, after)


def near_swap(value):
    return lax.ppermute(value, "dp", [(i, i ^ 1) for i in range(lax.axis_size("dp"))])


def far_groups():
    count = lax.axis_size("dp")
    return [list(range(near, count, 2)) for near in range(2)]


def gather_far(value):
    return lax.all_gather(value, "dp", axis=0, tiled=True, axis_index_groups=far_groups())


def flat(blocks):
    return blocks.reshape(-1, blocks.shape[-1])


def join_near(own, other, count):
    odd = lax.axis_index("dp") % 2
    own = own.reshape(-1, count, own.shape[1])
    other = other.reshape(own.shape)
    return flat(
        jnp.stack([jnp.where(odd == 0, own, other), jnp.where(odd == 0, other, own)], axis=1)
    )


def swap_half(parts):
    odd = lax.axis_index("dp") % 2
    send = lax.dynamic_index_in_dim(parts, 1 - odd, 1, keepdims=False)
    return near_swap(send.reshape(-1, send.shape[2])).reshape(send.shape)


def sum_half(parts, other):
    odd = lax.axis_index("dp") % 2
    keep = lax.dynamic_index_in_dim(parts, odd, 1, keepdims=False)
    return flat(half(keep.astype(jnp.float32) + other.astype(jnp.float32)))


def scatter_far(value):
    return lax.psum_scatter(
        value, "dp", scatter_dimension=0, tiled=True, axis_index_groups=far_groups()
    )


def swap_tensor(value, bits):
    return lax.ppermute(value, "tensor", [(i, i ^ bits) for i in range(lax.axis_size("tensor"))])


def owner(place):
    if lax.axis_size("tensor") == 4:
        return lax.axis_index("tensor") ^ place
    return jnp.int32(place)


def spread(value):
    count = lax.axis_size("tensor")
    if count == 4:
        near = swap_tensor(value, 1)
        far = swap_tensor(value, 2)
        return [value, near, far, swap_tensor(far, 1)]
    whole = lax.all_gather(value, "tensor", axis=0, tiled=False)
    return [whole[i] for i in range(count)]


def collect_near(parts):
    if len(parts) == 4:
        rows = parts[0].shape[0]
        sent = swap_tensor(half(jnp.concatenate([parts[3], parts[1]], axis=0)), 1)
        sent = sent.astype(jnp.float32)
        return (parts[0] + sent[rows:], half(parts[2] + sent[:rows]))
    return (half(jnp.concatenate(parts, axis=0)),)


def collect_far(sums):
    if len(sums) == 2:
        return sums[0] + swap_tensor(sums[1], 2).astype(jnp.float32)
    return lax.psum_scatter(
        sums[0], "tensor", scatter_dimension=0, tiled=True
    ).astype(jnp.float32)


def collect(parts):
    return collect_far(collect_near(parts))


def in_place(blocks):
    if len(blocks) == 4:
        stacked = jnp.stack(blocks)
        mine = lax.axis_index("tensor")
        blocks = [
            lax.dynamic_index_in_dim(stacked, mine ^ i, 0, keepdims=False)
            for i in range(len(blocks))
        ]
    return jnp.concatenate(blocks, axis=0)


def dp_neighbour():
    mine = lax.axis_index("dp")
    return mine + 1 - 2 * (mine % 2)


def meet(everyone, neighbour):
    barrier = pltpu.get_barrier_semaphore()
    if everyone:
        others = [
            {axis: (lax.axis_index(axis) + step) % lax.axis_size(axis)}
            for axis in ("dp", "tensor")
            for step in range(1, lax.axis_size(axis))
        ]
    else:
        _, near, far, _ = row_peers()
        others = [{"tensor": near}, {"tensor": far}]
        if neighbour:
            others.append({"dp": dp_neighbour()})
    for other in others:
        pl.semaphore_signal(barrier, inc=1, device_id=other, device_id_type=MESH)
    pl.semaphore_wait(barrier, len(others))


def remote_call(
    kernel,
    name,
    number,
    operands,
    outs,
    scratch,
    carry=(),
    everyone=False,
    neighbour=False,
    after=(),
    late=(),
    late_outs=(),
):
    copies = sum(array.shape[0] if len(array.shape) == 4 else 1 for array in carry)
    traded = [
        jax.ShapeDtypeStruct(
            (array.shape[0], *array.shape[2:]) if len(array.shape) == 4 else array.shape,
            array.dtype,
        )
        for array in carry
    ]

    def run(*refs):
        refs = list(refs)
        ins = [refs.pop(0) for _ in (*operands, *late)]
        sources = [refs.pop(0) for _ in carry]
        del refs[: len(after)]
        results = [refs.pop(0) for _ in (*outs, *late_outs)]
        targets = [refs.pop(0) for _ in carry]
        meet(everyone, neighbour or bool(carry))
        started = []
        if carry:
            sems = refs.pop()
            other = dp_neighbour()
            pairs = []
            for source, target in zip(sources, targets):
                if len(source.shape) == 2:
                    pairs.append((source, target))
                else:
                    pairs += [
                        (source.at[i, other % 2], target.at[i]) for i in range(source.shape[0])
                    ]
            for i, (source, target) in enumerate(pairs):
                copy = pltpu.make_async_remote_copy(
                    src_ref=source,
                    dst_ref=target,
                    send_sem=sems.at[0, i],
                    recv_sem=sems.at[1, i],
                    device_id={"dp": other},
                    device_id_type=MESH,
                )
                copy.start()
                started.append(copy)
        kernel(*ins, *results, *refs)
        for copy in started:
            copy.wait()

    whole = pl.BlockSpec(memory_space=pltpu.VMEM)
    anywhere = pl.BlockSpec(memory_space=pl.ANY)
    return pl.pallas_call(
        run,
        out_shape=[*outs, *late_outs, *traded],
        in_specs=[whole] * len(operands) + [anywhere] * (len(late) + len(carry) + len(after)),
        out_specs=[whole] * len(outs) + [anywhere] * (len(late_outs) + len(carry)),
        scratch_shapes=[
            *scratch,
            *([pltpu.SemaphoreType.DMA((2, copies))] if carry else []),
        ],
        compiler_params=pltpu.CompilerParams(
            collective_id=number, has_side_effects=True, vmem_limit_bytes=60 * 1024 * 1024
        ),
        cost_estimate=pl.CostEstimate(flops=1 << 20, bytes_accessed=1 << 20, transcendentals=0),
        name=name,
    )(*operands, *late, *carry, *after)


def send_blocks(axis, pick, target, send_sem, recv_sem):
    count = lax.axis_size(axis)
    mine = lax.axis_index(axis)

    def copy(other, place):
        return pltpu.make_async_remote_copy(
            src_ref=pick(other),
            dst_ref=target.at[place],
            send_sem=send_sem.at[other],
            recv_sem=recv_sem.at[place],
            device_id={axis: other},
            device_id_type=MESH,
        )

    others = [(mine + step) % count for step in range(1, count)]
    for other in others:
        copy(other, mine).start()
    for other in others:
        copy(other, mine).wait_send()
        copy(other, other).wait_recv()


def spread_kernel(source, target, middle, send_dp, recv_dp, send_tensor, recv_tensor):
    mine = lax.axis_index("dp")
    middle[mine] = source[mine]
    send_blocks("dp", lambda other: source.at[other], middle, send_dp, recv_dp)
    target[lax.axis_index("tensor")] = middle[...]
    send_blocks("tensor", lambda other: middle, target, send_tensor, recv_tensor)


def return_kernel(
    source, target, middle, summed, last, send_dp, recv_dp, send_tensor, recv_tensor
):
    place = lax.axis_index("tensor")
    middle[place] = source[place]
    send_blocks("tensor", lambda other: source.at[other], middle, send_tensor, recv_tensor)
    total = middle[0]
    for other in range(1, lax.axis_size("tensor")):
        total += middle[other]
    summed[...] = total
    mine = lax.axis_index("dp")
    last[mine] = summed[mine]
    send_blocks("dp", lambda other: summed.at[other], last, send_dp, recv_dp)
    target[...] = last[...]


def total_kernel(source, target, near, far, part, send_dp, recv_dp, send_tensor, recv_tensor):
    near[lax.axis_index("tensor")] = source[...]
    send_blocks("tensor", lambda other: source, near, send_tensor, recv_tensor)
    part[...] = jnp.sum(near[...], axis=0)
    far[lax.axis_index("dp")] = part[...]
    send_blocks("dp", lambda other: part, far, send_dp, recv_dp)
    target[...] = jnp.sum(far[...], axis=0)


def exchange_scratch(shapes):
    sizes = (lax.axis_size("dp"),) * 2 + (lax.axis_size("tensor"),) * 2
    return [pltpu.VMEM(shape, jnp.float32) for shape in shapes] + [
        pltpu.SemaphoreType.DMA((size,)) for size in sizes
    ]


CHUNKS = 4


def row_peers():
    mine = lax.axis_index("tensor")
    near = mine + 1 - 2 * (mine % 2)
    return (mine, near, (mine + 2) % 4, (near + 2) % 4)


def remote(source, target, sems, index, other):
    return pltpu.make_async_remote_copy(
        src_ref=source,
        dst_ref=target,
        send_sem=sems.at[0, index],
        recv_sem=sems.at[1, index],
        device_id={"tensor": other},
        device_id_type=MESH,
    )


def chunk_rows(total):
    size = total // CHUNKS
    return [slice(i * size, (i + 1) * size) for i in range(CHUNKS)]


def sum_blocks(partial, finish, work, sems, by_columns=False):
    mine, near, far, both = row_peers()
    send_both, send_near, near_both, near_own, send_far, far_own, base = work
    size, width = base.shape[0] // 2, base.shape[1]
    step = width // CHUNKS
    if by_columns:
        chunks = [(slice(None), slice(i * step, (i + 1) * step)) for i in range(CHUNKS)]
    else:
        chunks = [(rows, slice(None)) for rows in chunk_rows(size)]

    def terms(block, place):
        rows, columns = place
        first, count = rows.start or 0, size if by_columns else size // CHUNKS
        start = pl.multiple_of((block % 2) * size + first, count)
        return base[pl.ds(start, count), columns]

    def hand_over(chip, block, source, target, kind):
        copies = []
        if not by_columns:
            partial(chip, base, None)
        for i, place in enumerate(chunks):
            if by_columns:
                partial(chip, base, place[1])
            source[place] = half(terms(block, place))
            copies.append(
                remote(source.at[place], target.at[place], sems, CHUNKS * kind + i, near)
            )
            copies[i].start()
            if by_columns and i:
                yield i - 1, copies[i - 1]
        for i in range(CHUNKS - 1 if by_columns else 0, CHUNKS):
            yield i, copies[i]

    across = []
    for i, copy in hand_over(far // 2, both, send_both, near_both, 0):
        place = chunks[i]
        copy.wait()
        send_far[place] = half(terms(far, place) + near_both[place].astype(jnp.float32))
        across.append(
            remote(send_far.at[place], far_own.at[place], sems, 2 * CHUNKS + i, far)
        )
        across[i].start()
    for i, copy in hand_over(mine // 2, near, send_near, near_own, 1):
        place = chunks[i]
        copy.wait()
        across[i].wait()
        finish(
            i,
            place[1] if by_columns else place[0],
            terms(mine, place)
            + near_own[place].astype(jnp.float32)
            + far_own[place].astype(jnp.float32),
        )


SUM_SEMAPHORES = 3 * CHUNKS


def chip_rows(chip, size):
    return pl.ds(pl.multiple_of(chip * 2 * size, 2 * size), 2 * size)


def sum_scratch(rows, columns):
    narrow = pltpu.VMEM((rows, columns), jnp.bfloat16)
    return [narrow] * 6 + [pltpu.VMEM((2 * rows, columns), jnp.float32)]


class Spread:
    def __init__(self, gathered, sems, base):
        self.gathered, self.sems, self.base = gathered, sems, base
        self.mine, self.near, self.far, self.both = row_peers()
        self.chunks = chunk_rows(gathered.shape[1])
        self.started = []

    def copy(self, block, i, kind, other):
        part = self.gathered.at[block, self.chunks[i]]
        return remote(part, part, self.sems, self.base + CHUNKS * kind + i, other)

    def offer(self, i, value):
        self.gathered[self.mine, self.chunks[i], :] = value
        for kind, other in ((0, self.far), (1, self.near)):
            copy = self.copy(self.mine, i, kind, other)
            copy.start()
            self.started.append(copy)

    def settle(self):
        for i in range(CHUNKS):
            self.copy(self.far, i, 0, self.far).wait_recv()
            forward = self.copy(self.far, i, 2, self.near)
            forward.start()
            self.started.append(forward)
        for i in range(CHUNKS):
            self.copy(self.near, i, 1, self.near).wait_recv()
            self.copy(self.both, i, 2, self.near).wait_recv()
        for copy in self.started:
            copy.wait_send()


def tiles_of(total, size):
    def run(step):
        def body(index, carry):
            step(pl.ds(pl.multiple_of(index * size, size), size))
            return carry

        lax.fori_loop(0, total // size, body, 0)

    return run


def pick(chooser, factor, which, rows):
    width = factor.shape[1] // 4
    return jnp.dot(
        chooser[rows, :],
        factor[:, which * width : (which + 1) * width],
        precision=HIGH,
        preferred_element_type=jnp.float32,
    )


def add_up(place, target, value):
    target[place] += jnp.sum(value.reshape(-1, 8, value.shape[1]), axis=0)


def add_images(choose, i, place, target, value):
    target[place] += jnp.dot(
        choose[i], value, precision=HIGH, preferred_element_type=jnp.float32
    )


def enter_kernel(latents, factor, chooser, gain, gathered, sems):
    share = Spread(gathered, sems, 0)
    for i, rows in enumerate(share.chunks):
        scale = pick(chooser, factor, 0, rows)
        share.offer(i, enter_point(latents[rows, :].astype(jnp.float32), scale, gain[0:1]))
    share.settle()


def project_kernel(weight, captions, total, *rest):
    work, sems = rest[:-1], rest[-1]
    local = total.shape[0]

    def partial(chip, base, columns):
        base[:, columns] = dot(weight[chip_rows(chip, local), :], captions[columns, :], 1, 1)

    def finish(i, columns, value):
        total[:, columns] = value

    sum_blocks(partial, finish, work, sems, by_columns=True)


def transposed_partial(left, weight, lhs, size):
    def partial(chip, base, _):
        lhs[...] = half(left[:, chip_rows(chip, size)].astype(jnp.float32).T)

        @tiles_of(weight.shape[0], 512)
        def _(columns):
            base[:, columns] = dot(lhs[...], weight[columns, :], 1, 1)

    return partial


def attention_out_kernel(
    mixed, weight, latents, factor, chooser, gain, summed, middle, gathered, *rest
):
    lhs, work, sems = rest[0], rest[1:-1], rest[-1]
    share = Spread(gathered, sems, SUM_SEMAPHORES)

    def finish(i, rows, value):
        summed[rows, :] = value
        middle[rows, :], out = middle_point(
            value,
            latents[rows, :].astype(jnp.float32),
            pick(chooser, factor, 1, rows),
            pick(chooser, factor, 2, rows),
            gain[1:2],
            gain[2:3],
        )
        share.offer(i, out)

    sum_blocks(transposed_partial(mixed, weight, lhs, latents.shape[0]), finish, work, sems)
    share.settle()


def begin_copies(pairs, sems):
    copies = [
        pltpu.make_async_copy(source, target, sems.at[i])
        for i, (source, target) in enumerate(pairs)
    ]
    for copy in copies:
        copy.start()
    return copies


def feed_kernel(
    inputs, feed, factor, chooser, choose, gain, down_far, middle_far, cotangent_far,
    hidden, out, factor_grad, row_grad, gathered, gate_far, *rest
):
    gate_up, down, middle, cotangent, moves = rest[:5]
    work, sems = rest[5:-1], rest[-1]
    size = middle.shape[0]
    units = hidden.shape[1]
    loads = begin_copies(
        [(down_far, down), (middle_far, middle), (cotangent_far, cotangent)], moves
    )
    saves = []
    factor_grad[...] = jnp.zeros_like(factor_grad)
    row_grad[...] = jnp.zeros_like(row_grad)

    def partial(chip, base, _):
        own = chip_rows(chip, size)

        @tiles_of(units, 512)
        def _(columns):
            other = pl.ds(pl.multiple_of(columns.start + units, 512), 512)
            first = dot(inputs[own, :], feed[:, columns], 1, 0)
            second = dot(inputs[own, :], feed[:, other], 1, 0)
            gate_up[own, columns] = first
            gate_up[own, other] = second
            hidden[own, columns] = half(first * jax.nn.sigmoid(first) * second)

        save = pltpu.make_async_copy(
            gate_up.at[own], gate_far.at[own], moves.at[3 + len(saves)]
        )
        save.start()
        saves.append(save)
        for load in loads[:1] if len(saves) == 1 else loads[1:]:
            load.wait()

        @tiles_of(down.shape[0], 512)
        def _(columns):
            base[:, columns] = dot(hidden[own, :], down[columns, :], 1, 1)

    share = Spread(gathered, sems, SUM_SEMAPHORES)

    def finish(i, rows, value):
        out[rows, :], back, gate_grad, row = end_point(
            value,
            middle[rows, :],
            pick(chooser, factor, 3, rows),
            cotangent[rows, :],
            gain[3:4],
        )
        share.offer(i, back)
        add_images(choose, i, 0, factor_grad, gate_grad)
        add_up(0, row_grad, row)

    sum_blocks(partial, finish, work, sems)
    share.settle()
    for save in saves:
        save.wait()


def feed_back_kernel(
    back, down, factor, chooser, choose, gain, gate_far, feed_far, summed_far, middle_far,
    cotangent_far, middle_grad, factor_grad, row_grad, gathered, pair_far, *rest
):
    gate_up, feed, summed, middle, cotangent, pair, moves = rest[:7]
    work, sems = rest[7:-1], rest[-1]
    size = middle.shape[0]
    units = down.shape[1]
    mine, _, far, _ = row_peers()
    first_rows, last_rows = chip_rows(far // 2, size), chip_rows(mine // 2, size)
    loads = begin_copies(
        [
            (gate_far.at[first_rows], gate_up.at[first_rows]),
            (feed_far, feed),
            (gate_far.at[last_rows], gate_up.at[last_rows]),
            (summed_far, summed),
            (middle_far, middle),
            (cotangent_far, cotangent),
        ],
        moves,
    )
    saves = []
    factor_grad[...] = jnp.zeros_like(factor_grad)
    row_grad[...] = jnp.zeros_like(row_grad)

    def partial(chip, base, _):
        own = chip_rows(chip, size)
        loads[2 if saves else 0].wait()

        @tiles_of(units, 512)
        def _(columns):
            other = pl.ds(pl.multiple_of(columns.start + units, 512), 512)
            grad = dot(back[own, :], down[:, columns], 1, 0)
            first, second = gate_up[own, columns], gate_up[own, other]
            pair[own, columns], pair[own, other] = pair_point(grad, first, second)

        save = pltpu.make_async_copy(pair.at[own], pair_far.at[own], moves.at[6 + len(saves)])
        save.start()
        saves.append(save)
        for load in loads[1:2] if len(saves) == 1 else loads[3:]:
            load.wait()

        @tiles_of(feed.shape[0], 512)
        def _(columns):
            base[:, columns] = dot(pair[own, :], feed[columns, :], 1, 1)

    share = Spread(gathered, sems, SUM_SEMAPHORES)

    def finish(i, rows, value):
        middle_grad[rows, :], out, gate_grad, scale_grad, first_row, second_row = (
            middle_back_point(
                value,
                summed[rows, :],
                middle[rows, :],
                pick(chooser, factor, 1, rows),
                pick(chooser, factor, 2, rows),
                cotangent[rows, :],
                gain[1:2],
                gain[2:3],
            )
        )
        share.offer(i, out)
        add_images(choose, i, 0, factor_grad, gate_grad)
        add_images(choose, i, 1, factor_grad, scale_grad)
        add_up(0, row_grad, first_row)
        add_up(1, row_grad, second_row)

    sum_blocks(partial, finish, work, sems)
    share.settle()
    for save in saves:
        save.wait()


def enter_back_kernel(
    triple, weight, latents, factor, chooser, choose, middle_grad, gain,
    latent_grad, factor_grad, row_grad, *rest
):
    lhs, work, sems = rest[0], rest[1:-1], rest[-1]
    factor_grad[...] = jnp.zeros_like(factor_grad)
    row_grad[...] = jnp.zeros_like(row_grad)

    def finish(i, rows, value):
        latent_grad[rows, :], scale_grad, row = enter_back_point(
            value,
            latents[rows, :].astype(jnp.float32),
            pick(chooser, factor, 0, rows),
            middle_grad[rows, :],
            gain[0:1],
        )
        add_images(choose, i, 0, factor_grad, scale_grad)
        add_up(0, row_grad, row)

    sum_blocks(transposed_partial(triple, weight, lhs, latents.shape[0]), finish, work, sems)


def text_kernel(
    own, captions_far, summed, gathered, kept, sent, arrived, captions, moves, sems
):
    (load,) = begin_copies([(captions_far, captions)], moves)
    mine, near, far, both = row_peers()
    other = dp_neighbour()
    odd = 1 - other % 2
    size = own.shape[0] // CHUNKS
    each = CHUNKS // 2
    started = []

    def part(k):
        base = (1 - odd) if k < each else odd
        return pl.ds(pl.multiple_of((base * each + k % each) * size, size), size)

    def move(block, k, kind, device):
        rows = gathered.at[block, part(k)]
        return remote(rows, rows, sems, CHUNKS * kind + k, device)

    def across(block, order, k):
        rows = pl.ds(k * size, size)
        return pltpu.make_async_remote_copy(
            src_ref=sent.at[block, rows],
            dst_ref=arrived.at[block, rows],
            send_sem=sems.at[0, 3 * CHUNKS + order * each + k],
            recv_sem=sems.at[1, 3 * CHUNKS + order * each + k],
            device_id={"dp": other},
            device_id_type=MESH,
        )

    def begin(copy):
        copy.start()
        started.append(copy)

    def work(block, order, k):
        value = dot(gathered[block, part(k), :], captions[...], 1, 0)
        rows = pl.ds((k % each) * size, size)
        if k < each:
            sent[block, rows, :] = half(value)
            begin(across(block, order, k))
        else:
            kept[block, rows, :] = value

    for k in range(CHUNKS):
        gathered[mine, part(k), :] = own[part(k), :]
        begin(move(mine, k, 0, far))
        begin(move(mine, k, 1, near))
    load.wait()
    for k in range(CHUNKS):
        work(mine, 0, k)
    for k in range(CHUNKS):
        move(near, k, 1, near).wait_recv()
        work(near, 1, k)
    for k in range(CHUNKS):
        move(far, k, 0, far).wait_recv()
        begin(move(far, k, 2, near))
        work(far, 2, k)
        if k:
            move(both, k - 1, 2, near).wait_recv()
            work(both, 3, k - 1)
    move(both, CHUNKS - 1, 2, near).wait_recv()
    work(both, 3, CHUNKS - 1)
    for order, block in enumerate((mine, near, far, both)):
        for k in range(each):
            across(block, order, k).wait_recv()
            rows = pl.ds(k * size, size)
            summed[block, rows, :] = half(
                kept[block, rows, :] + arrived[block, rows, :].astype(jnp.float32)
            )
    for copy in started:
        copy.wait_send()


def enter_point(source, scale, gain):
    normed, _ = rms_parts(source)
    return half(normed * gain * (1.0 + scale))


def middle_point(summed, source, gate, scale, first_gain, second_gain):
    normed, _ = rms_parts(summed)
    middle = source + jnp.tanh(gate) * (normed * first_gain)
    return (middle, enter_point(middle, scale, second_gain))


def end_point(summed, middle, gate, cotangent, gain):
    normed, inverse = rms_parts(summed)
    turned = jnp.tanh(gate)
    branch = normed * gain
    grad = turned * cotangent
    return (
        middle + turned * branch,
        half(rms_back(normed, inverse, grad * gain)),
        cotangent * branch * (1.0 - turned * turned),
        grad * normed,
    )


def pair_point(grad, first, second):
    sigmoid = jax.nn.sigmoid(first)
    return (
        half(grad * second * (sigmoid + first * sigmoid * (1.0 - sigmoid))),
        half(grad * (first * sigmoid)),
    )


def middle_back_point(
    input_grad, summed, middle, gate, scale, cotangent, first_gain, second_gain
):
    normed, inverse = rms_parts(middle)
    gained = input_grad * (1.0 + scale)
    middle_grad = cotangent + rms_back(normed, inverse, gained * second_gain)
    scale_grad, second_row = input_grad * normed * second_gain, gained * normed
    normed, inverse = rms_parts(summed)
    turned = jnp.tanh(gate)
    branch = turned * middle_grad
    return (
        middle_grad,
        half(rms_back(normed, inverse, branch * first_gain)),
        middle_grad * (normed * first_gain) * (1.0 - turned * turned),
        scale_grad,
        branch * normed,
        second_row,
    )


def enter_back_point(input_grad, source, scale, middle_grad, gain):
    normed, inverse = rms_parts(source)
    gained = input_grad * (1.0 + scale)
    return (
        middle_grad + rms_back(normed, inverse, gained * gain),
        input_grad * normed * gain,
        gained * normed,
    )


def spans(heads):
    return [slice(head * HEAD, (head + 1) * HEAD) for head in range(heads)]


def head_norm(value):
    inverse = lax.rsqrt(jnp.mean(value * value, axis=0, keepdims=True) + EPS)
    return (value * inverse, inverse)


def head_back(normed, inverse, grad):
    return inverse * (grad - normed * jnp.mean(grad * normed, axis=0, keepdims=True))


def turn(value, cosine, sine):
    middle = HEAD // 2
    first, second = value[:middle], value[middle:]
    return jnp.concatenate(
        [first * cosine - second * sine, second * cosine + first * sine], axis=0
    )


def self_bias(step, ids_row, ids_column):
    start = pl.multiple_of(step * TILE, TILE)
    return jnp.where(ids_column[pl.ds(start, TILE), :] == ids_row[...], 0.0, NEG)


def cross_bias(step, ids_row, lengths):
    slots = lax.broadcasted_iota(jnp.int32, (TILE, 1), 0) < lengths[step]
    return jnp.where(slots & (ids_row[...] == step), 0.0, NEG)


def attend_tile(heads, meta, bias_of, query, key_rows, value, out, total, inv_ref):
    base = 2 * pl.program_id(0)
    factor = HEAD ** (-0.5) * LOG2E
    out[...] = jnp.zeros_like(out)
    total[...] = jnp.zeros_like(total)

    def step(index, carry):
        bias = bias_of(index)
        rows = pl.ds(pl.multiple_of(index * TILE, TILE), TILE)
        scores = [
            dot(key_rows[head, rows, :], query[span, :], 1, 0)
            for head, span in enumerate(spans(heads))
        ]
        for head, span in enumerate(spans(heads)):
            expo = jnp.exp2(scores[head] * factor + bias)
            total[head] += jnp.sum(expo.reshape(TILE // 8, 8, TILE), axis=0)
            out[span, :] += dot(value[span, rows], half(expo), 1, 0)
        return carry

    lax.fori_loop(meta[base], meta[base + 1], step, 0)
    for head, span in enumerate(spans(heads)):
        inverse = 1.0 / jnp.sum(total[head], axis=0, keepdims=True)
        inv_ref[head] = jnp.broadcast_to(inverse, (8, TILE))
        out[span, :] = out[span, :] * inverse


def attend_back_tile(
    heads, meta, bias_of, query, key_rows, key, value_rows, inv_ref, out, back, dq, dk, dv, centre
):
    base = 2 * pl.program_id(0)
    scale = HEAD ** (-0.5)
    dq[...] = jnp.zeros_like(dq)
    for head, span in enumerate(spans(heads)):
        both = out[span, :] * back[span, :].astype(jnp.float32)
        centre[head] = jnp.broadcast_to(jnp.sum(both, axis=0, keepdims=True), (8, TILE))

    def step(index, carry):
        bias = bias_of(index)
        rows = pl.ds(pl.multiple_of(index * TILE, TILE), TILE)
        def products(head):
            span = spans(heads)[head]
            return (
                dot(key_rows[head, rows, :], query[span, :], 1, 0),
                dot(value_rows[head, rows, :], back[span, :], 1, 0),
            )

        ahead = [products(head) for head in range(min(AHEAD, heads))]
        for head, span in enumerate(spans(heads)):
            scores, prob_grad = ahead.pop(0)
            if head + AHEAD < heads:
                ahead.append(products(head + AHEAD))
            probs = jnp.exp2(scores * (scale * LOG2E) + bias)
            probs = probs * inv_ref[head, 0:1, :]
            score_grad = half(probs * (prob_grad - centre[head, 0:1, :]))
            dv[span, rows] += dot(back[span, :], half(probs), 1, 1)
            dk[span, rows] += dot(query[span, :], score_grad, 1, 1) * scale
            dq[span, :] += dot(key[span, rows], score_grad, 1, 0) * scale
        return carry

    lax.fori_loop(meta[base], meta[base + 1], step, 0)


def self_forward_kernel(
    heads,
    meta,
    ids_row,
    ids_column,
    gain,
    cosine,
    sine,
    cosine_all,
    sine_all,
    raw_query,
    raw_key,
    raw_value,
    query,
    key,
    key_rows,
    value_rows,
    out,
    inv_ref,
    value,
    total,
):
    local = heads * HEAD

    @pl.when(pl.program_id(0) == 0)
    def _():
        for head, span in enumerate(spans(heads)):
            normed, _ = head_norm(raw_key[span, :])
            turned = turn(normed * gain[span, 1:2], cosine_all[...], sine_all[...])
            key[span, :] = half(turned)
            key_rows[head] = half(turned.T)
            plain = raw_value[span, :]
            value[span, :] = half(plain)
            value_rows[head] = half(plain.T)

    for span in spans(heads):
        normed, _ = head_norm(raw_query[span, :])
        query[span, :] = half(turn(normed * gain[span, 0:1], cosine[...], sine[...]))
    attend_tile(
        heads,
        meta,
        lambda index: self_bias(index, ids_row, ids_column),
        query,
        key_rows,
        value,
        out,
        total,
        inv_ref,
    )


def cross_forward_kernel(
    heads,
    meta,
    lengths,
    ids_row,
    gain,
    query,
    own_out,
    raw_key,
    raw_value,
    key,
    key_rows,
    value_rows,
    out,
    inv_ref,
    mixed,
    value,
    total,
):
    @pl.when(pl.program_id(0) == 0)
    def _():
        for head, span in enumerate(spans(heads)):
            normed, _ = head_norm(raw_key[span, :])
            normed = normed * gain[span, 2:3]
            key[span, :] = half(normed)
            key_rows[head] = half(normed.T)
            plain = raw_value[span, :]
            value[span, :] = half(plain)
            value_rows[head] = half(plain.T)

    attend_tile(
        heads,
        meta,
        lambda index: cross_bias(index, ids_row, lengths),
        query,
        key_rows,
        value,
        out,
        total,
        inv_ref,
    )
    mixed[...] = half(own_out[...] + jnp.tanh(gain[:, 3:4]) * out[...])


def cross_backward_kernel(
    heads,
    meta,
    lengths,
    ids_row,
    gain,
    query,
    key_rows,
    key,
    value_rows,
    inv_ref,
    out,
    mixed_grad,
    raw_key,
    dq,
    dk,
    dv,
    gain_grad,
    back,
    centre,
    dk_sum,
    dv_sum,
    gate_sum,
):
    place = pl.program_id(0)

    @pl.when(place == 0)
    def _():
        dk_sum[...] = jnp.zeros_like(dk_sum)
        dv_sum[...] = jnp.zeros_like(dv_sum)
        gate_sum[...] = jnp.zeros_like(gate_sum)

    gate = jnp.tanh(gain[:, 3:4])
    back[...] = half(gate * mixed_grad[...])
    gate_sum[...] += mixed_grad[...] * out[...]
    attend_back_tile(
        heads,
        meta,
        lambda index: cross_bias(index, ids_row, lengths),
        query,
        key_rows,
        key,
        value_rows,
        inv_ref,
        out,
        back,
        dq,
        dk_sum,
        dv_sum,
        centre,
    )

    @pl.when(place == pl.num_programs(0) - 1)
    def _():
        dv[...] = half(dv_sum[...])
        gate_grad = jnp.sum(gate_sum[...], axis=1, keepdims=True) * (1.0 - gate * gate)
        gain_grad[:, 0:128] = jnp.broadcast_to(gate_grad, (heads * HEAD, 128))
        for span in spans(heads):
            normed, inverse = head_norm(raw_key[span, :])
            grad = dk_sum[span, :]
            summed = jnp.sum(grad * normed, axis=1, keepdims=True)
            gain_grad[span, 128:256] = jnp.broadcast_to(summed, (HEAD, 128))
            dk[span, :] = half(head_back(normed, inverse, grad * gain[span, 2:3]))


def self_backward_kernel(
    heads,
    meta,
    ids_row,
    ids_column,
    gain,
    cosine,
    sine,
    cosine_all,
    sine_all,
    query,
    key_rows,
    key,
    value_rows,
    inv_ref,
    out,
    mixed_grad,
    other_dq,
    raw_query,
    raw_key,
    triple,
    gain_grad,
    back,
    centre,
    dq,
    dk_sum,
    dv_sum,
    query_sum,
):
    place = pl.program_id(0)
    local = heads * HEAD

    @pl.when(place == 0)
    def _():
        dk_sum[...] = jnp.zeros_like(dk_sum)
        dv_sum[...] = jnp.zeros_like(dv_sum)
        query_sum[...] = jnp.zeros_like(query_sum)

    back[...] = half(mixed_grad[...])
    attend_back_tile(
        heads,
        meta,
        lambda index: self_bias(index, ids_row, ids_column),
        query,
        key_rows,
        key,
        value_rows,
        inv_ref,
        out,
        back,
        dq,
        dk_sum,
        dv_sum,
        centre,
    )
    columns = pl.ds(pl.multiple_of(place * TILE, TILE), TILE)
    for span in spans(heads):
        normed, inverse = head_norm(raw_query[span, :])
        grad = turn(dq[span, :] + other_dq[span, :], cosine[...], -sine[...])
        query_sum[span, :] += grad * normed
        triple[span, columns] = half(head_back(normed, inverse, grad * gain[span, 0:1]))

    @pl.when(place == pl.num_programs(0) - 1)
    def _():
        summed = jnp.sum(query_sum[...], axis=1, keepdims=True)
        gain_grad[:, 0:128] = jnp.broadcast_to(summed, (local, 128))
        triple[2 * local :, :] = half(dv_sum[...])
        for head, span in enumerate(spans(heads)):
            normed, inverse = head_norm(raw_key[span, :])
            grad = turn(dk_sum[span, :], cosine_all[...], -sine_all[...])
            summed = jnp.sum(grad * normed, axis=1, keepdims=True)
            gain_grad[span, 128:256] = jnp.broadcast_to(summed, (HEAD, 128))
            triple[local + head * HEAD : local + (head + 1) * HEAD, :] = half(
                head_back(normed, inverse, grad * gain[span, 1:2])
            )


def attention_call(kernel, name, scalars, operands, outs, scratch, tokens, weight, after=()):
    def block(array, tiled):
        lead = array.shape[:-1]
        if tiled is not True and tiled is not False:
            third = (lead[0] // 3, tokens if tiled else TILE)
            return pl.BlockSpec(third, lambda i, *_: (tiled, 0) if tiled else (0, i))
        if tiled:
            return pl.BlockSpec((*lead, TILE), lambda i, *_: (*([0] * len(lead)), i))
        return pl.BlockSpec(array.shape, lambda i, *_: (0,) * len(array.shape))

    count = len(scalars) + len(operands)

    def run(*refs):
        kernel(*refs[:count], *refs[count + len(after) :])

    return pl.pallas_call(
        run,
        grid_spec=pltpu.PrefetchScalarGridSpec(
            num_scalar_prefetch=len(scalars),
            grid=(tokens // TILE,),
            in_specs=[block(*operand) for operand in operands]
            + [pl.BlockSpec(memory_space=pl.ANY)] * len(after),
            out_specs=[block(*out) for out in outs],
            scratch_shapes=scratch,
        ),
        out_shape=[out for out, _ in outs],
        compiler_params=pltpu.CompilerParams(
            vmem_limit_bytes=58 * 1024 * 1024, dimension_semantics=("arbitrary",)
        ),
        cost_estimate=pl.CostEstimate(
            flops=weight, bytes_accessed=weight, transcendentals=0
        ),
        name=name,
    )(*scalars, *(operand for operand, _ in operands), *after)


def adamw(grad, weight, moment, square, decay, rate):
    moment_new = BETA1 * moment + (1.0 - BETA1) * grad
    square_new = BETA2 * square + (1.0 - BETA2) * grad * grad
    step_size = (
        moment_new / (1.0 - BETA1**STEP) / (jnp.sqrt(square_new / (1.0 - BETA2**STEP)) + ADAM_EPS)
    )
    return (moment_new, square_new, weight - rate * (step_size + decay * weight))


def body(
    latents,
    cotangent,
    captions,
    conditions,
    image_ids,
    rope_rows,
    rope_cols,
    caption_lengths,
    attention_in,
    attention_out,
    feed_in,
    feed_out,
    caption_in,
    modulator,
    channels,
    moment_attention_in,
    square_attention_in,
    moment_attention_out,
    square_attention_out,
    moment_feed_in,
    square_feed_in,
    moment_feed_out,
    square_feed_out,
    moment_caption_in,
    square_caption_in,
    moment_modulator,
    square_modulator,
    moment_channels,
    square_channels,
):
    tensor_size = lax.axis_size("tensor")
    tensor_index = lax.axis_index("tensor")
    dp_size = lax.axis_size("dp")
    dp_index = lax.axis_index("dp")
    shard_rows, width = latents.shape
    local = attention_in.shape[2]
    heads = local // HEAD
    units = feed_in.shape[2]
    segment = image_ids[0]
    row_tokens = segment.shape[0]
    images = conditions.shape[0]
    per_row = caption_lengths.shape[1]
    lengths = caption_lengths[0]
    slots = captions.shape[0]
    offset = tensor_index * local
    own_ids = lax.dynamic_slice_in_dim(segment, tensor_index * shard_rows, shard_rows)

    rows = attention_in.shape[1]
    fused = tensor_size == 4
    caption_half = half(caption_in)
    key_line = gather_far(caption_half[0].T)
    value_line = gather_far(
        jnp.concatenate([caption_half[1].T, half(attention_out).T], axis=1)
    )
    in_half = half(attention_in)
    attention_line = gather_far(jnp.concatenate([in_half[0], in_half[1], in_half[2]], axis=1))
    down_line = gather_far(half(feed_out).T)
    feed_half = half(feed_in)
    feed_own = jnp.concatenate([feed_half[0], feed_half[1]], axis=1)

    augmented = half(
        jnp.concatenate([jax.nn.silu(conditions), jnp.ones((images, 1), jnp.float32)], axis=1)
    )
    factor_part = jnp.dot(augmented, half(modulator), preferred_element_type=jnp.float32)
    own_columns = factor_part.shape[1]
    payload = jnp.concatenate(
        [
            factor_part.reshape(dp_size, per_row, own_columns),
            jnp.broadcast_to(
                lax.reduce_precision(channels, 8, 7).reshape(-1, own_columns),
                (dp_size, channels.size // own_columns, own_columns),
            ),
        ],
        axis=1,
    )
    received, feed_other = remote_call(
        spread_kernel,
        "modulation_exchange",
        0,
        [payload],
        [jax.ShapeDtypeStruct((tensor_size, *payload.shape), jnp.float32)],
        exchange_scratch([payload.shape]),
        [feed_own],
        everyone=True,
    )
    feed_full = gather_far(join_near(feed_own, feed_other, rows))
    factor_row = jnp.transpose(received[:, :, :per_row], (2, 1, 0, 3)).reshape(per_row, -1)
    gains = received[0, :, per_row:].reshape(dp_size, 8, -1)
    gains = jnp.transpose(gains, (1, 0, 2)).reshape(8, width)
    local_gains = lax.dynamic_slice_in_dim(gains[4:], offset, local, 1).T
    chooser = (own_ids[:, None] == jnp.arange(per_row, dtype=jnp.int32)[None, :]).astype(
        jnp.float32
    )
    choose = jnp.transpose(chooser.reshape(CHUNKS, -1, per_row), (0, 2, 1))

    def token_factor(which):
        return pick(chooser, factor_row, which, slice(None))

    def split(value):
        return [value[i * shard_rows : (i + 1) * shard_rows] for i in range(tensor_size)]

    def by_image(*grads):
        return jnp.stack([jnp.dot(chooser.T, grad, precision=HIGH) for grad in grads])

    f32, bf16 = jnp.float32, jnp.bfloat16

    def shape(dims, dtype=f32):
        return jax.ShapeDtypeStruct(dims, dtype)

    gathered = shape((tensor_size, shard_rows, width), bf16)
    in_kernel = sum_scratch(shard_rows, width)

    def semaphores(count):
        return pltpu.SemaphoreType.DMA((2, count))

    sum_sems, all_sems = semaphores(SUM_SEMAPHORES), semaphores(SUM_SEMAPHORES + 3 * CHUNKS)
    source = latents.astype(f32)

    def caption_project(weight, carry, number):
        if fused:
            return remote_call(
                project_kernel,
                "project",
                number,
                [weight, captions],
                [shape((local, slots))],
                [*sum_scratch(local, slots), sum_sems],
                carry,
            )
        total = collect(
            [
                dot(
                    lax.dynamic_slice_in_dim(weight, owner(i) * local, local), captions, 1, 1
                )
                for i in range(tensor_size)
            ]
        )
        return (total, *(near_swap(array) for array in carry))

    if fused:
        attn_full, key_other = remote_call(
            enter_kernel,
            "enter",
            3,
            [latents, factor_row, chooser, gains],
            [gathered],
            [semaphores(3 * CHUNKS)],
            [key_line],
        )
        attn_full = attn_full.reshape(row_tokens, width)
    else:
        attn_full = in_place(spread(enter_point(source, token_factor(0), gains[0])))
        key_other = near_swap(key_line)
    text_key_raw, value_other = caption_project(
        join_near(key_line, key_other, rows), [value_line], 4
    )
    features = captions.shape[1]
    value_full, out_full = (
        join_near(value_line[:, part], value_other[:, part], rows)
        for part in (slice(0, features), slice(features, None))
    )
    text_value_raw, attention_other = caption_project(value_full, [attention_line], 11)
    in_full = join_near(attention_line, attention_other, rows)
    projected = dot(in_full, attn_full, 0, 1)
    cosine, sine = rope_tables(rope_rows[0], rope_cols[0])

    tiles = row_tokens // TILE
    first_id = segment.reshape(tiles, TILE)[:, 0]
    last_id = segment.reshape(tiles, TILE)[:, TILE - 1]
    low = jnp.sum((segment[None] < first_id[:, None]).astype(jnp.int32), axis=1) // TILE
    high = (
        jnp.sum((segment[None] <= last_id[:, None]).astype(jnp.int32), axis=1) + TILE - 1
    ) // TILE
    self_meta = jnp.stack([low, high], axis=1).reshape(-1)
    cross_meta = jnp.stack([first_id, last_id + 1], axis=1).reshape(-1)
    ids_row = image_ids
    ids_column = segment[:, None]
    wide = jax.ShapeDtypeStruct((local, row_tokens), jnp.float32)
    narrow = jax.ShapeDtypeStruct((local, row_tokens), jnp.bfloat16)
    sums = jax.ShapeDtypeStruct((heads, 8, row_tokens), jnp.float32)
    by_rows = jax.ShapeDtypeStruct((heads, row_tokens, HEAD), jnp.bfloat16)
    text_narrow = jax.ShapeDtypeStruct((local, slots), jnp.bfloat16)
    text_rows = jax.ShapeDtypeStruct((heads, slots, HEAD), jnp.bfloat16)
    gain_shape = jax.ShapeDtypeStruct((local, 256), jnp.float32)
    tile_sums = pltpu.VMEM((heads, 8, TILE), jnp.float32)
    tables = [(cosine, True), (sine, True), (cosine, False), (sine, False)]
    queries, keys, key_rows, value_rows, own_out, own_inv = attention_call(
        functools.partial(self_forward_kernel, heads),
        "self_forward",
        [self_meta],
        [
            (ids_row, True),
            (ids_column, False),
            (local_gains, False),
            *tables,
            (projected, 0),
            (projected, 1),
            (projected, 2),
        ],
        [
            (narrow, True),
            (narrow, False),
            (by_rows, False),
            (by_rows, False),
            (wide, True),
            (sums, True),
        ],
        [pltpu.VMEM((local, row_tokens), jnp.bfloat16), tile_sums],
        row_tokens,
        15000,
    )
    text_keys, text_key_rows, text_value_rows, other_out, other_inv, mixed = attention_call(
        functools.partial(cross_forward_kernel, heads),
        "cross_forward",
        [cross_meta, lengths],
        [
            (ids_row, True),
            (local_gains, False),
            (queries, True),
            (own_out, True),
            (text_key_raw, False),
            (text_value_raw, False),
        ],
        [
            (text_narrow, False),
            (text_rows, False),
            (text_rows, False),
            (wide, True),
            (sums, True),
            (narrow, True),
        ],
        [pltpu.VMEM((local, slots), jnp.bfloat16), tile_sums],
        row_tokens,
        18000,
    )
    norm_gains = gains
    if fused:
        attn_sum, middle, feed_all, down_other = remote_call(
            attention_out_kernel,
            "attention_out",
            5,
            [mixed, out_full, latents, factor_row, chooser, norm_gains],
            [shape((shard_rows, width)), shape((shard_rows, width)), gathered],
            [pltpu.VMEM((2 * shard_rows, local), bf16), *in_kernel, all_sems],
            [down_line],
        )
        feed_all = feed_all.reshape(row_tokens, width)
        down_full = join_near(down_line, down_other, rows)
        block = pltpu.VMEM((shard_rows, width), f32)
        hidden, block_out, end_factor, end_row, feed_sum_grad, gate_up = remote_call(
            feed_kernel,
            "feed_forward",
            6,
            [feed_all, feed_full, factor_row, chooser, choose, norm_gains],
            [
                shape((row_tokens, units), bf16),
                shape((shard_rows, width)),
                shape((1, per_row, width)),
                shape((1, 8, width)),
                gathered,
            ],
            [
                pltpu.VMEM((row_tokens, 2 * units), f32),
                pltpu.VMEM((width, units), bf16),
                block,
                block,
                pltpu.SemaphoreType.DMA((5,)),
                *in_kernel,
                all_sems,
            ],
            late=[down_full, middle, cotangent],
            late_outs=[shape((row_tokens, 2 * units))],
        )
        feed_sum_grad = feed_sum_grad.reshape(row_tokens, width)
    else:
        attn_sum = collect(
            [
                dot(
                    lax.dynamic_slice_in_dim(mixed, owner(i) * shard_rows, shard_rows, 1),
                    out_full,
                    0,
                    1,
                )
                for i in range(tensor_size)
            ]
        )
        middle, feed_block = middle_point(
            attn_sum, source, token_factor(1), token_factor(2), gains[1], gains[2]
        )
        feed_all = in_place(spread(feed_block))
        down_full = join_near(down_line, near_swap(down_line), rows)
        gate_up = dot(feed_all, feed_full, 1, 0)
        hidden = half(jax.nn.silu(gate_up[:, :units]) * gate_up[:, units:])
        feed_sum = collect(split(dot(hidden, down_full, 1, 1)))
        block_out, feed_block_grad, *grads = end_point(
            feed_sum, middle, token_factor(3), cotangent, gains[3]
        )
        end_factor, end_row = by_image(grads[0]), grads[1][None]
        feed_sum_grad = in_place(spread(feed_block_grad))
    feed_out_grad = half(dot(feed_sum_grad, hidden, 0, 0))
    feed_out_parts = feed_out_grad.reshape(dp_size // 2, 2, -1, units)
    if fused:
        (
            middle_grad,
            middle_factor,
            middle_row,
            attn_sum_grad,
            pair_grad,
            feed_out_other,
        ) = remote_call(
            feed_back_kernel,
            "feed_backward",
            7,
            [feed_sum_grad, down_full, factor_row, chooser, choose, norm_gains],
            [
                shape((shard_rows, width)),
                shape((2, per_row, width)),
                shape((2, 8, width)),
                gathered,
            ],
            [
                pltpu.VMEM((row_tokens, 2 * units), f32),
                pltpu.VMEM((width, 2 * units), bf16),
                block,
                block,
                block,
                pltpu.VMEM((row_tokens, 2 * units), bf16),
                pltpu.SemaphoreType.DMA((8,)),
                *in_kernel,
                all_sems,
            ],
            [feed_out_parts],
            late=[gate_up, feed_full, attn_sum, middle, cotangent],
            late_outs=[shape((row_tokens, 2 * units), bf16)],
        )
        attn_sum_grad = attn_sum_grad.reshape(row_tokens, width)
    else:
        hidden_grad = dot(feed_sum_grad, down_full, 1, 0)
        pair_grad = jnp.concatenate(
            pair_point(hidden_grad, gate_up[:, :units], gate_up[:, units:]), axis=1
        )
        feed_input_grad = collect(split(dot(pair_grad, feed_full, 1, 1)))
        middle_grad, attn_block_grad, *grads = middle_back_point(
            feed_input_grad,
            attn_sum,
            middle,
            token_factor(1),
            token_factor(2),
            cotangent,
            gains[1],
            gains[2],
        )
        middle_factor, middle_row = by_image(*grads[:2]), jnp.stack(grads[2:])
        attn_sum_grad = in_place(spread(attn_block_grad))
        feed_out_other = swap_half(feed_out_parts)
    feed_out_sum = scatter_far(sum_half(feed_out_parts, feed_out_other))
    outer_grad = half(dot(feed_all, pair_grad, 0, 0))
    outer_both = lax.psum_scatter(
        outer_grad, "dp", scatter_dimension=0, tiled=True, axis_index_groups=far_groups()
    )
    mixed_grad = dot(out_full, gate(attn_sum_grad, outer_grad), 0, 1)
    out_parts = half(dot(attn_sum_grad, mixed, 0, 1)).reshape(dp_size // 2, 2, -1, local)
    query_two, text_key_grad, text_value_grad, text_gains = attention_call(
        functools.partial(cross_backward_kernel, heads),
        "cross_backward",
        [cross_meta, lengths],
        [
            (ids_row, True),
            (local_gains, False),
            (queries, True),
            (text_key_rows, False),
            (text_keys, False),
            (text_value_rows, False),
            (other_inv, True),
            (other_out, True),
            (mixed_grad, True),
            (text_key_raw, False),
        ],
        [(wide, True), (text_narrow, False), (text_narrow, False), (gain_shape, False)],
        [
            pltpu.VMEM((local, TILE), jnp.bfloat16),
            tile_sums,
            pltpu.VMEM((local, slots), jnp.float32),
            pltpu.VMEM((local, slots), jnp.float32),
            pltpu.VMEM((local, TILE), jnp.float32),
        ],
        row_tokens,
        25000,
    )
    triple_grad, own_gains = attention_call(
        functools.partial(self_backward_kernel, heads),
        "self_backward",
        [self_meta],
        [
            (ids_row, True),
            (ids_column, False),
            (local_gains, False),
            *tables,
            (queries, True),
            (key_rows, False),
            (keys, False),
            (value_rows, False),
            (own_inv, True),
            (own_out, True),
            (mixed_grad, True),
            (query_two, True),
            (projected, 0),
            (projected, 1),
        ],
        [
            (jax.ShapeDtypeStruct((3 * local, row_tokens), jnp.bfloat16), False),
            (gain_shape, False),
        ],
        [
            pltpu.VMEM((local, TILE), jnp.bfloat16),
            tile_sums,
            pltpu.VMEM((local, TILE), jnp.float32),
            pltpu.VMEM((local, row_tokens), jnp.float32),
            pltpu.VMEM((local, row_tokens), jnp.float32),
            pltpu.VMEM((local, TILE), jnp.float32),
        ],
        row_tokens,
        25000,
        [feed_out_sum],
    )
    in_parts = half(dot(attn_full, triple_grad, 0, 1)).reshape(dp_size // 2, 2, -1, 3 * local)

    if fused:
        latent_grad, enter_factor, enter_row, in_other = remote_call(
            enter_back_kernel,
            "enter_backward",
            10,
            [
                triple_grad,
                in_full,
                latents,
                factor_row,
                chooser,
                choose,
                middle_grad,
                norm_gains,
            ],
            [
                shape((shard_rows, width)),
                shape((1, per_row, width)),
                shape((1, 8, width)),
            ],
            [pltpu.VMEM((2 * shard_rows, 3 * local), bf16), *in_kernel, sum_sems],
            [in_parts],
        )
    else:
        attn_input_grad = collect(
            [
                dot(
                    lax.dynamic_slice_in_dim(triple_grad, owner(i) * shard_rows, shard_rows, 1),
                    in_full,
                    0,
                    1,
                )
                for i in range(tensor_size)
            ]
        )
        in_other = swap_half(in_parts)
        latent_grad, *grads = enter_back_point(
            attn_input_grad, source, token_factor(0), middle_grad, gains[0]
        )
        enter_factor, enter_row = by_image(grads[0]), grads[1][None]
    in_sum = scatter_far(sum_half(in_parts, in_other))

    columns = captions.shape[1]

    def caption_back(grad, carry, number, after):
        if not fused:
            parts = half(dot(in_place(spread(grad)), captions, 1, 0))
            parts = parts.reshape(dp_size // 2, 2, -1, columns)
            return (sum_half(parts, swap_half(parts)), *(swap_half(array) for array in carry))
        kept = (tensor_size, local // 2, columns)
        summed, *others = remote_call(
            text_kernel,
            "text_gradient",
            number,
            [grad],
            [shape(kept, bf16)],
            [
                pltpu.VMEM((tensor_size, local, slots), bf16),
                pltpu.VMEM(kept, f32),
                pltpu.VMEM(kept, bf16),
                pltpu.VMEM(kept, bf16),
                pltpu.VMEM(captions.shape, bf16),
                pltpu.SemaphoreType.DMA((1,)),
                semaphores(5 * CHUNKS),
            ],
            carry,
            neighbour=True,
            after=after,
            late=[captions],
        )
        return (flat(summed), *others)

    value_grad, out_other = caption_back(text_value_grad, [out_parts], 8, [latent_grad])
    value_sum = scatter_far(
        jnp.concatenate([value_grad, sum_half(out_parts, out_other)], axis=1)
    )
    (key_grad,) = caption_back(text_key_grad, [], 9, [outer_both, value_grad])
    key_sum = scatter_far(key_grad)
    shared_rows = jnp.sum(
        jnp.concatenate([enter_row, middle_row, end_row]), axis=1
    )
    head_rows = jnp.stack(
        [own_gains[:, 0], own_gains[:, 128], text_gains[:, 128], text_gains[:, 0]]
    )
    head_full = lax.dynamic_update_slice(
        jnp.zeros((4, width), jnp.float32), head_rows, (jnp.zeros((), jnp.int32), offset)
    )
    channel_part = jnp.concatenate([shared_rows, head_full], axis=0)
    factor_image = jnp.concatenate([enter_factor, middle_factor, end_factor])
    factor_image = jnp.transpose(factor_image, (1, 0, 2))
    factor_image = jnp.transpose(
        factor_image.reshape(per_row, dp_size, tensor_size, own_columns), (2, 1, 0, 3)
    )
    channel_blocks = jnp.transpose(channel_part.reshape(8, dp_size, -1), (1, 0, 2))
    channel_blocks = channel_blocks.reshape(dp_size, -1, own_columns)
    payload = jnp.concatenate(
        [factor_image, jnp.broadcast_to(channel_blocks, (tensor_size, *channel_blocks.shape))],
        axis=2,
    )
    blocks = payload.shape[1:]
    outer_parts = outer_both.reshape(1, 2, -1, outer_both.shape[1])
    received, outer_other = remote_call(
        return_kernel,
        "modulation_return",
        1,
        [payload],
        [shape(blocks)],
        exchange_scratch([payload.shape, blocks, blocks]),
        [outer_parts],
        everyone=True,
        after=[in_sum],
    )
    in_sum, value_sum = gate(in_sum, received), gate(value_sum, received)
    feed_out_sum = gate(feed_out_sum, received)
    value_sum, out_sum = value_sum[:, :columns], value_sum[:, columns:]
    feed_in_sum = lax.dynamic_index_in_dim(outer_parts, dp_index % 2, 1, keepdims=False)[0]
    feed_in_sum = feed_in_sum.astype(f32) + outer_other[0].astype(f32)
    factor_grad = received[:, :per_row].reshape(images, own_columns)
    channel_sum = jnp.sum(received[:, per_row:], axis=0).reshape(channels.shape)
    modulator_sum = jnp.dot(augmented.astype(jnp.float32).T, factor_grad, precision=HIGH)

    def square(value):
        value = value.astype(f32)
        return jnp.sum(value * value)

    squares = (
        square(in_sum)
        + square(out_sum)
        + square(feed_in_sum)
        + square(feed_out_sum)
        + square(key_sum)
        + square(value_sum)
        + square(modulator_sum)
        + square(channel_sum) / tensor_size
    )
    in_sum = jnp.stack([in_sum[:, i * local : (i + 1) * local] for i in range(3)])
    feed_in_sum = jnp.stack([feed_in_sum[:, i * units : (i + 1) * units] for i in range(2)])
    caption_sum = jnp.stack([key_sum.T, value_sum.T])
    (squares,) = remote_call(
        total_kernel,
        "norm_exchange",
        2,
        [jnp.broadcast_to(squares, (8, 128))],
        [shape((8, 128))],
        exchange_scratch([(tensor_size, 8, 128), (dp_size, 8, 128), (8, 128)]),
        everyone=True,
    )
    grad_norm = jnp.sqrt(squares[0, 0])
    factor = CLIP / jnp.maximum(grad_norm, CLIP)
    results = [
        adamw(grad.astype(f32) * factor, weight, moment, second, DECAY, RATE)
        for grad, weight, moment, second in (
            (in_sum, attention_in, moment_attention_in, square_attention_in),
            (out_sum.T, attention_out, moment_attention_out, square_attention_out),
            (feed_in_sum, feed_in, moment_feed_in, square_feed_in),
            (feed_out_sum.T, feed_out, moment_feed_out, square_feed_out),
            (caption_sum, caption_in, moment_caption_in, square_caption_in),
            (modulator_sum, modulator, moment_modulator, square_modulator),
        )
    ]
    results.append(
        adamw(channel_sum * factor, channels, moment_channels, square_channels, 0.0, GAIN_RATE)
    )
    return (block_out, latent_grad, grad_norm, *(part for result in results for part in result))


def solution(mesh):
    return jax.shard_map(
        body,
        mesh=mesh,
        in_specs=(
            P(("dp", "tensor"), None),
            P(("dp", "tensor"), None),
            P("dp", "tensor"),
            P(),
            P("dp", None),
            P("dp", None),
            P("dp", None),
            P("dp", None),
            P(None, "dp", "tensor"),
            P("tensor", "dp"),
            P(None, "dp", "tensor"),
            P("tensor", "dp"),
            P(None, "tensor", "dp"),
            P(None, ("dp", "tensor")),
            P(None, "dp"),
            P(None, "dp", "tensor"),
            P(None, "dp", "tensor"),
            P("tensor", "dp"),
            P("tensor", "dp"),
            P(None, "dp", "tensor"),
            P(None, "dp", "tensor"),
            P("tensor", "dp"),
            P("tensor", "dp"),
            P(None, "tensor", "dp"),
            P(None, "tensor", "dp"),
            P(None, ("dp", "tensor")),
            P(None, ("dp", "tensor")),
            P(None, "dp"),
            P(None, "dp"),
        ),
        out_specs=(
            P(("dp", "tensor"), None),
            P(("dp", "tensor"), None),
            P(),
            P(None, "dp", "tensor"),
            P(None, "dp", "tensor"),
            P(None, "dp", "tensor"),
            P("tensor", "dp"),
            P("tensor", "dp"),
            P("tensor", "dp"),
            P(None, "dp", "tensor"),
            P(None, "dp", "tensor"),
            P(None, "dp", "tensor"),
            P("tensor", "dp"),
            P("tensor", "dp"),
            P("tensor", "dp"),
            P(None, "tensor", "dp"),
            P(None, "tensor", "dp"),
            P(None, "tensor", "dp"),
            P(None, ("dp", "tensor")),
            P(None, ("dp", "tensor")),
            P(None, ("dp", "tensor")),
            P(None, "dp"),
            P(None, "dp"),
            P(None, "dp"),
        ),
        check_vma=False,
    )
```
